32 devices in a mesh: dp: 16 (over z, x, core), tensor: 2 (over y).
Axes of the slice: x: 2, y: 2, z: 4, core: 2. Of those that a mesh axis runs over, the one named last changes fastest.
Arguments:
- activations: bfloat16 [64, 512, 512], P('dp', 'tensor'), may hold values from -6 to 6
- memory_one: bfloat16 [64, 512, 512], P('dp'), may hold values from -6 to 6
- memory_two: bfloat16 [64, 512, 512], P('dp'), may hold values from -6 to 6
- neighbours: int32 [64, 512, 4], P('dp'), may hold values from 0 to 511
- resets: int32 [64], P('dp'), may hold values 0 or 1
- cotangent: bfloat16 [64, 512, 512], P('dp', 'tensor'), may hold values from -6 to 6
- qkv_weight: float32 [2, 3, 512, 512], P(None, None, 'dp', 'tensor'), may hold values from -0.26958446 to 0.26958446
- qkv_first: float32 [2, 3, 512, 512], P(None, None, 'dp', 'tensor'), may hold values from -8.855232e-05 to 8.855232e-05
- qkv_second: float32 [2, 3, 512, 512], P(None, None, 'dp', 'tensor'), may hold values from 1.589496e-10 to 6.357984e-10
- qkv_ema: float32 [2, 3, 512, 512], P(None, None, 'dp', 'tensor'), may hold values from -0.25 to 0.25
- out_weight: float32 [2, 512, 512], P(None, 'tensor', 'dp'), may hold values from -4 to 4
- out_first: float32 [2, 512, 512], P(None, 'tensor', 'dp'), may hold values from -1.3282848e-05 to 1.3282848e-05
- out_second: float32 [2, 512, 512], P(None, 'tensor', 'dp'), may hold values from 3.576366e-12 to 1.4305464e-11
- out_ema: float32 [2, 512, 512], P(None, 'tensor', 'dp'), may hold values from -4 to 4
- up_weight: float32 [2, 512, 2048], P(None, 'dp', 'tensor'), may hold values from -0.32261747 to 0.32261747
- up_first: float32 [2, 512, 2048], P(None, 'dp', 'tensor'), may hold values from -1.3282848e-05 to 1.3282848e-05
- up_second: float32 [2, 512, 2048], P(None, 'dp', 'tensor'), may hold values from 3.576366e-12 to 1.4305464e-11
- up_ema: float32 [2, 512, 2048], P(None, 'dp', 'tensor'), may hold values from -0.25 to 0.25
- down_weight: float32 [2, 2048, 512], P(None, 'tensor', 'dp'), may hold values from -0.125 to 0.125
- down_first: float32 [2, 2048, 512], P(None, 'tensor', 'dp'), may hold values from -8.855232e-05 to 8.855232e-05
- down_second: float32 [2, 2048, 512], P(None, 'tensor', 'dp'), may hold values from 1.589496e-10 to 6.357984e-10
- down_ema: float32 [2, 2048, 512], P(None, 'tensor', 'dp'), may hold values from -0.125 to 0.125
- gain_rows: float32 [4, 512], P(None, 'dp'), may hold values from 0.4 to 2.9
- gain_first: float32 [4, 512], P(None, 'dp'), may hold values from -0.000354209285 to 0.000354209285
- gain_second: float32 [4, 512], P(None, 'dp'), may hold values from 2.5431936e-09 to 1.01727744e-08
- gain_ema: float32 [4, 512], P(None, 'dp'), may hold values from 0.1 to 1.9
- gate_weight: float32 [512, 8], P('dp', 'tensor'), may hold values from -0.25 to 0.25
- gate_first: float32 [512, 8], P('dp', 'tensor'), may hold values from -8.855232e-05 to 8.855232e-05
- gate_second: float32 [512, 8], P('dp', 'tensor'), may hold values from 1.589496e-10 to 6.357984e-10
- gate_ema: float32 [512, 8], P('dp', 'tensor'), may hold values from -0.25 to 0.25
Outputs:
- result_rows: bfloat16 [64, 512, 512], P('dp', 'tensor')
- input_grad: float32 [64, 512, 512], P('dp', 'tensor')
- grad_norm: float32 [], replicated
- qkv_first_new: float32 [2, 3, 512, 512], P(None, None, 'dp', 'tensor')
- qkv_second_new: float32 [2, 3, 512, 512], P(None, None, 'dp', 'tensor')
- qkv_weight_new: float32 [2, 3, 512, 512], P(None, None, 'dp', 'tensor')
- qkv_ema_new: float32 [2, 3, 512, 512], P(None, None, 'dp', 'tensor')
- out_first_new: float32 [2, 512, 512], P(None, 'tensor', 'dp')
- out_second_new: float32 [2, 512, 512], P(None, 'tensor', 'dp')
- out_weight_new: float32 [2, 512, 512], P(None, 'tensor', 'dp')
- out_ema_new: float32 [2, 512, 512], P(None, 'tensor', 'dp')
- up_first_new: float32 [2, 512, 2048], P(None, 'dp', 'tensor')
- up_second_new: float32 [2, 512, 2048], P(None, 'dp', 'tensor')
- up_weight_new: float32 [2, 512, 2048], P(None, 'dp', 'tensor')
- up_ema_new: float32 [2, 512, 2048], P(None, 'dp', 'tensor')
- down_first_new: float32 [2, 2048, 512], P(None, 'tensor', 'dp')
- down_second_new: float32 [2, 2048, 512], P(None, 'tensor', 'dp')
- down_weight_new: float32 [2, 2048, 512], P(None, 'tensor', 'dp')
- down_ema_new: float32 [2, 2048, 512], P(None, 'tensor', 'dp')
- gain_first_new: float32 [4, 512], P(None, 'dp')
- gain_second_new: float32 [4, 512], P(None, 'dp')
- gain_rows_new: float32 [4, 512], P(None, 'dp')
- gain_ema_new: float32 [4, 512], P(None, 'dp')
- gate_first_new: float32 [512, 8], P('dp', 'tensor')
- gate_second_new: float32 [512, 8], P('dp', 'tensor')
- gate_weight_new: float32 [512, 8], P('dp', 'tensor')
- gate_ema_new: float32 [512, 8], P('dp', 'tensor')
- feed_gain_grads: float32 [2, 512], P(None, 'dp')
The draws below stay inside these ranges and needn't reach their ends.
Inputs may be any that keep to these rules, and one draw needn't show every extreme that they name: `neighbours`: each entry names a memory row of the same segment.
All inputs are finite; a program needn't handle non-finite values. No bound on the sum of `resets` on one device may be relied on, other than what follows from the above.
Results may differ from the reference program's by a relative error of at most 0.03.
The reference program's roundings to bfloat16 on the way count: a program that leaves them out, or rounds other values in their place, can miss the bound.
Values may be sent and summed in bfloat16 or wider, within the bound.
A program may use at most 256 MiB of HBM per device.

```python
import math
import jax
import jax.numpy as jnp
from jax import lax

D = 512
HEADS = 8
HEAD_DIM = 64
FF = 2048
NEIGH = 4
SEG = 512
MEM = 512
STEP = 4
SEGS = 64
PARAMS = 6297600


def rising(length, bottom, summit):
    return jnp.exp(jnp.linspace(math.log(bottom), math.log(summit), length)).astype(jnp.float32)


def first_state(key, extent, magnitude):
    sign_key, size_key = jax.random.split(key)
    sign_values = jnp.where(jax.random.bernoulli(sign_key, 0.5, extent), 1.0, -1.0)
    sizes_drawn = jnp.exp(jax.random.uniform(size_key, extent, jnp.float32, math.log(0.5), math.log(2.0)))
    return (sign_values * sizes_drawn * magnitude / 9.0).astype(jnp.float32)


def second_state(key, extent, magnitude):
    drawn = jnp.exp(jax.random.uniform(key, extent, jnp.float32, math.log(1.0), math.log(4.0)))
    return drawn * magnitude * magnitude / 999.0


def draw_qkv_weight(key, part):
    key = jax.random.fold_in(key, 11)
    base_draw = jax.random.truncated_normal(key, -4.0, 4.0, (2, 3, D, D), jnp.float32)
    columns = rising(D, 0.65, 1.5)
    return base_draw * columns * D ** (-0.5)


def draw_up_weight(key, part):
    key = jax.random.fold_in(key, 12)
    base_draw = jax.random.truncated_normal(key, -4.0, 4.0, (2, D, FF), jnp.float32)
    columns = rising(FF, 0.6, 1.8)
    return base_draw * columns * D ** (-0.5)


def draw_gain_rows(key, part):
    key = jax.random.fold_in(key, 13)
    jitter = 1.0 + 0.1 * jax.random.truncated_normal(key, -3.0, 3.0, (4, D), jnp.float32)
    return jitter * rising(D, 0.6, 1.8)


def draw_qkv_first(key, part):
    key = jax.random.fold_in(key, 21)
    return first_state(key, (2, 3, D, D), PARAMS ** (-0.5))


def draw_qkv_second(key, part):
    key = jax.random.fold_in(key, 22)
    return second_state(key, (2, 3, D, D), PARAMS ** (-0.5))


def draw_out_first(key, part):
    key = jax.random.fold_in(key, 23)
    return first_state(key, (2, D, D), 0.15 * PARAMS ** (-0.5))


def draw_out_second(key, part):
    key = jax.random.fold_in(key, 24)
    return second_state(key, (2, D, D), 0.15 * PARAMS ** (-0.5))


def draw_up_first(key, part):
    key = jax.random.fold_in(key, 25)
    return first_state(key, (2, D, FF), 0.15 * PARAMS ** (-0.5))


def draw_up_second(key, part):
    key = jax.random.fold_in(key, 26)
    return second_state(key, (2, D, FF), 0.15 * PARAMS ** (-0.5))


def draw_down_first(key, part):
    key = jax.random.fold_in(key, 27)
    return first_state(key, (2, FF, D), PARAMS ** (-0.5))


def draw_down_second(key, part):
    key = jax.random.fold_in(key, 28)
    return second_state(key, (2, FF, D), PARAMS ** (-0.5))


def draw_gain_first(key, part):
    key = jax.random.fold_in(key, 29)
    return first_state(key, (4, D), 4.0 * PARAMS ** (-0.5))


def draw_gain_second(key, part):
    key = jax.random.fold_in(key, 30)
    return second_state(key, (4, D), 4.0 * PARAMS ** (-0.5))


def draw_gate_first(key, part):
    key = jax.random.fold_in(key, 31)
    return first_state(key, (D, HEADS), PARAMS ** (-0.5))


def draw_gate_second(key, part):
    key = jax.random.fold_in(key, 32)
    return second_state(key, (D, HEADS), PARAMS ** (-0.5))


def with_ends(values, own_key, smallest, largest):
    longest = values.shape.index(max(values.shape))
    spots = []
    for shift in (0, 1):
        where = [jax.random.randint(jax.random.fold_in(own_key, axis), (), 0, length) for axis, length in enumerate(values.shape)]
        where[longest] = (where[longest] + shift) % values.shape[longest]
        spots.append(tuple(where))
    return values.at[spots[0]].set(smallest).at[spots[1]].set(largest)


def block_scale(stream_key, dims, shards, least, high):
    level, own = 1.0, jax.random.fold_in(stream_key, 6)
    for position, parts in shards:
        steps = jnp.exp(jax.random.uniform(jax.random.fold_in(own, position), (parts,), jnp.float32, least / len(shards), high / len(shards)))
        level = level * jnp.repeat(steps, dims[position] // parts).reshape([-1 if axis == position else 1 for axis in range(len(dims))])
    return level


def gaussian(stream_key, shape, scale, most, cuts=(), dtype=jnp.bfloat16):
    array = scale * jax.random.normal(stream_key, shape, jnp.float32)
    if cuts:
        array = array * block_scale(stream_key, shape, cuts, -0.22, 0.18)
    return jnp.clip(array, -most, most).astype(dtype)


def setup_inputs(seed: int = 0) -> dict:
    streams_of = jax.random.split(jax.random.key(seed), 31)
    activations = gaussian(streams_of[0], (SEGS, SEG, D), 1.0, 6.0, ((0, 16), (1, 2)))
    memory_one = gaussian(streams_of[1], (SEGS, MEM, D), 1.0, 6.0, ((0, 16),))
    memory_two = gaussian(streams_of[2], (SEGS, MEM, D), 1.0, 6.0, ((0, 16),))
    neighbours = with_ends(jax.random.randint(streams_of[3], (SEGS, SEG, NEIGH), 0, MEM), jax.random.fold_in(streams_of[3], 1), 0, MEM - 1).astype(jnp.int32)
    resets = with_ends((jax.random.randint(streams_of[4], (SEGS,), 0, 4) < 1).astype(jnp.int32), jax.random.fold_in(streams_of[4], 1), 0, 1)
    cotangent = gaussian(streams_of[5], (SEGS, SEG, D), 1.0, 6.0, ((0, 16), (1, 2)))
    qkv_weight = draw_qkv_weight(jax.random.fold_in(streams_of[30], 71), 0)
    qkv_first = draw_qkv_first(jax.random.fold_in(streams_of[30], 71), 0)
    qkv_second = draw_qkv_second(jax.random.fold_in(streams_of[30], 71), 0)
    qkv_ema = gaussian(streams_of[9], (2, 3, D, D), D ** -0.5, 0.25, ((2, 16), (3, 2)), jnp.float32)
    out_weight = gaussian(streams_of[10], (2, D, D), (max(4 * D // (MEM + SEG), 1)) ** -0.5, 4.0, ((1, 2), (2, 16)), jnp.float32)
    out_first = draw_out_first(jax.random.fold_in(streams_of[30], 71), 0)
    out_second = draw_out_second(jax.random.fold_in(streams_of[30], 71), 0)
    out_ema = gaussian(streams_of[13], (2, D, D), (max(4 * D // (MEM + SEG), 1)) ** -0.5, 4.0, ((1, 2), (2, 16)), jnp.float32)
    up_weight = draw_up_weight(jax.random.fold_in(streams_of[30], 71), 0)
    up_first = draw_up_first(jax.random.fold_in(streams_of[30], 71), 0)
    up_second = draw_up_second(jax.random.fold_in(streams_of[30], 71), 0)
    up_ema = gaussian(streams_of[17], (2, D, FF), D ** -0.5, 0.25, ((1, 16), (2, 2)), jnp.float32)
    down_weight = gaussian(streams_of[18], (2, FF, D), FF ** -0.5, 0.125, ((1, 2), (2, 16)), jnp.float32)
    down_first = draw_down_first(jax.random.fold_in(streams_of[30], 71), 0)
    down_second = draw_down_second(jax.random.fold_in(streams_of[30], 71), 0)
    down_ema = gaussian(streams_of[21], (2, FF, D), FF ** -0.5, 0.125, ((1, 2), (2, 16)), jnp.float32)
    gain_rows = draw_gain_rows(jax.random.fold_in(streams_of[30], 71), 0)
    gain_first = draw_gain_first(jax.random.fold_in(streams_of[30], 71), 0)
    gain_second = draw_gain_second(jax.random.fold_in(streams_of[30], 71), 0)
    gain_ema = jnp.clip(1.0 + 0.18 * jax.random.normal(streams_of[25], (4, D), jnp.float32), 0.1, 1.9)
    gate_weight = gaussian(streams_of[26], (D, HEADS), D ** -0.5, 0.25, ((0, 16), (1, 2)), jnp.float32)
    gate_first = draw_gate_first(jax.random.fold_in(streams_of[30], 71), 0)
    gate_second = draw_gate_second(jax.random.fold_in(streams_of[30], 71), 0)
    gate_ema = gaussian(streams_of[29], (D, HEADS), D ** -0.5, 0.25, ((0, 16), (1, 2)), jnp.float32)
    return {"activations": activations, "memory_one": memory_one, "memory_two": memory_two, "neighbours": neighbours, "resets": resets, "cotangent": cotangent, "qkv_weight": qkv_weight, "qkv_first": qkv_first, "qkv_second": qkv_second, "qkv_ema": qkv_ema, "out_weight": out_weight, "out_first": out_first, "out_second": out_second, "out_ema": out_ema, "up_weight": up_weight, "up_first": up_first, "up_second": up_second, "up_ema": up_ema, "down_weight": down_weight, "down_first": down_first, "down_second": down_second, "down_ema": down_ema, "gain_rows": gain_rows, "gain_first": gain_first, "gain_second": gain_second, "gain_ema": gain_ema, "gate_weight": gate_weight, "gate_first": gate_first, "gate_second": gate_second, "gate_ema": gate_ema}


@jax.custom_vjp
def low(v):
    return lax.optimization_barrier(v.astype(jnp.bfloat16)).astype(jnp.float32)

@jax.custom_vjp
def low_back(v):
    return v

def low_keep(v):
    return (low(v), None)

def low_pass(kept, grad):
    return (grad,)

def back_keep(v):
    return (v, None)

def back_low(kept, grad):
    return (low(grad),)
low.defvjp(low_keep, low_pass)
low_back.defvjp(back_keep, back_low)
HIGH = lax.Precision.HIGHEST
CLIP = 1.0
BETA_ONE = 0.9
BETA_TWO = 0.999
EPS_ADAM = 1e-08
STEP_RATES = (0.05, 0.5, 0.05, 0.03, 0.5, 0.05)
STEP_DECAYS = (0.1, 0.1, 0.1, 0.1, 0.0, 0.1)

def product(left, right):
    return jnp.dot(left, right, precision=HIGH, preferred_element_type=jnp.float32)

def normed(values, gain_row):
    spread = lax.rsqrt(lax.optimization_barrier(jnp.mean(values * values, axis=-1, keepdims=True)) + 1e-06)
    return values * spread * gain_row

def turning(length, offset):
    half_dim = HEAD_DIM // 2
    places = (jnp.arange(length) + offset).astype(jnp.float32)
    frequency = jnp.exp(-math.log(10000.0) * jnp.arange(half_dim).astype(jnp.float32) / half_dim)
    angles = places[:, None] * frequency[None, :]
    return (jnp.cos(angles), jnp.sin(angles))

def rotate(values, cosine, sine_table):
    half_dim = values.shape[-1] // 2
    first_half = values[..., :half_dim]
    second_half = values[..., half_dim:]
    cosine_b = cosine[:, None, :]
    sine_b = sine_table[:, None, :]
    return jnp.concatenate([first_half * cosine_b - second_half * sine_b, first_half * sine_b + second_half * cosine_b], axis=-1)

def to_heads(values):
    return values.reshape(values.shape[:-1] + (values.shape[-1] // HEAD_DIM, HEAD_DIM))

def allowed_keys(reset_flag):
    row_place = jnp.arange(SEG)[:, None]
    key_place = jnp.arange(MEM + SEG)[None, :]
    return jnp.where(key_place < MEM, reset_flag == 0, key_place - MEM <= row_place)

def block_attention(hidden, memory, neighbour_rows, reset_flag, qkv_layer, out_layer, gain_row, gate_cols, retrieve):
    score_scale = HEAD_DIM ** (-0.5)
    normal_rows = low(normed(hidden, gain_row))
    normal_mem = low(normed(memory, gain_row))
    query_raw = low_back(product(normal_rows, qkv_layer[0]))
    key_raw = low_back(product(normal_rows, qkv_layer[1]))
    key_mem = low_back(product(normal_mem, qkv_layer[1]))
    value_rows = low(low_back(product(normal_rows, qkv_layer[2])))
    value_mem = low(low_back(product(normal_mem, qkv_layer[2])))
    cosine_rows, sine_rows = turning(SEG, MEM)
    cosine_mem, sine_mem = turning(MEM, 0)
    query_rot = low(rotate(to_heads(query_raw), cosine_rows, sine_rows))
    key_rot = low(jnp.concatenate([rotate(to_heads(key_mem), cosine_mem, sine_mem), rotate(to_heads(key_raw), cosine_rows, sine_rows)], axis=0))
    value_all = jnp.concatenate([to_heads(value_mem), to_heads(value_rows)], axis=0)
    scores = jnp.einsum('ihd,jhd->hij', query_rot, key_rot, precision=HIGH) * score_scale
    scores = jnp.where(allowed_keys(reset_flag), low_back(scores), -1e+30)
    weights_soft = low(jax.nn.softmax(scores, axis=-1))
    attended = jnp.einsum('hij,jhd->ihd', weights_soft, value_all, precision=HIGH)
    if retrieve:
        query_plain = low(to_heads(query_raw))
        key_plain = low(to_heads(key_mem))
        near_keys = key_plain[neighbour_rows]
        near_values = to_heads(value_mem)[neighbour_rows]
        logits = jnp.einsum('ihd,ikhd->ihk', query_plain, near_keys, precision=HIGH) * score_scale
        near_weights = jax.nn.softmax(logits, axis=-1)
        fetched = jnp.einsum('ihk,ikhd->ihd', near_weights, near_values, precision=HIGH)
        gate_open = jax.nn.sigmoid(low_back(product(normal_rows, gate_cols)))[:, :, None]
        mixture = low(low_back(gate_open * low_back(attended) + (1.0 - gate_open) * fetched))
    else:
        mixture = low(low_back(attended))
    return hidden + low_back(product(mixture.reshape(SEG, D), out_layer))

def block_feed(hidden, up_layer, down_layer, gain_row):
    normal_rows = low(normed(hidden, gain_row))
    pre_active = low_back(product(normal_rows, up_layer))
    active = low(jax.nn.gelu(pre_active))
    return hidden + low_back(product(active, down_layer))

def segment_forward(params, rows, memory_one, memory_two, neighbour_rows, reset_flag):
    qkv_weight, out_weight, up_weight, down_weight, gain_rows, gate_weight = params
    gate_low = low(gate_weight)
    hidden = block_attention(rows, memory_one, neighbour_rows, reset_flag, low(qkv_weight[0]), low(out_weight[0]), low(gain_rows[0]), gate_low, False)
    hidden = block_feed(hidden, low(up_weight[0]), low(down_weight[0]), low(gain_rows[1]))
    hidden = block_attention(hidden, memory_two, neighbour_rows, reset_flag, low(qkv_weight[1]), low(out_weight[1]), low(gain_rows[2]), gate_low, True)
    hidden = block_feed(hidden, low(up_weight[1]), low(down_weight[1]), low(gain_rows[3]))
    return hidden

def adamw(weight, first, second, average, grad, rate, decay):
    ema_keep = min(0.999, (1.0 + STEP) / (10.0 + STEP))
    first_new = BETA_ONE * first + (1.0 - BETA_ONE) * grad
    second_new = BETA_TWO * second + (1.0 - BETA_TWO) * grad * grad
    first_hat = first_new / (1.0 - BETA_ONE ** STEP)
    second_hat = second_new / (1.0 - BETA_TWO ** STEP)
    weight_new = weight - rate * (first_hat / (jnp.sqrt(second_hat) + EPS_ADAM) + decay * weight)
    average_new = ema_keep * average + (1.0 - ema_keep) * weight_new
    return (first_new, second_new, weight_new, average_new)

def reference(activations, memory_one, memory_two, neighbours, resets, cotangent, qkv_weight, qkv_first, qkv_second, qkv_ema, out_weight, out_first, out_second, out_ema, up_weight, up_first, up_second, up_ema, down_weight, down_first, down_second, down_ema, gain_rows, gain_first, gain_second, gain_ema, gate_weight, gate_first, gate_second, gate_ema):
    params = (qkv_weight, out_weight, up_weight, down_weight, gain_rows, gate_weight)
    memory_low = memory_one.astype(jnp.float32)
    memory_high = memory_two.astype(jnp.float32)
    checked = jax.checkpoint(segment_forward)

    def forward(weights_all, rows_all):
        return lax.map(lambda items: checked(weights_all, items[0], items[1], items[2], items[3], items[4]), (rows_all, memory_low, memory_high, neighbours, resets))
    outputs, pullback = jax.vjp(forward, params, activations.astype(jnp.float32))
    grads, grad_input = pullback(cotangent.astype(jnp.float32))
    squares = sum((jnp.sum(piece_grad * piece_grad) for piece_grad in grads))
    grad_norm = jnp.sqrt(squares)
    factor = CLIP / jnp.maximum(grad_norm, CLIP)
    firsts = (qkv_first, out_first, up_first, down_first, gain_first, gate_first)
    seconds = (qkv_second, out_second, up_second, down_second, gain_second, gate_second)
    averages = (qkv_ema, out_ema, up_ema, down_ema, gain_ema, gate_ema)
    updated = []
    for group in range(6):
        updated.append(adamw(params[group], firsts[group], seconds[group], averages[group], grads[group] * factor, STEP_RATES[group], STEP_DECAYS[group]))
    feed_gain_grads = jnp.stack([grads[4][1], grads[4][3]]) * factor
    return (outputs.astype(jnp.bfloat16), grad_input, grad_norm, updated[0][0], updated[0][1], updated[0][2], updated[0][3], updated[1][0], updated[1][1], updated[1][2], updated[1][3], updated[2][0], updated[2][1], updated[2][2], updated[2][3], updated[3][0], updated[3][1], updated[3][2], updated[3][3], updated[4][0], updated[4][1], updated[4][2], updated[4][3], updated[5][0], updated[5][1], updated[5][2], updated[5][3], feed_gain_grads)
```

```python
import functools
import itertools
import math

import jax
import jax.numpy as jnp
import numpy as np
from jax import lax
from jax.experimental import pallas as pl
from jax.experimental.pallas import tpu as pltpu
from jax.sharding import PartitionSpec as P

HEAD_DIM = 64
SEG = 512
MEM = 512
STEP = 4
DP = "dp"
TENSOR = "tensor"


CLIP = 1.0
BETA_ONE = 0.9
BETA_TWO = 0.999
EPS_ADAM = 1e-08
STEP_RATES = (0.05, 0.5, 0.05, 0.03, 0.5, 0.05)
STEP_DECAYS = (0.1, 0.1, 0.1, 0.1, 0.0, 0.1)
HIGH = lax.Precision.HIGHEST
RULE_0 = "hij,ihd->jhd"
RULE_1 = "hij,jhd->ihd"
RULE_2 = "ihd,jhd->hij"
RULE_4 = "sic,sie->ce"
RULE_9 = "sie,ce->sic"
RULE_13 = "sihd,sikhd->sihk"
RULE_14 = "sihk,sihd->sikhd"
RULE_15 = "sihk,sikhd->sihd"
RULE_18 = "sjc,sje->ce"
RULE_19 = "sje,ce->sjc"
KEEP_ACTIVE = "active"
KEEP_ATTENDED = "attended"
KEEP_DOWN_WHOLE = "down_whole"
KEEP_FETCHED = "fetched"
KEEP_GATE_OPEN = "gate_open"
KEEP_HIDDEN = "hidden"
KEEP_KEY_ROT = "key_rot"
KEEP_LOG_TOTAL = "log_total"
KEEP_MIXTURE_LOW = "mixture_low"
KEEP_NEAR_KEYS = "near_keys"
KEEP_NEAR_VALUES = "near_values"
KEEP_NEAR_WEIGHTS = "near_weights"
KEEP_NORMAL_MEM = "normal_mem"
KEEP_NORMAL_ROWS = "normal_rows"
KEEP_PRE_ACTIVE = "pre_active"
KEEP_QUERY_PLAIN = "query_plain"
KEEP_QUERY_ROT = "query_rot"
KEEP_UP_WHOLE = "up_whole"
KEEP_VALUE_ALL = "value_all"


def normed(values, gain_row):
    spread = lax.rsqrt(jnp.mean(values * values, axis=-1, keepdims=True) + 1e-06)
    return values * spread * gain_row


def turning(length, offset):
    half_dim = HEAD_DIM // 2
    places = (jnp.arange(length) + offset).astype(jnp.float32)
    frequency = jnp.exp(-math.log(10000.0) * jnp.arange(half_dim).astype(jnp.float32) / half_dim)
    angles = places[:, None] * frequency[None, :]
    return (jnp.cos(angles), jnp.sin(angles))


def rotate(values, cosine, sine_table):
    half_dim = values.shape[-1] // 2
    first_half = values[..., :half_dim]
    second_half = values[..., half_dim:]
    cosine_b = cosine[:, None, :]
    sine_b = sine_table[:, None, :]
    return jnp.concatenate(
        [
            first_half * cosine_b - second_half * sine_b,
            first_half * sine_b + second_half * cosine_b,
        ],
        axis=-1,
    )


def to_heads(values):
    return values.reshape(values.shape[:-1] + (values.shape[-1] // HEAD_DIM, HEAD_DIM))


def flat_low(values):
    return values.reshape(values.shape[0], values.shape[1], -1).astype(jnp.bfloat16)


def allowed_keys(reset_flag):
    row_place = jnp.arange(SEG)[:, None]
    key_place = jnp.arange(MEM + SEG)[None, :]
    return jnp.where(key_place < MEM, reset_flag == 0, key_place - MEM <= row_place)


def masked_scores(query_rot, key_rot, reset_flag):
    scores = jnp.einsum(
        RULE_2, query_rot, key_rot, preferred_element_type=jnp.float32
    ) * HEAD_DIM ** (-0.5)
    return jnp.where(allowed_keys(reset_flag), scores, -1e30)


def attend_forward(query_rot, key_rot, value_all, reset_flag):
    scores = masked_scores(query_rot, key_rot, reset_flag)
    row_max = jnp.max(scores, axis=-1, keepdims=True)
    raised = jnp.exp(scores - row_max)
    summed = jnp.sum(raised, axis=-1, keepdims=True)
    weights_soft = (raised / summed).astype(jnp.bfloat16)
    attended = jnp.einsum(
        RULE_1, weights_soft, value_all, preferred_element_type=jnp.float32
    )
    return (attended, row_max[..., 0] + jnp.log(summed[..., 0]))


def attend_backward(query_rot, key_rot, value_all, reset_flag, log_total, grad_attended):
    scores = masked_scores(query_rot, key_rot, reset_flag)
    probs_exact = jnp.exp(scores - log_total[..., None])
    grad_value = jnp.einsum(
        RULE_0,
        probs_exact.astype(jnp.bfloat16),
        grad_attended,
        preferred_element_type=jnp.float32,
    )
    grad_probs = jnp.einsum(
        RULE_2, grad_attended, value_all, preferred_element_type=jnp.float32
    )
    weighted = jnp.sum(probs_exact * grad_probs, axis=-1, keepdims=True)
    grad_scores = (probs_exact * (grad_probs - weighted)).astype(jnp.bfloat16)
    grad_query = jnp.einsum(
        RULE_1, grad_scores, key_rot, preferred_element_type=jnp.float32
    ) * HEAD_DIM ** (-0.5)
    grad_key = jnp.einsum(
        RULE_0, grad_scores, query_rot, preferred_element_type=jnp.float32
    ) * HEAD_DIM ** (-0.5)
    return (grad_query, grad_key, grad_value)


def selection(neighbours, kind):
    return (neighbours[..., None] == jnp.arange(MEM)[None, None, None, :]).astype(kind)


def pick_rows(table, neighbours):
    flat_table = table.reshape(table.shape[0], table.shape[1], -1)
    chosen = jnp.einsum(
        "sikm,smc->sikc",
        selection(neighbours, table.dtype),
        flat_table,
        preferred_element_type=jnp.float32,
    )
    return chosen.reshape(chosen.shape[:3] + table.shape[2:])


def place_rows(values, neighbours):
    flat_values = values.reshape(values.shape[:3] + (-1,))
    placed = jnp.einsum(
        "sikm,sikc->smc", selection(neighbours, jnp.float32), flat_values, precision=HIGH
    )
    return placed.reshape((values.shape[0], MEM) + values.shape[3:])


def collect_rows(values):
    return lax.all_gather(values, TENSOR, axis=1, tiled=True)


def spread_rows(partial_term):
    return lax.psum_scatter(partial_term, TENSOR, scatter_dimension=1, tiled=True)


def collect_grads(values):
    return lax.all_gather(values, TENSOR, axis=1, tiled=True)


def spread_grads(partial_term):
    return lax.psum_scatter(partial_term, TENSOR, scatter_dimension=1, tiled=True)


def attention_forward(
    hidden, memory, neighbours, resets, qkv_layer, out_layer, gain_row, gate_cols, retrieve
):
    seg_count = hidden.shape[0]
    normal_rows = collect_rows(normed(hidden, gain_row).astype(jnp.bfloat16))
    normal_mem = normed(memory.astype(jnp.float32), gain_row).astype(jnp.bfloat16)
    query_raw = jnp.dot(normal_rows, qkv_layer[0], preferred_element_type=jnp.float32)
    key_raw = jnp.dot(normal_rows, qkv_layer[1], preferred_element_type=jnp.float32)
    key_mem = jnp.dot(normal_mem, qkv_layer[1], preferred_element_type=jnp.float32)
    value_rows = jnp.dot(normal_rows, qkv_layer[2], preferred_element_type=jnp.float32).astype(
        jnp.bfloat16
    )
    value_mem = jnp.dot(normal_mem, qkv_layer[2], preferred_element_type=jnp.float32).astype(
        jnp.bfloat16
    )
    cosine_rows, sine_rows = turning(SEG, MEM)
    cosine_mem, sine_mem = turning(MEM, 0)
    query_rot = rotate(to_heads(query_raw), cosine_rows, sine_rows).astype(jnp.bfloat16)
    key_rot = jnp.concatenate(
        [
            rotate(to_heads(key_mem), cosine_mem, sine_mem),
            rotate(to_heads(key_raw), cosine_rows, sine_rows),
        ],
        axis=1,
    ).astype(jnp.bfloat16)
    value_all = jnp.concatenate([to_heads(value_mem), to_heads(value_rows)], axis=1)
    attended, log_total = lax.map(
        lambda items: attend_forward(*items), (query_rot, key_rot, value_all, resets)
    )
    saved = {
        KEEP_HIDDEN: hidden,
        KEEP_NORMAL_ROWS: normal_rows,
        KEEP_NORMAL_MEM: normal_mem,
        KEEP_QUERY_ROT: query_rot,
        KEEP_KEY_ROT: key_rot,
        KEEP_VALUE_ALL: value_all,
        KEEP_LOG_TOTAL: log_total,
        KEEP_ATTENDED: attended,
    }
    if retrieve:
        query_plain = to_heads(query_raw).astype(jnp.bfloat16)
        near_keys = pick_rows(to_heads(key_mem).astype(jnp.bfloat16), neighbours).astype(
            jnp.bfloat16
        )
        near_values = pick_rows(to_heads(value_mem), neighbours)
        logits = jnp.einsum(
            RULE_13, query_plain, near_keys, preferred_element_type=jnp.float32
        ) * HEAD_DIM ** (-0.5)
        near_weights = jax.nn.softmax(logits, axis=-1)
        fetched = jnp.einsum(RULE_15, near_weights, near_values, precision=HIGH)
        gate_open = jax.nn.sigmoid(
            jnp.dot(normal_rows, gate_cols, preferred_element_type=jnp.float32)
        )[..., None]
        mixture = gate_open * attended + (1.0 - gate_open) * fetched
        saved[KEEP_QUERY_PLAIN] = query_plain
        saved[KEEP_NEAR_KEYS] = near_keys
        saved[KEEP_NEAR_VALUES] = near_values
        saved[KEEP_NEAR_WEIGHTS] = near_weights
        saved[KEEP_FETCHED] = fetched
        saved[KEEP_GATE_OPEN] = gate_open
    else:
        mixture = attended
    mixture_low = mixture.astype(jnp.bfloat16).reshape(seg_count, SEG, -1)
    saved[KEEP_MIXTURE_LOW] = mixture_low
    hidden_new = hidden + spread_rows(
        jnp.dot(mixture_low, out_layer, preferred_element_type=jnp.float32)
    )
    return (hidden_new, saved)


def attention_backward(
    grad_hidden,
    saved,
    memory,
    neighbours,
    resets,
    qkv_layer,
    out_layer,
    gain_row,
    gate_cols,
    retrieve,
):
    normal_rows = saved[KEEP_NORMAL_ROWS]
    normal_mem = saved[KEEP_NORMAL_MEM]
    grad_full = collect_grads(grad_hidden.astype(jnp.bfloat16))
    grad_out_layer = jnp.einsum(
        "sic,sid->cd", saved[KEEP_MIXTURE_LOW], grad_full, preferred_element_type=jnp.float32
    )
    grad_mixture = to_heads(
        jnp.einsum("sid,cd->sic", grad_full, out_layer, preferred_element_type=jnp.float32).astype(
            jnp.bfloat16
        )
    )
    extra_query = 0.0
    extra_key = 0.0
    extra_value = 0.0
    grad_gate_layer = None
    if retrieve:
        gate_open = saved[KEEP_GATE_OPEN]
        near_weights = saved[KEEP_NEAR_WEIGHTS]
        grad_mix_f = grad_mixture.astype(jnp.float32)
        grad_attended = (gate_open * grad_mix_f).astype(jnp.bfloat16)
        grad_fetched = (1.0 - gate_open) * grad_mix_f
        gate_value = gate_open[..., 0]
        grad_gate_logit = (
            jnp.sum(grad_mix_f * (saved[KEEP_ATTENDED] - saved[KEEP_FETCHED]), axis=-1)
            * gate_value
            * (1.0 - gate_value)
        ).astype(jnp.bfloat16)
        grad_near_weights = jnp.einsum(
            RULE_13, grad_fetched, saved[KEEP_NEAR_VALUES], precision=HIGH
        )
        grad_near_values = jnp.einsum(
            RULE_14, near_weights, grad_fetched, precision=HIGH
        )
        weighted = jnp.sum(near_weights * grad_near_weights, axis=-1, keepdims=True)
        grad_logits = near_weights * (grad_near_weights - weighted) * HEAD_DIM ** (-0.5)
        extra_query = jnp.einsum(
            RULE_15, grad_logits, saved[KEEP_NEAR_KEYS].astype(jnp.float32), precision=HIGH
        )
        grad_near_keys = jnp.einsum(
            RULE_14,
            grad_logits,
            saved[KEEP_QUERY_PLAIN].astype(jnp.float32),
            precision=HIGH,
        )
        extra_key = place_rows(grad_near_keys, neighbours)
        extra_value = place_rows(grad_near_values, neighbours)
        grad_gate_layer = jnp.einsum(
            "sic,sih->ch", normal_rows, grad_gate_logit, preferred_element_type=jnp.float32
        )
    else:
        grad_attended = grad_mixture
    grad_query_rot, grad_key_rot, grad_value_all = lax.map(
        lambda items: attend_backward(*items),
        (
            saved[KEEP_QUERY_ROT],
            saved[KEEP_KEY_ROT],
            saved[KEEP_VALUE_ALL],
            resets,
            saved[KEEP_LOG_TOTAL],
            grad_attended,
        ),
    )
    cosine_rows, sine_rows = turning(SEG, MEM)
    cosine_mem, sine_mem = turning(MEM, 0)
    grad_query = flat_low(rotate(grad_query_rot, cosine_rows, -sine_rows) + extra_query)
    grad_key_mem = flat_low(rotate(grad_key_rot[:, :MEM], cosine_mem, -sine_mem) + extra_key)
    grad_key_rows = flat_low(rotate(grad_key_rot[:, MEM:], cosine_rows, -sine_rows))
    grad_value_mem = flat_low(grad_value_all[:, :MEM] + extra_value)
    grad_value_rows = flat_low(grad_value_all[:, MEM:])
    grad_qkv_layer = jnp.stack(
        [
            jnp.einsum(RULE_4, normal_rows, grad_query, preferred_element_type=jnp.float32),
            jnp.einsum(
                RULE_4, normal_rows, grad_key_rows, preferred_element_type=jnp.float32
            )
            + jnp.einsum(
                RULE_18, normal_mem, grad_key_mem, preferred_element_type=jnp.float32
            ),
            jnp.einsum(
                RULE_4, normal_rows, grad_value_rows, preferred_element_type=jnp.float32
            )
            + jnp.einsum(
                RULE_18, normal_mem, grad_value_mem, preferred_element_type=jnp.float32
            ),
        ]
    )
    rows_term = (
        jnp.einsum(RULE_9, grad_query, qkv_layer[0], preferred_element_type=jnp.float32)
        + jnp.einsum(RULE_9, grad_key_rows, qkv_layer[1], preferred_element_type=jnp.float32)
        + jnp.einsum(
            RULE_9, grad_value_rows, qkv_layer[2], preferred_element_type=jnp.float32
        )
    )
    if retrieve:
        rows_term = rows_term + jnp.einsum(
            "sih,ch->sic", grad_gate_logit, gate_cols, preferred_element_type=jnp.float32
        )
    grad_normal = spread_grads(rows_term)
    grad_normal_mem = jnp.einsum(
        RULE_19, grad_key_mem, qkv_layer[1], preferred_element_type=jnp.float32
    ) + jnp.einsum(RULE_19, grad_value_mem, qkv_layer[2], preferred_element_type=jnp.float32)
    grad_gain_mem = jnp.sum(grad_normal_mem * normed(memory.astype(jnp.float32), 1.0), axis=(0, 1))
    _, pullback = jax.vjp(normed, saved[KEEP_HIDDEN], gain_row)
    grad_inputs, grad_gain_part = pullback(grad_normal)
    return (
        grad_hidden + grad_inputs,
        grad_qkv_layer,
        grad_out_layer,
        grad_gain_part + grad_gain_mem,
        grad_gate_layer,
    )


def feed_forward(hidden, up_layer, down_layer, gain_row):
    up_whole, down_whole = (up_layer, down_layer)
    normal_rows = collect_rows(normed(hidden, gain_row).astype(jnp.bfloat16))
    pre_active = jnp.dot(normal_rows, up_whole, preferred_element_type=jnp.float32)
    active = jax.nn.gelu(pre_active).astype(jnp.bfloat16)
    branch_out = jnp.dot(active, down_whole, preferred_element_type=jnp.float32)
    hidden_new = hidden + spread_rows(branch_out)
    saved = {
        KEEP_HIDDEN: hidden,
        KEEP_NORMAL_ROWS: normal_rows,
        KEEP_PRE_ACTIVE: pre_active,
        KEEP_ACTIVE: active,
        KEEP_UP_WHOLE: up_whole,
        KEEP_DOWN_WHOLE: down_whole,
    }
    return (hidden_new, saved)


def feed_backward(grad_hidden, saved, gain_row):
    grad_full = collect_grads(grad_hidden.astype(jnp.bfloat16))
    grad_down = jnp.einsum(
        "sif,sid->fd", saved[KEEP_ACTIVE], grad_full, preferred_element_type=jnp.float32
    )
    grad_active = jnp.einsum(
        "sid,fd->sif", grad_full, saved[KEEP_DOWN_WHOLE], preferred_element_type=jnp.float32
    )
    _, gelu_pull = jax.vjp(jax.nn.gelu, saved[KEEP_PRE_ACTIVE])
    grad_pre = gelu_pull(grad_active)[0].astype(jnp.bfloat16)
    grad_up = jnp.einsum(
        "sic,sif->cf", saved[KEEP_NORMAL_ROWS], grad_pre, preferred_element_type=jnp.float32
    )
    rows_term = jnp.einsum(
        "sif,cf->sic", grad_pre, saved[KEEP_UP_WHOLE], preferred_element_type=jnp.float32
    )
    grad_normal = spread_grads(rows_term)
    _, pullback = jax.vjp(normed, saved[KEEP_HIDDEN], gain_row)
    grad_inputs, grad_gain_part = pullback(grad_normal)
    return (grad_hidden + grad_inputs, grad_up, grad_down, grad_gain_part)


def adamw(weight, first, second, average, grad, rate, decay):
    ema_keep = min(0.999, (1.0 + STEP) / (10.0 + STEP))
    first_new = BETA_ONE * first + (1.0 - BETA_ONE) * grad
    second_new = BETA_TWO * second + (1.0 - BETA_TWO) * grad * grad
    first_hat = first_new / (1.0 - BETA_ONE**STEP)
    second_hat = second_new / (1.0 - BETA_TWO**STEP)
    weight_new = weight - rate * (first_hat / (jnp.sqrt(second_hat) + EPS_ADAM) + decay * weight)
    average_new = ema_keep * average + (1.0 - ema_keep) * weight_new
    return (first_new, second_new, weight_new, average_new)


def body(
    activations,
    memory_one,
    memory_two,
    neighbours,
    resets,
    cotangent,
    qkv_weight,
    qkv_first,
    qkv_second,
    qkv_ema,
    out_weight,
    out_first,
    out_second,
    out_ema,
    up_weight,
    up_first,
    up_second,
    up_ema,
    down_weight,
    down_first,
    down_second,
    down_ema,
    gain_rows,
    gain_first,
    gain_second,
    gain_ema,
    gate_weight,
    gate_first,
    gate_second,
    gate_ema,
):
    qkv_full, out_full, up_full, down_full, gains_full, gate_full = (
        lax.all_gather(qkv_weight.astype(jnp.bfloat16), DP, axis=2, tiled=True),
        lax.all_gather(out_weight.astype(jnp.bfloat16), DP, axis=2, tiled=True),
        lax.all_gather(up_weight.astype(jnp.bfloat16), DP, axis=1, tiled=True),
        lax.all_gather(down_weight.astype(jnp.bfloat16), DP, axis=2, tiled=True),
        lax.all_gather(gain_rows.astype(jnp.bfloat16), DP, axis=1, tiled=True),
        lax.all_gather(gate_weight.astype(jnp.bfloat16), DP, axis=0, tiled=True),
    )
    gain_values = gains_full.astype(jnp.float32)
    memories = (memory_one, memory_two)
    hidden = activations.astype(jnp.float32)
    saved_attention = []
    saved_feed = []
    for depth in range(2):
        hidden, saved = attention_forward(
            hidden,
            memories[depth],
            neighbours,
            resets,
            qkv_full[depth],
            out_full[depth],
            gain_values[2 * depth],
            gate_full,
            depth == 1,
        )
        saved_attention.append(saved)
        hidden, saved = feed_forward(
            hidden, up_full[depth], down_full[depth], gain_values[2 * depth + 1]
        )
        saved_feed.append(saved)
    result_rows = hidden.astype(jnp.bfloat16)
    grad_hidden = cotangent.astype(jnp.float32)
    grad_qkv_list = [None, None]
    grad_out_list = [None, None]
    grad_up_list = [None, None]
    grad_down_list = [None, None]
    grad_gain_list = [None, None, None, None]
    grad_gate = None
    for depth in (1, 0):
        grad_hidden, grad_up_list[depth], grad_down_list[depth], grad_gain_list[2 * depth + 1] = (
            feed_backward(grad_hidden, saved_feed[depth], gain_values[2 * depth + 1])
        )
        (
            grad_hidden,
            grad_qkv_list[depth],
            grad_out_list[depth],
            grad_gain_list[2 * depth],
            gate_part,
        ) = attention_backward(
            grad_hidden,
            saved_attention[depth],
            memories[depth],
            neighbours,
            resets,
            qkv_full[depth],
            out_full[depth],
            gain_values[2 * depth],
            gate_full,
            depth == 1,
        )
        if depth == 1:
            grad_gate = gate_part
    grad_qkv = jnp.stack(grad_qkv_list)
    grad_out = jnp.stack(grad_out_list)
    grad_up = jnp.stack(grad_up_list)
    grad_down = jnp.stack(grad_down_list)
    grad_gains = jnp.stack(grad_gain_list)
    grad_qkv, grad_out, grad_up, grad_down, gain_part, grad_gate = (
        lax.psum_scatter(grad_qkv, DP, scatter_dimension=2, tiled=True),
        lax.psum_scatter(grad_out, DP, scatter_dimension=2, tiled=True),
        lax.psum_scatter(grad_up, DP, scatter_dimension=1, tiled=True),
        lax.psum_scatter(grad_down, DP, scatter_dimension=2, tiled=True),
        lax.psum_scatter(grad_gains, DP, scatter_dimension=1, tiled=True),
        lax.psum_scatter(grad_gate, DP, scatter_dimension=0, tiled=True),
    )
    grad_gains = lax.psum(gain_part, TENSOR)
    local_squares = sum(
        (
            jnp.sum(piece_grad * piece_grad)
            for piece_grad in (grad_qkv, grad_out, grad_up, grad_down, grad_gate)
        )
    )
    local_squares = local_squares + jnp.sum(grad_gains * grad_gains) / lax.axis_size(TENSOR)
    squares = lax.psum(local_squares, (DP, TENSOR))
    grad_norm = jnp.sqrt(squares)
    factor = CLIP / jnp.maximum(grad_norm, CLIP)
    masters = (qkv_weight, out_weight, up_weight, down_weight, gain_rows, gate_weight)
    firsts = (qkv_first, out_first, up_first, down_first, gain_first, gate_first)
    seconds = (qkv_second, out_second, up_second, down_second, gain_second, gate_second)
    averages = (qkv_ema, out_ema, up_ema, down_ema, gain_ema, gate_ema)
    grads = (grad_qkv, grad_out, grad_up, grad_down, grad_gains, grad_gate)
    updated = []
    for group in range(6):
        updated.append(
            adamw(
                masters[group],
                firsts[group],
                seconds[group],
                averages[group],
                grads[group] * factor,
                STEP_RATES[group],
                STEP_DECAYS[group],
            )
        )
    feed_gain_grads = jnp.stack([grad_gains[1], grad_gains[3]]) * factor
    return (
        result_rows,
        grad_hidden,
        grad_norm,
        updated[0][0],
        updated[0][1],
        updated[0][2],
        updated[0][3],
        updated[1][0],
        updated[1][1],
        updated[1][2],
        updated[1][3],
        updated[2][0],
        updated[2][1],
        updated[2][2],
        updated[2][3],
        updated[3][0],
        updated[3][1],
        updated[3][2],
        updated[3][3],
        updated[4][0],
        updated[4][1],
        updated[4][2],
        updated[4][3],
        updated[5][0],
        updated[5][1],
        updated[5][2],
        updated[5][3],
        feed_gain_grads,
    )


VMEM_BYTES = 60 * 1024 * 1024
LOW = jnp.bfloat16
F32 = jnp.float32
WIDE = 128


def nn(left, right):
    return lax.dot_general(left, right, (((1,), (0,)), ((), ())), preferred_element_type=F32)


def nt(left, right):
    return lax.dot_general(left, right, (((1,), (1,)), ((), ())), preferred_element_type=F32)


def unit_rows(values):
    spread = lax.rsqrt(jnp.mean(values * values, axis=-1, keepdims=True) + 1e-06)
    return values * spread, spread


def low_normal(values, gain):
    hat, _ = unit_rows(values.astype(F32))
    return (hat * gain).astype(LOW)


def norm_back_rows(values, gain, grad_normal, grad):
    hat, spread = unit_rows(values.astype(F32))
    return grad.astype(F32) + norm_back(hat, spread, gain, grad_normal)


def norm_back(hat, spread, gain, grad_normal):
    scaled = grad_normal * gain
    inner = jnp.mean(scaled * hat, axis=-1, keepdims=True)
    return spread * (scaled - hat * inner)


def turn_store(target, base, columns, values, cosine, sine, scale):
    half = HEAD_DIM // 2
    first = values[:half]
    second = values[half:]
    target[base : base + half, columns] = ((first * cosine - second * sine).astype(LOW) * scale).astype(LOW)
    target[base + half : base + 2 * half, columns] = (
        (first * sine + second * cosine).astype(LOW) * scale
    ).astype(LOW)


def turned_back(values, cosine, sine):
    half = HEAD_DIM // 2
    first = values[:half]
    second = values[half:]
    return jnp.concatenate(
        [first * cosine + second * sine, second * cosine - first * sine], axis=0
    )


def per_head(values):
    return values.reshape(values.shape[0] // HEAD_DIM, HEAD_DIM, values.shape[1])


def head_sums(values):
    return jnp.sum(per_head(values), axis=1)


def spread_heads(values, like):
    return jnp.broadcast_to(values[:, None, :], (values.shape[0], HEAD_DIM, values.shape[1])).reshape(like)


def later(scores):
    count = scores.shape[1]
    place = lax.broadcasted_iota(jnp.int32, (count, count), 0)
    row = lax.broadcasted_iota(jnp.int32, (count, count), 1)
    own = jnp.where(place <= row, scores[-count:], -1e30)
    return jnp.concatenate([scores[:-count], own], axis=0)


def three_parts(values):
    high = values.astype(LOW).astype(F32)
    rest = values - high
    middle = rest.astype(LOW).astype(F32)
    return high, middle, rest - middle


def with_rows(top, first, parts):
    count = top.shape[1]
    row = lax.broadcasted_iota(jnp.int32, (16, count), 0)
    under = jnp.where(row == 0, first, 0.0)
    for index, part in enumerate(parts):
        under = jnp.where(row == index + 1, part, under)
    blank = jnp.zeros((WIDE - HEAD_DIM - 16, count), LOW)
    return jnp.concatenate([top, under.astype(LOW), blank], axis=0)


def extra_rows(count, bias):
    row = lax.broadcasted_iota(jnp.int32, (WIDE - HEAD_DIM, count), 0)
    place = lax.broadcasted_iota(jnp.int32, (WIDE - HEAD_DIM, count), 1)
    first = jnp.where(place < MEM, bias, 0.0)
    return jnp.where(row == 0, first, jnp.where(row <= 3, 1.0, 0.0)).astype(LOW)


ROWS = 256
BEGIN = -1
POST = -2
END = -3


def retrieved(near, c_ref, v_ref):
    place = lax.broadcasted_iota(jnp.int32, (MEM, SEG), 0)
    chosen = [(place == near[0, r : r + 1, :]).astype(F32).astype(LOW) for r in range(near.shape[1])]
    keys = [nn(c_ref[0], c).astype(LOW) for c in chosen]
    values = [nn(v_ref[0, :, :MEM], c).astype(LOW) for c in chosen]
    return keys, values, chosen


def column_sum(values):
    return jnp.sum(values, axis=0, keepdims=True)


def near_weights(plain, keys):
    logits = [column_sum(plain * key.astype(F32)) * HEAD_DIM ** (-0.5) for key in keys]
    top = functools.reduce(jnp.maximum, logits)
    raised = [jnp.exp(logit - top) for logit in logits]
    inverse = 1.0 / functools.reduce(jnp.add, raised)
    return [e * inverse for e in raised]


def weigh(soft, values):
    return functools.reduce(jnp.add, [a * v.astype(F32) for a, v in zip(soft, values)])


def small_row(small, row):
    return small[0].astype(F32).T[row : row + 1]


def gate_logits(small, normal, heads):
    each = heads // small.shape[0]
    rows = [small[part].astype(F32).T[:each] for part in range(small.shape[0])]
    blank = jnp.zeros((WIDE - heads, small.shape[1]), F32)
    return nn(jnp.concatenate(rows + [blank], axis=0).astype(LOW), normal)[:heads]


def attend_kernel(retrieve, guest, *refs):
    refs = list(refs)
    resets, hidden, memory, slab, small, cosine, sine = refs[:7]
    refs = refs[7:]
    if retrieve:
        near = refs.pop(0)
    guest_ins, refs = refs[: guest.ins], refs[guest.ins :]
    out, q_ref, k_ref, v_ref, log_ref, mix_ref = refs[:6]
    refs = refs[6:]
    if retrieve:
        o_ref, qu_ref, c_ref = refs[:3]
        refs = refs[3:]
    guest_outs, refs = refs[: guest.outs], refs[guest.outs :]
    turned, k_rows, n_both = refs[:3]
    step = pl.program_id(0)
    visit = guest.bind(guest_ins, guest_outs, refs[3:], step)
    parts, width, _ = slab.shape
    visit(BEGIN)
    gain = small_row(small, guest.gain_row)
    cols = width // parts
    pairs = width // WIDE

    @pl.when(step == 0)
    def _():
        for part in range(parts):
            for kind in range(3):
                turned[pl.ds(kind * width + part * cols, cols), :] = slab[
                    part, :, kind * cols : (kind + 1) * cols
                ].T

    bias = jnp.where(resets[lax.axis_index(TENSOR) * pl.num_programs(0) + step] == 0, 0.0, -1e30)
    n_both[:, MEM:] = low_normal(hidden[0], gain).T
    n_both[:, :MEM] = low_normal(memory[0], gain).T
    scale = HEAD_DIM ** (-0.5)
    all_rows = slice(None)
    query = nn(turned[:width], n_both[:, MEM:])
    for head in range(width // HEAD_DIM):
        base = head * HEAD_DIM
        turn_store(
            q_ref.at[0], base, all_rows, query[base : base + HEAD_DIM], cosine[:, MEM:], sine[:, MEM:], scale
        )
    if retrieve:
        qu_ref[0] = query.astype(LOW)
    keys = nn(turned[width : 2 * width], n_both[...])
    for head in range(width // HEAD_DIM):
        base = head * HEAD_DIM
        turn_store(k_ref.at[0], base, all_rows, keys[base : base + HEAD_DIM], cosine[...], sine[...], 1.0)
    if retrieve:
        c_ref[0] = keys[:, :MEM].astype(LOW)
    v_ref[0] = nn(turned[2 * width :], n_both[...]).astype(LOW)
    extra = extra_rows(k_ref.shape[2], bias)
    for head in range(width // HEAD_DIM):
        own = slice(head * HEAD_DIM, (head + 1) * HEAD_DIM)
        k_rows[head] = jnp.concatenate([k_ref[0, own, :], extra], axis=0).T

    def head_pair(pair, carry):
        visit(pair)
        for which in range(2):
            head = pair * 2 + which
            own = pl.ds(pl.multiple_of(head * HEAD_DIM, HEAD_DIM), HEAD_DIM)
            for block in range(SEG // ROWS):
                count = MEM + (block + 1) * ROWS
                span = slice(block * ROWS, (block + 1) * ROWS)
                wanted = with_rows(q_ref[0, own, span], 1.0, ())
                scores = later(nn(k_rows[head, :count], wanted))
                top = jnp.max(scores, axis=0, keepdims=True)
                soft = jnp.exp(scores - top)
                total = jnp.sum(soft, axis=0, keepdims=True)
                got = nn(v_ref[0, own, :count], soft.astype(LOW)) * (1.0 / total)
                log_ref[0, pl.ds(head, 1), span] = top + jnp.log(total)
                if retrieve:
                    o_ref[0, own, span] = got
                else:
                    mix_ref[0, own, span] = got.astype(LOW)
        return carry

    lax.fori_loop(0, pairs, head_pair, 0)
    visit(POST)
    if retrieve:
        keys_near, values_near, _ = retrieved(near, c_ref, v_ref)
        opened = jax.nn.sigmoid(gate_logits(small, n_both[:, MEM:], width // HEAD_DIM))
        for head in range(width // HEAD_DIM):
            own = slice(head * HEAD_DIM, (head + 1) * HEAD_DIM)
            soft = near_weights(qu_ref[0, own, :].astype(F32), [a[own] for a in keys_near])
            fetched = weigh(soft, [a[own] for a in values_near])
            gate = opened[head : head + 1]
            mix_ref[0, own, :] = (gate * o_ref[0, own, :] + (1.0 - gate) * fetched).astype(LOW)
    mix = mix_ref[0].T
    total = hidden[0].astype(F32)
    for part in range(parts):
        total = total + nt(mix[:, part * cols : (part + 1) * cols], slab[part, :, 3 * cols : 4 * cols])
    out[0] = total
    visit(END)


def attend_back_kernel(retrieve, guest, *refs):
    refs = list(refs)
    resets, hidden, memory, slab, small, cosine, sine = refs[:7]
    grad, q_ref, k_ref, v_ref, log_ref, mix_ref = refs[7:13]
    refs = refs[13:]
    if retrieve:
        near, o_ref, qu_ref, c_ref = refs[:4]
        refs = refs[4:]
    guest_ins, refs = refs[: guest.ins], refs[guest.ins :]
    grad_in, grad_slab = refs[:2]
    refs = refs[2:]
    if not retrieve:
        away = refs.pop(0)
    guest_outs, refs = refs[: guest.outs], refs[guest.outs :]
    wo, k_rows, v_rows, n_both, do, dq, dk, dv, total, inner_ref = refs[:10]
    visit = guest.bind(guest_ins, guest_outs, refs[10:], pl.program_id(0))
    visit(BEGIN)
    gain = small_row(small, guest.gain_row)
    parts, width, _ = slab.shape
    cols = width // parts
    pairs = width // WIDE
    heads = width // HEAD_DIM
    step = pl.program_id(0)

    @pl.when(step == 0)
    def _():
        total[...] = jnp.zeros_like(total)
        for part in range(parts):
            wo[pl.ds(part * cols, cols), :] = slab[part, :, 3 * cols : 4 * cols].T

    bias = jnp.where(resets[lax.axis_index(TENSOR) * pl.num_programs(0) + step] == 0, 0.0, -1e30)
    scale = HEAD_DIM ** (-0.5)
    n_both[:, MEM:] = low_normal(hidden[0], gain).T
    n_both[:, :MEM] = low_normal(memory[0], gain).T
    grad_low = grad[0].astype(LOW)
    grad_t = grad_low.T
    for part in range(parts):
        total[part, :, 3 * cols : 4 * cols] += nt(grad_t, mix_ref[0, part * cols : (part + 1) * cols, :])
    grad_mix = nn(wo[...], grad_t).astype(LOW)
    if retrieve:
        keys_near, values_near, chosen = retrieved(near, c_ref, v_ref)
        opened = jax.nn.sigmoid(gate_logits(small, n_both[:, MEM:], heads))
        gate_rows, extra_q = [], []
        near_k, near_v = [[] for _ in chosen], [[] for _ in chosen]
        for head in range(heads):
            own = slice(head * HEAD_DIM, (head + 1) * HEAD_DIM)
            plain = qu_ref[0, own, :].astype(F32)
            keys, values = [a[own] for a in keys_near], [a[own] for a in values_near]
            soft = near_weights(plain, keys)
            gate = opened[head : head + 1]
            grads = grad_mix[own].astype(F32)
            attended = o_ref[0, own, :]
            grad_attended = (gate * grads).astype(LOW)
            do[own, :] = grad_attended
            inner_ref[head : head + 1, :] = column_sum(grad_attended.astype(F32) * attended)
            gate_sum = column_sum(grads * (attended - weigh(soft, values)))
            gate_rows.append(gate_sum * gate * (1.0 - gate))
            grad_fetched = (1.0 - gate) * grads
            grad_soft = [column_sum(grad_fetched * v.astype(F32)) for v in values]
            mean = functools.reduce(jnp.add, [a * b for a, b in zip(soft, grad_soft)])
            grad_logits = [a * (b - mean) * scale for a, b in zip(soft, grad_soft)]
            extra_q.append(weigh(grad_logits, keys))
            for r in range(len(chosen)):
                near_k[r].append((grad_logits[r] * plain).astype(LOW))
                near_v[r].append((soft[r] * grad_fetched).astype(LOW))
        grad_gate = jnp.concatenate(gate_rows, axis=0)
        both = jnp.concatenate(chosen, axis=1)
        extra_k = nt(jnp.concatenate([jnp.concatenate(a, axis=0) for a in near_k], axis=1), both)
        extra_v = nt(jnp.concatenate([jnp.concatenate(a, axis=0) for a in near_v], axis=1), both)
    else:
        do[...] = grad_mix
        for head in range(heads):
            own = slice(head * HEAD_DIM, (head + 1) * HEAD_DIM)
            inner_ref[head : head + 1, :] = column_sum(
                grad_mix[own].astype(F32) * mix_ref[0, own, :].astype(F32)
            )
    extra = extra_rows(k_ref.shape[2], bias)
    for head in range(heads):
        own = slice(head * HEAD_DIM, (head + 1) * HEAD_DIM)
        k_rows[head] = jnp.concatenate([k_ref[0, own, :], extra], axis=0).T
        v_rows[head] = jnp.concatenate([v_ref[0, own, :], extra], axis=0).T

    def head_pair(pair, carry):
        visit(pair)
        for which in range(2):
            head = pair * 2 + which
            own = pl.ds(pl.multiple_of(head * HEAD_DIM, HEAD_DIM), HEAD_DIM)
            row = pl.ds(head, 1)
            for block in reversed(range(SEG // ROWS)):
                count = MEM + (block + 1) * ROWS
                span = slice(block * ROWS, (block + 1) * ROWS)
                wanted = with_rows(q_ref[0, own, span], 1.0, three_parts(-log_ref[0, row, span]))
                grad_o = with_rows(do[own, span], 0.0, three_parts(-inner_ref[row, span]))
                probs = jnp.exp(later(nn(k_rows[head, :count], wanted)))
                probs_low = probs.astype(LOW)
                grad_scores = (probs * nn(v_rows[head, :count], grad_o)).astype(LOW)
                dq[own, span] = nn(k_ref[0, own, :count], grad_scores) * scale
                key_part = nt(q_ref[0, own, span], grad_scores)
                value_part = nt(do[own, span], probs_low)
                if block == SEG // ROWS - 1:
                    dk[own, :] = key_part
                    dv[own, :] = value_part
                else:
                    dk[own, :count] += key_part
                    dv[own, :count] += value_part
        return carry

    lax.fori_loop(0, pairs, head_pair, 0)
    visit(POST)
    cos_rows, sin_rows = cosine[:, MEM:], sine[:, MEM:]
    turned_q = []
    turned_k = []
    for head in range(heads):
        own = slice(head * HEAD_DIM, (head + 1) * HEAD_DIM)
        turned_q.append(turned_back(dq[own, :], cos_rows, sin_rows))
        turned_k.append(turned_back(dk[own, :], cosine[...], sine[...]))
    grad_q = jnp.concatenate(turned_q, axis=0)
    grad_k = jnp.concatenate(turned_k, axis=0)
    grad_v = dv[...]
    if retrieve:
        grad_q = grad_q + jnp.concatenate(extra_q, axis=0)
        grad_k = jnp.concatenate([grad_k[:, :MEM] + extra_k, grad_k[:, MEM:]], axis=1)
        grad_v = jnp.concatenate([grad_v[:, :MEM] + extra_v, grad_v[:, MEM:]], axis=1)
    grad_q = grad_q.astype(LOW)
    grad_k = grad_k.astype(LOW)
    grad_v = grad_v.astype(LOW)
    normal_t = jnp.zeros((width, SEG), F32)
    for part in range(parts):
        own = slice(part * cols, (part + 1) * cols)
        total[part, :, :cols] += nt(n_both[:, MEM:], grad_q[own])
        total[part, :, cols : 2 * cols] += nt(n_both[...], grad_k[own])
        total[part, :, 2 * cols : 3 * cols] += nt(n_both[...], grad_v[own])
        normal_t = (
            normal_t
            + nn(slab[part, :, :cols], grad_q[own])
            + nn(slab[part, :, cols : 2 * cols], grad_k[own, MEM:])
            + nn(slab[part, :, 2 * cols : 3 * cols], grad_v[own, MEM:])
        )
    if retrieve:
        each = heads // parts
        blank = jnp.zeros((WIDE - each, SEG), F32)
        for part in range(parts):
            own_gate = jnp.concatenate([grad_gate[part * each : (part + 1) * each], blank], axis=0)
            own_gate = own_gate.astype(LOW)
            normal_t = normal_t + nn(small[part], own_gate)
            total[part, :, 4 * cols :] += nt(n_both[:, MEM:], own_gate)
    grad_in[0] = norm_back_rows(hidden[0], gain, normal_t.T, grad[0])
    if not retrieve:
        half = away.shape[1]
        other = pl.multiple_of((1 - lax.axis_index(TENSOR)) * half, half)
        away[0] = grad_in[0, pl.ds(other, half), :].astype(LOW)

    @pl.when(step == pl.num_programs(0) - 1)
    def _():
        grad_slab[...] = total[...].astype(grad_slab.dtype)

    visit(END)


GELU_A = math.sqrt(2.0 / math.pi)
GELU_B = 0.044715


def feed_kernel(guest, *refs):
    hidden, small, up, down = refs[:4]
    guest_ins, refs = refs[4 : 4 + guest.ins], refs[4 + guest.ins :]
    out, guest_outs, refs = refs[0], refs[1 : 1 + guest.outs], refs[1 + guest.outs :]
    normal = refs[0]
    visit = guest.bind(guest_ins, guest_outs, refs[1:], pl.program_id(0))
    visit(BEGIN)

    @pl.when(pl.program_id(0) == 0)
    def _():
        rows = hidden[...]
        normal[...] = low_normal(rows, small_row(small, guest.gain_row))
        out[...] = rows

    pre = nn(normal[...], up[0])
    bent = jnp.tanh(GELU_A * (pre + GELU_B * (pre * pre * pre)))
    active = (0.5 * pre * (1.0 + bent)).astype(LOW)
    out[...] += nt(active, down[0])
    visit(END)


def feed_back_kernel(ahead, guest, *refs):
    hidden, small, up, down, grad = refs[:5]
    refs = list(refs[5:])
    guest_ins, refs = refs[: guest.ins], refs[guest.ins :]
    if ahead:
        result = refs.pop(0)
    grad_in, grad_slab = refs[:2]
    guest_outs, refs = refs[2 : 2 + guest.outs], refs[2 + guest.outs :]
    normal, normal_t, grad_low, grad_t, total = refs[:5]
    refs = refs[5:]
    if ahead:
        rows_out = refs.pop(0)
    visit = guest.bind(guest_ins, guest_outs, refs, pl.program_id(0))
    visit(BEGIN)

    @pl.when(pl.program_id(0) == 0)
    def _():
        low = low_normal(hidden[...], small_row(small, guest.gain_row))
        normal[...] = low
        normal_t[...] = low.T
        start = grad[...].astype(LOW)
        grad_low[...] = start
        grad_t[...] = start.T
        total[...] = jnp.zeros_like(total)
        if ahead:
            rows_out[...] = hidden[...]

    pre = nn(normal[...], up[0])
    square = pre * pre
    bent = jnp.tanh(GELU_A * (pre + GELU_B * (square * pre)))
    active = (0.5 * pre * (1.0 + bent)).astype(LOW)
    if ahead:
        rows_out[...] += nt(active, down[0])
    slope = 0.5 * (1.0 + bent) + 0.5 * pre * (1.0 - bent * bent) * (
        GELU_A * (1.0 + 3.0 * GELU_B * square)
    )
    grad_pre = (nn(grad_low[...], down[0]) * slope).astype(LOW)
    grad_slab[0, 0] = nn(normal_t[...], grad_pre).astype(grad_slab.dtype)
    grad_slab[1, 0] = nn(grad_t[...], active).astype(grad_slab.dtype)
    total[...] += nt(grad_pre, up[0])

    @pl.when(pl.program_id(0) == pl.num_programs(0) - 1)
    def _():
        gain = small_row(small, guest.gain_row)
        grad_in[...] = norm_back_rows(hidden[...], gain, total[...], grad[...])
        if ahead:
            result[...] = rows_out[...].astype(LOW)

    visit(END)


def whole_spec(shape):
    return pl.BlockSpec(shape, lambda i: (0,) * len(shape))


def seg_spec(shape):
    return pl.BlockSpec((1,) + tuple(shape[1:]), lambda i: (i,) + (0,) * (len(shape) - 1))


def cost(flops, moved):
    return pl.CostEstimate(flops=int(flops), bytes_accessed=int(moved), transcendentals=0)


def any_spec():
    return pl.BlockSpec(memory_space=pl.ANY)


def slab_specs(slab, width, cols):
    columns = 4 * cols
    return pl.BlockSpec((slab.shape[0], width, columns), lambda i: (0, 0, 0))


def small_spec(slab):
    last = slab.shape[2] // WIDE - 1
    return pl.BlockSpec((slab.shape[0], slab.shape[1], WIDE), lambda i: (0, 0, last))


def run(kernel, guest, grid, ins, specs, outs, out_specs, scratch, flops, moved):
    more_ins, more_outs, more_out_specs, more_scratch = guest.parts()
    params = dict(vmem_limit_bytes=VMEM_BYTES)
    if guest.number is not None:
        params.update(collective_id=guest.number, has_side_effects=True)
    return pl.pallas_call(
        kernel,
        grid=(grid,),
        in_specs=specs + [any_spec()] * len(more_ins),
        out_specs=out_specs + more_out_specs,
        out_shape=outs + more_outs,
        scratch_shapes=scratch + more_scratch,
        compiler_params=pltpu.CompilerParams(**params),
        cost_estimate=cost(flops, moved),
        input_output_aliases=guest.aliases(len(ins), len(outs)),
    )(*ins, *more_ins)


def attend(hidden, memory, resets, slab, small, cosine, sine, near, guest):
    retrieve = near is not None
    count, rows, width = hidden.shape
    keys = memory.shape[1] + rows
    heads = width // HEAD_DIM
    cols = width // slab.shape[0]
    ins = [resets, hidden, memory, slab, small, cosine, sine]
    specs = [pl.BlockSpec(memory_space=pltpu.SMEM), seg_spec(hidden.shape), seg_spec(memory.shape)]
    specs += [slab_specs(slab, width, cols), small_spec(small)]
    specs += [whole_spec(cosine.shape), whole_spec(sine.shape)]
    if retrieve:
        ins.append(near)
        specs.append(seg_spec(near.shape))
    outs = [
        jax.ShapeDtypeStruct((count, rows, width), F32),
        jax.ShapeDtypeStruct((count, width, rows), LOW),
        jax.ShapeDtypeStruct((count, width, keys), LOW),
        jax.ShapeDtypeStruct((count, width, keys), LOW),
        jax.ShapeDtypeStruct((count, heads, rows), F32),
        jax.ShapeDtypeStruct((count, width, rows), LOW),
    ]
    if retrieve:
        outs += [
            jax.ShapeDtypeStruct((count, width, rows), F32),
            jax.ShapeDtypeStruct((count, width, rows), LOW),
            jax.ShapeDtypeStruct((count, width, memory.shape[1]), LOW),
        ]
    scratch = [
        pltpu.VMEM((3 * width, width), LOW),
        pltpu.VMEM((heads, keys, WIDE), LOW),
        pltpu.VMEM((width, keys), LOW),
    ]
    kernel = functools.partial(attend_kernel, retrieve, guest)
    out_specs = [seg_spec(o.shape) for o in outs]
    return run(kernel, guest, count, ins, specs, outs, out_specs, scratch, count * 1.2e10, 2e7)


def attend_back(hidden, memory, resets, slab, small, cosine, sine, grad, saved, near, guest):
    retrieve = near is not None
    count, rows, width = hidden.shape
    keys = memory.shape[1] + rows
    heads = width // HEAD_DIM
    parts = slab.shape[0]
    cols = width // parts
    ins = [resets, hidden, memory, slab, small, cosine, sine, grad] + list(saved[:5])
    specs = [pl.BlockSpec(memory_space=pltpu.SMEM), seg_spec(hidden.shape), seg_spec(memory.shape)]
    specs += [slab_specs(slab, width, cols), small_spec(small)]
    specs += [whole_spec(cosine.shape), whole_spec(sine.shape)]
    specs += [seg_spec(a.shape) for a in ins[7:]]
    if retrieve:
        more = [near] + list(saved[5:8])
        ins += more
        specs += [seg_spec(a.shape) for a in more]
    total = (parts, width, 4 * cols + (WIDE if retrieve else 0))
    outs = [
        jax.ShapeDtypeStruct((count, rows, width), F32),
        jax.ShapeDtypeStruct(total, LOW),
    ]
    out_specs = [seg_spec(outs[0].shape), whole_spec(total)]
    if not retrieve:
        outs.append(jax.ShapeDtypeStruct((count, rows // parts, width), LOW))
        out_specs.append(seg_spec(outs[-1].shape))
    scratch = [
        pltpu.VMEM((width, width), LOW),
        pltpu.VMEM((heads, keys, WIDE), LOW),
        pltpu.VMEM((heads, keys, WIDE), LOW),
        pltpu.VMEM((width, keys), LOW),
        pltpu.VMEM((width, rows), LOW),
        pltpu.VMEM((width, rows), F32),
        pltpu.VMEM((width, keys), F32),
        pltpu.VMEM((width, keys), F32),
        pltpu.VMEM(total, F32),
        pltpu.VMEM((heads, rows), F32),
    ]
    kernel = functools.partial(attend_back_kernel, retrieve, guest)
    return run(kernel, guest, count, ins, specs, outs, out_specs, scratch, count * 3e10, 3e7)


def feed_specs(width, units, chunk):
    each = units // chunk
    up = pl.BlockSpec((1, width, chunk), lambda i: (i // each, 0, i % each))
    down = pl.BlockSpec((1, width, chunk), lambda i: (i // each, 0, each + i % each))
    return up, down, each


CHUNK = 512


def feed(hidden, slab, small, guest):
    rows, width = hidden.shape
    parts, _, both = slab.shape
    up, down, each = feed_specs(width, both // 2, CHUNK)
    ins = [hidden, small, slab, slab]
    specs = [whole_spec(hidden.shape), small_spec(small), up, down]
    outs = [jax.ShapeDtypeStruct(hidden.shape, F32)]
    scratch = [pltpu.VMEM((rows, width), LOW)]
    kernel = functools.partial(feed_kernel, guest)
    flops = 2 * rows * width * parts * both
    return run(kernel, guest, parts * each, ins, specs, outs, [whole_spec(hidden.shape)], scratch, flops, 1e7)


def feed_back(hidden, slab, small, grad, ahead, guest):
    rows, width = hidden.shape
    parts, _, both = slab.shape
    units = both // 2
    up, down, each = feed_specs(width, units, CHUNK)
    outs = [
        jax.ShapeDtypeStruct((rows, width), F32),
        jax.ShapeDtypeStruct((2, parts, width, units), LOW),
    ]
    out_specs = [
        whole_spec((rows, width)),
        pl.BlockSpec((2, 1, width, CHUNK), lambda i: (0, i // each, 0, i % each)),
    ]
    scratch = [
        pltpu.VMEM((rows, width), LOW),
        pltpu.VMEM((width, rows), LOW),
        pltpu.VMEM((rows, width), LOW),
        pltpu.VMEM((width, rows), LOW),
        pltpu.VMEM((rows, width), F32),
    ]
    if ahead:
        outs.insert(0, jax.ShapeDtypeStruct((rows, width), LOW))
        out_specs.insert(0, whole_spec((rows, width)))
        scratch.append(pltpu.VMEM((rows, width), F32))
    ins = [hidden, small, slab, slab, grad]
    specs = [whole_spec(hidden.shape), small_spec(small), up, down, whole_spec(grad.shape)]
    kernel = functools.partial(feed_back_kernel, ahead, guest)
    flops = 6 * rows * width * parts * both
    return run(kernel, guest, parts * each, ins, specs, outs, out_specs, scratch, flops, 2e7)


MESH = pl.DeviceIdType.MESH


def spot():
    place = lax.axis_index(DP)
    return place // 4, place // 2 % 2, place % 2, lax.axis_index(TENSOR)


def at(z, x, core, y):
    return ((z * 2 + x) * 2 + core, y)


def announce(partners):
    for partner in partners:
        pl.semaphore_signal(
            pltpu.get_barrier_semaphore(), inc=1, device_id=partner, device_id_type=MESH
        )


def await_all(partners):
    pl.semaphore_wait(pltpu.get_barrier_semaphore(), len(partners))


def greet(partners):
    announce(partners)
    await_all(partners)


def send(source, target, sems, device):
    return pltpu.make_async_remote_copy(
        src_ref=source,
        dst_ref=target,
        send_sem=sems[0],
        recv_sem=sems[1],
        device_id=device,
        device_id_type=MESH,
    )


def halves(cols):
    first = cols // (2 * WIDE) * WIDE
    return pl.ds(0, first), pl.ds(first, cols - first)


class Hop:
    def __init__(self, source, target, buffer, sems):
        self.first = pltpu.make_async_copy(source, buffer, sems.at[0])
        self.second = pltpu.make_async_copy(buffer, target, sems.at[1])

    def start(self):
        self.first.start()

    def push(self):
        self.first.wait()
        self.second.start()

    def wait(self):
        self.second.wait()


class Burst:
    def __init__(self, source, target, sems, device, cuts):
        self.whole = send(source, target, sems, device)
        self.pieces = []
        for place in itertools.product(*[range(cut) for cut in cuts]):
            self.pieces.append(send(source.at[place], target.at[place], sems, device))

    def start(self):
        for piece in self.pieces:
            piece.start()

    def wait(self):
        self.whole.wait()


class Gather:
    def __init__(self, shard, full, sends, receives, local, line=None, buffer=None):
        self.shard, self.full, self.local, self.line, self.buffer = shard, full, local, line, buffer
        self.sems = lambda k: (sends.at[k], receives.at[k])
        self.depth = full.shape[1]
        self.left, self.right = halves(full.shape[-1])

    def sibling(self, source, place, k):
        z, x, core, y = spot()
        return Burst(source, place, self.sems(self.depth + k), at(z, x, 1 - core, y), (self.depth,))

    def along_z(self):
        z, x, core, y = spot()
        mine = self.full.at[y, z, x, core]
        return [
            send(self.shard, mine, self.sems(k - 1), at((z + k) % self.depth, x, core, y))
            for k in range(1, self.depth)
        ]

    def to_sides(self):
        z, x, core, y = spot()
        mine = self.full.at[y, :, x, core]
        held = mine if self.line is None else self.line
        base = self.depth + 4
        return [
            Burst(held, mine, self.sems(base), at(z, 1 - x, core, y), (self.depth,)),
            Burst(held, mine, self.sems(base + 1), at(z, x, core, 1 - y), (self.depth,)),
            self.sibling(held, mine, 0),
        ]

    def onward(self):
        z, x, core, y = spot()
        base = self.depth + 6
        one = self.full.at[y, :, 1 - x, core]
        two = self.full.at[1 - y, :, x, core]
        left = one.at[:, :, self.left]
        right = two.at[:, :, self.right]
        return [
            Burst(left, left, self.sems(base), at(z, x, core, 1 - y), (self.depth,)),
            Burst(right, right, self.sems(base + 1), at(z, 1 - x, core, y), (self.depth,)),
            self.sibling(one, one, 1),
            self.sibling(two, two, 2),
        ]

    def to_sibling(self):
        z, x, core, y = spot()
        mine = self.full.at[1 - y, :, 1 - x, core]
        return [self.sibling(mine, mine, 3)]

    def keep(self):
        z, x, core, y = spot()
        if self.line is not None:
            return Hop(self.line, self.full.at[y, :, x, core], self.buffer, self.local)
        return pltpu.make_async_copy(self.shard, self.full.at[y, z, x, core], self.local)

    def start(self, phase):
        first = phase == (0 if self.line is None else 1)
        if first:
            self.keep().start()
        for copy in self.phase(phase):
            copy.start()
        if first and self.line is not None:
            self.keep().push()

    def finish(self, phase):
        if phase == (0 if self.line is None else 1):
            self.keep().wait()
        for copy in self.phase(phase):
            copy.wait()

    def phase(self, phase):
        return (self.along_z, self.to_sides, self.onward, self.to_sibling)[phase]()


EXTRA = 8
PHASES = 4


def neighbours_of(depth):
    z, x, core, y = spot()
    around = [at((z + k) % depth, x, core, y) for k in range(1, depth)]
    return around + [at(z, 1 - x, core, y), at(z, x, core, 1 - y), at(z, x, 1 - core, y)]


def pipelined(groups):
    for stage in range(len(groups) + PHASES):
        for index, group in enumerate(groups):
            phase = stage - index
            if 0 < phase <= PHASES:
                group.finish(phase - 1)
            if 0 <= phase < PHASES:
                group.start(phase)


class Line:
    def __init__(self, shard, line, sends, receives, local):
        self.shard, self.line, self.sends, self.receives, self.local = shard, line, sends, receives, local

    def copies(self):
        z, x, core, y = spot()
        depth = self.line.shape[0]
        mine = self.line.at[z]
        away = [
            send(self.shard, mine, (self.sends.at[k], self.receives.at[k]), at((z + k) % depth, x, core, y))
            for k in range(1, depth)
        ]
        return [pltpu.make_async_copy(self.shard, mine, self.local)] + away

    def start(self):
        for copy in self.copies():
            copy.start()

    def finish(self):
        for copy in self.copies():
            copy.wait()


class Trade:
    def __init__(self, source, target, sends, receives, local, buffer, first=0):
        self.source, self.target, self.first = source, target, first
        self.sems, self.local, self.buffer = (sends, receives), local, buffer

    def copies(self):
        z, x, core, y = spot()
        share, rows, count = self.target.shape[0], self.source.shape[1], self.buffer.shape[0]
        place = self.target.at[
            pl.ds(self.first, count), pl.ds(pl.multiple_of(y * rows, rows), rows)
        ]
        mine = self.source.at[pl.ds(y * share + self.first, count)]
        away = self.source.at[pl.ds((1 - y) * share + self.first, count)]
        return [
            Hop(mine, place, self.buffer, self.local),
            send(away, place, self.sems, at(z, x, core, 1 - y)),
        ]

    def start(self):
        copies = self.copies()
        for copy in copies:
            copy.start()
        copies[0].push()

    def finish(self):
        for copy in self.copies():
            copy.wait()


def sems(*counts):
    return [pltpu.SemaphoreType.DMA((count,)) for count in counts]


def trade_buffer(rows, count=None):
    share = rows.shape[0] // lax.axis_size(TENSOR)
    return pltpu.VMEM((count or share,) + rows.shape[1:], rows.dtype)


def columns(ref, first, last):
    return ref.at[(slice(None),) * (len(ref.shape) - 1) + (pl.ds(first, last - first),)]


def start_kernel(*refs):
    qkv, out, up, down, gain, gate, acts, memory_one, memory_two, near = refs[:10]
    attn_one, attn_two, feed_one, feed_two, full, line, rows, own_one, own_two, own_near = refs[10:20]
    sends, receives, local, more_sends, more_receives, trade_sems, own_sems, trade_buffer = refs[20:28]
    buffers = refs[28:]
    cols = out.shape[2]
    units = up.shape[2]
    y = lax.axis_index(TENSOR)
    pairs = ((memory_one, own_one), (memory_two, own_two), (near, own_near))
    owns = [
        Hop(a.at[pl.ds(y * b.shape[0], b.shape[0])], b, buffers[k], own_sems.at[k])
        for k, (a, b) in enumerate(pairs)
    ]

    def pack_attn(target, depth):
        for kind in range(3):
            target[:, kind * cols : (kind + 1) * cols] = qkv[depth, kind].astype(LOW)
        target[:, 3 * cols : 4 * cols] = out[depth].astype(LOW)

    def pack_feed(target, depth):
        target[:, :units] = up[depth].astype(LOW)
        target[:, units:] = down[depth].astype(LOW)

    pack_attn(attn_one, 0)
    blank = jnp.zeros((WIDE - gate.shape[0] - gain.shape[0], gain.shape[1]), F32)
    small = jnp.concatenate([gate[...], gain[...], blank], axis=0)
    attn_one[:, 4 * cols :] = small.T.astype(LOW)
    groups = []
    for g, (first, last) in enumerate(((0, 2 * cols), (2 * cols, 4 * cols + WIDE))):
        part, whole = columns(attn_one, first, last), columns(full, first, last)
        groups.append(Gather(part, whole, sends.at[g], receives.at[g], local.at[g]))
    trade = Trade(acts, rows, more_sends.at[0], more_receives.at[0], trade_sems, trade_buffer)
    fetch = Line(feed_one, line, more_sends, more_receives, local.at[2])
    greet(neighbours_of(groups[0].depth))
    groups[0].start(0)
    trade.start()
    groups[1].start(0)
    for copy in owns:
        copy.start()
    pack_feed(feed_one, 0)
    pack_attn(attn_two, 1)
    pack_feed(feed_two, 1)
    for copy in owns:
        copy.push()
    for phase in range(PHASES):
        for group in groups:
            group.finish(phase)
            if phase + 1 < PHASES:
                group.start(phase + 1)
        if phase == 0:
            fetch.start()
    trade.finish()
    fetch.finish()
    for copy in owns:
        copy.wait()


def start_up(qkv, out, up, down, gain, gate, acts, memory_one, memory_two, near, number):
    depth = lax.axis_size(DP) // 4
    parts = lax.axis_size(TENSOR)
    rows, cols, units = qkv.shape[2], qkv.shape[3], up.shape[2]
    vmem = pl.BlockSpec(memory_space=pltpu.VMEM)
    shapes = [(rows, 4 * cols + WIDE), (rows, 4 * cols), (rows, 2 * units), (rows, 2 * units)]
    shapes += [(parts, depth, 2, 2, rows, 4 * cols + WIDE), (depth, rows, 2 * units)]
    shapes += [(acts.shape[0] // parts, acts.shape[1] * parts, acts.shape[2])]
    outs = [jax.ShapeDtypeStruct(s, LOW) for s in shapes]
    for a in (memory_one, memory_two, near):
        outs.append(jax.ShapeDtypeStruct((a.shape[0] // parts,) + a.shape[1:], a.dtype))
    return pl.pallas_call(
        start_kernel,
        out_shape=outs,
        in_specs=[vmem] * 6 + [any_spec()] * 4,
        out_specs=[vmem] * 4 + [any_spec()] * 6,
        scratch_shapes=[pltpu.SemaphoreType.DMA((2, depth + EXTRA))] * 2
        + sems(3, depth, depth, 2)
        + [pltpu.SemaphoreType.DMA((3, 2)), trade_buffer(acts)]
        + [pltpu.VMEM(o.shape, o.dtype) for o in outs[7:]],
        compiler_params=pltpu.CompilerParams(
            collective_id=number, has_side_effects=True, vmem_limit_bytes=VMEM_BYTES
        ),
    )(qkv, out, up, down, gain, gate, acts, memory_one, memory_two, near)


def flat(full):
    return full.reshape((full.shape[0], -1, full.shape[-1]))


class Reduce:
    def __init__(self, whole, out, own, one, two_left, two_right, three, four, sends, receives, local):
        self.whole, self.out, self.own, self.one = whole, out, own, one
        self.two_left, self.two_right, self.three, self.four = two_left, two_right, three, four
        self.sems = lambda k: (sends.at[k], receives.at[k])
        self.local = local
        self.kinds, self.parts, self.depth = whole.shape[:3]
        self.cols = whole.shape[-1]
        self.left, self.right = halves(self.cols)
        self.cut = self.left.size
        self.cuts = (self.kinds, self.depth)

    def keep(self):
        z, x, core, y = spot()
        return pltpu.make_async_copy(self.whole.at[:, :, :, :, core], self.own, self.local)

    def sibling(self, part, side, k):
        z, x, core, y = spot()
        away = self.whole.at[:, part, :, side, 1 - core]
        return Burst(away, self.one.at[:, part, :, side], self.sems(k), at(z, x, 1 - core, y), self.cuts)

    def first(self):
        z, x, core, y = spot()
        return [self.sibling(1 - y, 1 - x, 0)]

    def second(self):
        z, x, core, y = spot()
        far = self.own.at[:, 1 - y, :, 1 - x]
        return [
            Burst(far.at[:, :, :, self.left], self.two_left, self.sems(1), at(z, 1 - x, core, y), self.cuts),
            Burst(far.at[:, :, :, self.right], self.two_right, self.sems(2), at(z, x, core, 1 - y), self.cuts),
            self.sibling(y, 1 - x, 3),
            self.sibling(1 - y, x, 4),
        ]

    def third(self):
        z, x, core, y = spot()
        return [
            Burst(self.own.at[:, y, :, 1 - x], self.three, self.sems(5), at(z, 1 - x, core, y), self.cuts),
            Burst(self.own.at[:, 1 - y, :, x], self.four, self.sems(6), at(z, x, core, 1 - y), self.cuts),
            self.sibling(y, x, 7),
        ]

    def phase(self, phase):
        return (self.first, self.second, self.third)[phase]()

    def start(self, phase):
        if phase == 0:
            self.keep().start()
        for copy in self.phase(phase):
            copy.start()

    def finish(self, phase):
        if phase == 0:
            self.keep().wait()
        for copy in self.phase(phase):
            copy.wait()
        z, x, core, y = spot()
        own, one = self.own, self.one
        left, right = slice(0, self.cut), slice(self.cut, self.cols)

        def add(place, *sources):
            own[place] = functools.reduce(jnp.add, [s.astype(F32) for s in (own[place],) + sources]).astype(
                own.dtype
            )

        def over_z(k):
            def step(d, carry):
                if phase == 0:
                    add((k, 1 - y, d, 1 - x), one[k, 1 - y, d, 1 - x])
                elif phase == 1:
                    rows = slice(None)
                    add((k, 1 - y, d, x, rows, left), one[k, 1 - y, d, x, :, left], self.two_left[k, d])
                    add((k, 1 - y, d, x, rows, right), one[k, 1 - y, d, x, :, right])
                    add((k, y, d, 1 - x, rows, left), one[k, y, d, 1 - x, :, left])
                    add((k, y, d, 1 - x, rows, right), one[k, y, d, 1 - x, :, right], self.two_right[k, d])
                else:
                    sources = (own[k, y, d, x], one[k, y, d, x], self.three[k, d], self.four[k, d])
                    total = functools.reduce(jnp.add, [s.astype(F32) for s in sources])
                    self.out[k, d] = total.astype(self.out.dtype)
                return carry

            return step

        for k in range(self.kinds):
            lax.fori_loop(0, self.depth, over_z(k), 0)


class AlongZ:
    def __init__(self, partial, out, mine, rest, sends, receives, local):
        self.partial, self.out, self.mine, self.rest = partial, out, mine, rest
        self.sends, self.receives, self.local = sends, receives, local

    def copies(self):
        z, x, core, y = spot()
        depth = self.partial.shape[1]
        copies = [pltpu.make_async_copy(self.partial.at[:, z], self.mine, self.local)]
        for k in range(1, depth):
            to = (z + k) % depth
            pair = (self.sends.at[k], self.receives.at[k])
            copies.append(send(self.partial.at[:, to], self.rest.at[k - 1], pair, at(to, x, core, y)))
        return copies

    def start(self):
        for copy in self.copies():
            copy.start()

    def finish(self):
        for copy in self.copies():
            copy.wait()
        for k in range(self.out.shape[0]):
            total = self.mine[k].astype(F32)
            for other in range(self.rest.shape[0]):
                total = total + self.rest[other, k].astype(F32)
            self.out[k] = total


def along_z_shapes(partial):
    kinds, depth, rows, cols = partial
    return [
        pltpu.VMEM((kinds, rows, cols), LOW),
        pltpu.VMEM((depth - 1, kinds, rows, cols), LOW),
    ] + sems(depth, depth, 1)


def reduce_shapes(whole):
    kinds, parts, depth, _, _, rows, cols = whole.shape
    cut = halves(cols)[0].size
    return [
        pltpu.VMEM((kinds, parts, depth, 2, rows, cols), LOW),
        pltpu.VMEM((kinds, parts, depth, 2, rows, cols), LOW),
        pltpu.VMEM((kinds, depth, rows, cut), LOW),
        pltpu.VMEM((kinds, depth, rows, cols - cut), LOW),
        pltpu.VMEM((kinds, depth, rows, cols), LOW),
        pltpu.VMEM((kinds, depth, rows, cols), LOW),
    ]


PIECES = 6


def on(step, point, here, table):
    for (at_step, at_point), actions in table.items():
        if isinstance(here, int):
            if here != at_point:
                continue
            wanted = step == at_step
        else:
            if at_point < 0:
                continue
            wanted = jnp.logical_and(step == at_step, here == at_point)

        @pl.when(wanted)
        def _(actions=actions):
            for action in actions:
                action()


class Guest:
    ins = outs = 0
    number = None

    def __init__(self, gain_row):
        self.gain_row = gain_row

    def parts(self):
        return [], [], [], []

    def aliases(self, first_in, first_out):
        return {}

    def bind(self, ins, outs, scratch, step):
        table = self.table(ins, outs, scratch)
        return lambda point: on(step, None, point, table)

    def table(self, ins, outs, scratch):
        return {}


def call(method, *args):
    return functools.partial(method, *args)


class FirstForward(Guest):
    ins, outs = 3, 3

    def __init__(self, gain_row, number, line, shard, feed_shard):
        self.gain_row, self.number = gain_row, number
        self.line, self.shard, self.feed_shard = line, shard, feed_shard

    def parts(self):
        parts, depth = lax.axis_size(TENSOR), self.line.shape[0]
        rows = self.shard.shape[0]
        shapes = [(parts, depth, 2, 2, rows, a.shape[-1]) for a in (self.line, self.shard)]
        outs = [jax.ShapeDtypeStruct(s, LOW) for s in shapes + [self.line.shape]]
        scratch = sems(depth + EXTRA, depth + EXTRA, depth + EXTRA, depth + EXTRA, 2, depth, depth, 2)
        scratch.append(pltpu.VMEM(self.line.shape, LOW))
        return [self.line, self.shard, self.feed_shard], outs, [any_spec()] * 3, scratch

    def table(self, ins, outs, scratch):
        sends, receives, more_sends, more_receives, hop, line_sends, line_receives, local, buffer = scratch
        feeds = Gather(None, outs[0], sends, receives, hop, ins[0], buffer)
        attn = Gather(ins[1], outs[1], more_sends, more_receives, local.at[0])
        fetch = Line(ins[2], outs[2], line_sends, line_receives, local.at[1])
        return {
            (0, BEGIN): [call(greet, neighbours_of(attn.depth)), call(attn.start, 0), call(feeds.start, 1)],
            (0, 1): [call(attn.finish, 0)],
            (0, 3): [call(attn.start, 1), fetch.start],
            (0, POST): [call(feeds.finish, 1), call(feeds.start, 2)],
            (1, 1): [call(attn.finish, 1), call(attn.start, 2)],
            (1, 3): [call(feeds.finish, 2), call(feeds.start, 3)],
            (1, END): [fetch.finish, call(attn.finish, 2), call(feeds.finish, 3)],
        }


class MiddleForward(Guest):
    ins, outs = 2, 2

    def __init__(self, gain_row, number, full, rows, early, steps):
        self.gain_row, self.number, self.full, self.steps = gain_row, number, full, steps
        self.rows, self.early = rows, early

    def parts(self):
        depth = self.full.shape[1]
        count, held, width = self.rows.shape
        parts = lax.axis_size(TENSOR)
        outs = [
            jax.ShapeDtypeStruct(self.full.shape, LOW),
            jax.ShapeDtypeStruct((count // parts, held * parts, width), LOW),
        ]
        scratch = sems(depth + EXTRA, depth + EXTRA, 1, 2) + [pltpu.SemaphoreType.DMA] * 2
        scratch.append(trade_buffer(self.rows, self.early))
        return [self.full, self.rows], outs, [any_spec()] * 2, scratch

    def aliases(self, first_in, first_out):
        return {first_in: first_out}

    def table(self, ins, outs, scratch):
        sends, receives, local, hop, one_send, one_receive, buffer = scratch
        attn = Gather(None, outs[0], sends, receives, local.at[0])
        trade = Trade(ins[1], outs[1], one_send, one_receive, hop, buffer)
        return {
            (0, BEGIN): [call(greet, neighbours_of(attn.depth)), call(attn.start, 3), trade.start],
            (self.steps - 1, END): [call(attn.finish, 3), trade.finish],
        }


class SecondForward(Guest):
    ins, outs = 3, 2

    def __init__(self, gain_row, number, line, rows, ending, early):
        self.gain_row, self.number, self.line, self.rows = gain_row, number, line, rows
        self.ending, self.early = ending, early

    def parts(self):
        parts, depth = lax.axis_size(TENSOR), self.line.shape[0]
        shapes = [(parts, depth, 2, 2) + self.line.shape[1:], self.ending.shape]
        outs = [jax.ShapeDtypeStruct(s, LOW) for s in shapes]
        scratch = sems(depth + EXTRA, depth + EXTRA, 2, 2) + [pltpu.SemaphoreType.DMA] * 2
        scratch.append(pltpu.VMEM(self.line.shape, LOW))
        scratch.append(trade_buffer(self.rows, self.ending.shape[0] - self.early))
        return [self.line, self.rows, self.ending], outs, [any_spec()] * 2, scratch

    def aliases(self, first_in, first_out):
        return {first_in + 2: first_out + 1}

    def table(self, ins, outs, scratch):
        sends, receives, hop, trade_hop, one_send, one_receive, buffer, rows_buffer = scratch
        feeds = Gather(None, outs[0], sends, receives, hop, ins[0], buffer)
        table = {
            (0, BEGIN): [call(greet, neighbours_of(feeds.depth)), call(feeds.start, 1)],
            (0, POST): [call(feeds.finish, 1), call(feeds.start, 2)],
            (1, 2): [call(feeds.finish, 2), call(feeds.start, 3)],
            (1, END): [call(feeds.finish, 3)],
        }
        if self.early < self.ending.shape[0]:
            trade = Trade(ins[1], outs[1], one_send, one_receive, trade_hop, rows_buffer, self.early)
            table[0, POST].append(trade.start)
            table[1, END].append(trade.finish)
        return table


def split_whole(whole):
    kinds, parts, width, cols = whole.shape
    depth = lax.axis_size(DP) // 4
    return whole.reshape(kinds, parts, depth, 2, 2, width // (4 * depth), cols)


class ReduceTail:
    def __init__(self, whole, own, partial, base, one, three, four, sends, receives, local):
        self.whole, self.own, self.partial = whole, own, partial
        self.base, self.one, self.three, self.four = base, one, three, four
        self.sems = lambda k: (sends.at[k], receives.at[k])
        self.local = local

    def copies(self):
        z, x, core, y = spot()
        own, cuts = self.own, self.partial.shape[:2]
        away = self.whole.at[:, y, :, x, 1 - core]
        return [
            pltpu.make_async_copy(own.at[:, y, :, x], self.base, self.local),
            Burst(own.at[:, y, :, 1 - x], self.three, self.sems(0), at(z, 1 - x, core, y), cuts),
            Burst(own.at[:, 1 - y, :, x], self.four, self.sems(1), at(z, x, core, 1 - y), cuts),
            Burst(away, self.one, self.sems(2), at(z, x, 1 - core, y), cuts),
        ]

    def start(self):
        for copy in self.copies():
            copy.start()

    def finish(self):
        for copy in self.copies():
            copy.wait()
        for k in range(self.partial.shape[0]):
            for d in range(self.partial.shape[1]):
                sources = (self.base, self.one, self.three, self.four)
                total = functools.reduce(jnp.add, [s[k, d].astype(F32) for s in sources])
                self.partial[k, d] = total.astype(self.partial.dtype)


class Backward(Guest):
    def __init__(self, gain_row, number, whole, points, rows=None, partial=None, half=False, pending=None, late=False):
        self.gain_row, self.number, self.points, self.rows = gain_row, number, points, rows
        self.whole, self.partial, self.half, self.late = split_whole(whole), partial, half, late
        self.pending = pending and (split_whole(pending[0]), pending[1])
        self.outs = 1 + (rows is not None) + (partial is not None) + (pending is not None)
        self.ins = self.outs + (pending is not None)

    def parts(self):
        shape = self.whole.shape
        depth = shape[2]
        kept = shape[:4] + shape[5:] if self.half else (shape[0], depth, shape[5], shape[6])
        outs = [jax.ShapeDtypeStruct(kept, LOW)]
        specs = [whole_spec(outs[0].shape)]
        ins = [self.whole]
        scratch = reduce_shapes(self.whole)[1 if self.half else 0 :] + sems(EXTRA, EXTRA, 1)
        if self.rows is not None:
            count, rows, width = self.rows.shape
            ins.append(self.rows)
            outs.append(jax.ShapeDtypeStruct((count, rows // 2, width), self.rows.dtype))
            specs.append(any_spec())
            scratch += [pltpu.SemaphoreType.DMA] * 2
        line = None
        if self.partial is not None:
            ins.append(self.partial)
            line = self.partial.shape
        if self.pending is not None:
            ins += list(self.pending)
            kinds, _, depth, _, _, rows, cols = self.pending[0].shape
            line = (kinds, depth, rows, cols)
            scratch += [pltpu.VMEM(line, LOW)] * 5 + sems(3, 3, 1)
        if line is not None:
            outs.append(jax.ShapeDtypeStruct((line[0],) + line[2:], F32))
            specs.append(whole_spec(outs[-1].shape))
            scratch += along_z_shapes(line)
        return ins, outs, specs, scratch

    def table(self, ins, outs, scratch):
        kept = PIECES - self.half
        buffers, scratch = list(scratch[:kept]), scratch[kept:]
        if self.half:
            buffers.insert(0, outs[0])
        sends, receives, local = scratch[:3]
        scratch = scratch[3:]
        group = Reduce(ins[0], outs[0], *buffers, sends, receives, local.at[0])
        near = neighbours_of(group.depth)
        first, last = [call(group.start, 0)], []
        points = self.points
        if self.rows is not None:
            z, x, core, y = spot()
            half = outs[1].shape[1]
            away = ins[1].at[:, pl.ds(pl.multiple_of((1 - y) * half, half), half)]
            copy = send(away, outs[1], (scratch[0], scratch[1]), at(z, x, core, 1 - y))
            first.append(copy.start)
            last.append(copy.wait)
            scratch = scratch[2:]
        middle = []
        if self.pending is not None:
            partial, base, one, three, four, sends, receives, local = scratch[:8]
            scratch = scratch[8:]
            tail = ReduceTail(ins[-2], ins[-1], partial, base, one, three, four, sends, receives, local.at[0])
            first.insert(0, tail.start)
            middle.append(tail.finish)
        if self.partial is not None or self.pending is not None:
            if self.partial is not None:
                partial = ins[-1]
            mine, rest, sends, receives, local = scratch
            line = AlongZ(partial, outs[-1], mine, rest, sends, receives, local.at[0])
            (first if self.pending is None else middle).append(line.start)
            last.append(line.finish)
        if self.late:
            table = {(0, BEGIN): [call(announce, near)], (0, 0): [call(await_all, near)] + first}
        else:
            table = {(0, BEGIN): [call(greet, near)] + first}
        phases = 2 if self.half else 3
        for phase in range(phases):
            actions = table.setdefault(points[phase], [])
            if phase == 0:
                actions.extend(middle)
            actions.append(call(group.finish, phase))
            if phase + 1 < phases:
                actions.append(call(group.start, phase + 1))
        table[points[phases - 1]].extend(last)
        return table


def reduce_kernel(total, heads_each, *refs):
    whole, away, feed_partial, part_two, feed_two_grad = refs[:5]
    attn_one, feed_one, attn_two, feed_two = refs[5:9]
    out, feed_one_grad, arrived, stats = refs[9:13]
    refs = refs[13:]
    groups, lines = [], []
    place = 0
    for half in range(2):
        cols = refs[0].shape[-1]
        buffers, line_refs, refs = refs[:PIECES], refs[PIECES : PIECES + 6], refs[PIECES + 6 :]
        partial, mine, rest, sends, receives, local = line_refs
        part = columns(whole, place, place + cols)
        group_sems, refs = refs[:3], refs[3:]
        groups.append(Reduce(part, partial, *buffers, group_sems[0], group_sems[1], group_sems[2].at[0]))
        target = columns(out, place, place + cols)
        lines.append(AlongZ(partial, target, mine, rest, sends, receives, local.at[0]))
        place += cols
    mine, rest, sends, receives, local = refs[:5]
    feed_line = AlongZ(feed_partial, feed_one_grad, mine, rest, sends, receives, local.at[0])
    tiles, stat_sends, stat_receives, one_send, one_receive = refs[5:]
    parts = lax.axis_size(TENSOR)
    me = lax.axis_index(DP) * parts + lax.axis_index(TENSOR)
    others = [(me + k) % total for k in range(1, total)]
    z, x, core, y = spot()
    handed = send(away, arrived, (one_send, one_receive), at(z, x, core, 1 - y))
    greet([(other // parts, other % parts) for other in others])
    for group in groups:
        group.start(0)
    feed_line.start()
    for phase in range(3):
        for group, line in zip(groups, lines):
            group.finish(phase)
            if phase < 2:
                group.start(phase + 1)
            else:
                line.start()
    handed.start()
    feed_line.finish()
    for line in lines:
        line.finish()
    outs = (feed_two_grad, part_two, feed_one_grad, out)
    attn_two_grad, attn_one_grad = part_two, out
    qkv = 3 * (attn_two.shape[1] // 4)
    small = attn_one[:, 4 * (attn_two.shape[1] // 4) :].astype(F32)
    gate_grad = attn_two_grad[0, :, attn_two.shape[1] :]
    units = feed_one.shape[1] // 2

    def row_sums(values):
        return jnp.sum(values, axis=1, keepdims=True)

    lane = lax.broadcasted_iota(jnp.int32, small.shape, 1)
    gate_only = jnp.where(lane < heads_each, small, 0.0)
    sums = [
        row_sums(attn_one[:, :qkv].astype(F32) * attn_one_grad[0, :, :qkv]),
        row_sums(feed_one[:, :units].astype(F32) * feed_one_grad[0]),
        row_sums(attn_two[:, :qkv].astype(F32) * attn_two_grad[0, :, :qkv])
        + row_sums(gate_only * gate_grad),
        row_sums(feed_two[:, :units].astype(F32) * feed_two_grad[0]),
    ]
    squares = functools.reduce(
        jnp.add, [row_sums(out[k] * out[k]) for out in outs for k in range(out.shape[0])]
    )
    tile = jnp.where(lane == 4, squares, 0.0)
    for row in range(4):
        gain = row_sums(jnp.where(lane == heads_each + row, small, 0.0))
        tile = tile + jnp.where(lane == row, sums[row] / gain, 0.0)
    blank = jnp.zeros((WIDE - tile.shape[0], WIDE), F32)
    tiles[me] = jnp.concatenate([tile, blank], axis=0).T[:8]
    copies = [
        send(tiles.at[me], tiles.at[me], (stat_sends.at[k], stat_receives.at[k]), (o // parts, o % parts))
        for k, o in enumerate(others)
    ]
    for copy in copies:
        copy.start()
    for copy in copies:
        copy.wait()
    row = lax.broadcasted_iota(jnp.int32, (8, WIDE), 0)
    found = jnp.zeros((8, WIDE), F32)
    for device in range(0, total, parts):
        pair = functools.reduce(jnp.add, [tiles[device + part] for part in range(parts)])
        found = found + jnp.where(row < 4, pair * pair, jnp.where(row == 4, pair, 0.0))
    start = me - me % parts
    stats[0] = functools.reduce(jnp.add, [tiles[start + part] for part in range(parts)])
    stats[1] = jnp.broadcast_to(jnp.sum(found, keepdims=True), found.shape)
    handed.wait()


def finish_reduce(whole, away, feed_partial, grads, shards, heads_each, number):
    depth = lax.axis_size(DP) // 4
    total = lax.axis_size(TENSOR) * lax.axis_size(DP)
    whole = split_whole(whole)
    kinds, _, _, _, _, rows, cols = whole.shape
    scratch = []
    for part in halves(cols):
        piece = jax.ShapeDtypeStruct(whole.shape[:-1] + (part.size,), LOW)
        line = (kinds, depth, rows, part.size)
        scratch += reduce_shapes(piece) + [pltpu.VMEM(line, LOW)] + along_z_shapes(line)
        scratch += sems(EXTRA, EXTRA, 1)
    scratch += along_z_shapes(feed_partial.shape)
    scratch += [pltpu.VMEM((total, 8, WIDE), F32)] + sems(total - 1, total - 1)
    vmem = pl.BlockSpec(memory_space=pltpu.VMEM)
    return pl.pallas_call(
        functools.partial(reduce_kernel, total, heads_each),
        out_shape=[
            jax.ShapeDtypeStruct((kinds, rows, cols), F32),
            jax.ShapeDtypeStruct((feed_partial.shape[0], rows, feed_partial.shape[3]), F32),
            jax.ShapeDtypeStruct(away.shape, away.dtype),
            jax.ShapeDtypeStruct((2, 8, WIDE), F32),
        ],
        in_specs=[any_spec()] * 3 + [vmem] * 6,
        out_specs=[vmem, vmem, any_spec(), vmem],
        scratch_shapes=scratch + [pltpu.SemaphoreType.DMA] * 2,
        compiler_params=pltpu.CompilerParams(
            collective_id=number, has_side_effects=True, vmem_limit_bytes=VMEM_BYTES
        ),
    )(whole, away, feed_partial, *grads, *shards)


def update_kernel(heads_each, *refs):
    grad, arrived_grad, result, arrived_rows = refs[:4]
    attn_one, attn_two, feed_one, feed_two, stats = refs[4:9]
    states = [refs[9 + 4 * g : 13 + 4 * g] for g in range(6)]
    refs = refs[33:]
    rows_out, grad_out, norm_out = refs[:3]
    outs = [refs[3 + 4 * g : 7 + 4 * g] for g in range(6)]
    feed_gains = refs[27]
    y = lax.axis_index(TENSOR)
    share, half = arrived_rows.shape[0], arrived_rows.shape[1]
    mine = pl.ds(pl.multiple_of(y * half, half), half)
    grad_out[pl.ds(y * share, share)] = grad[:, mine]
    grad_out[pl.ds((1 - y) * share, share)] = arrived_grad[...].astype(F32)
    rows_out[pl.ds(y * share, share)] = result[:, mine]
    rows_out[pl.ds((1 - y) * share, share)] = arrived_rows[...]
    norm = jnp.sqrt(stats[1, :1, :])
    norm_out[...] = norm
    factor = (CLIP / jnp.maximum(norm, CLIP))[:, :1]

    def apply(group, spot_at, piece):
        state = [ref[spot_at] for ref in states[group]]
        new = adamw(*state, piece * factor, STEP_RATES[group], STEP_DECAYS[group])
        for ref, value in zip(outs[group], new):
            ref[spot_at] = value

    cols = states[0][0].shape[3]
    for depth, part in enumerate((attn_one, attn_two)):
        for kind in range(3):
            apply(0, (depth, kind), part[0, :, kind * cols : (kind + 1) * cols])
        apply(1, (depth,), part[0, :, 3 * cols : 4 * cols])
    for depth, part in enumerate((feed_one, feed_two)):
        apply(2, (depth,), part[0])
        apply(3, (depth,), part[1])
    gains = stats[0][: states[4][0].shape[0], : states[4][0].shape[1]]
    apply(4, (slice(None),), gains)
    apply(5, (slice(None),), attn_two[0, :, 4 * cols :].T[:heads_each])
    feed_gains[0:1] = gains[1:2] * factor
    feed_gains[1:2] = gains[3:4] * factor


def update(moves, grads, stats, states, outs, heads_each):
    vmem = pl.BlockSpec(memory_space=pltpu.VMEM)
    flat_states = [a for group in states for a in group]
    ins = list(moves) + list(grads) + [stats] + flat_states
    shapes = list(outs[:3]) + [jax.ShapeDtypeStruct(a.shape, F32) for a in flat_states] + [outs[3]]
    return pl.pallas_call(
        functools.partial(update_kernel, heads_each),
        out_shape=shapes,
        in_specs=[vmem] * len(ins),
        out_specs=[vmem] * len(shapes),
        compiler_params=pltpu.CompilerParams(vmem_limit_bytes=VMEM_BYTES),
    )(*ins)


def tables(length):
    half_dim = HEAD_DIM // 2
    places = np.arange(length).astype(np.float32)
    frequency = np.exp(
        np.float32(-math.log(10000.0)) * np.arange(half_dim).astype(np.float32) / np.float32(half_dim)
    )
    angles = (frequency[:, None] * places[None, :]).astype(np.float64)
    return jnp.asarray(np.cos(angles), F32), jnp.asarray(np.sin(angles), F32)


def whole_body(
    activations,
    memory_one,
    memory_two,
    neighbours,
    resets,
    cotangent,
    qkv_weight,
    qkv_first,
    qkv_second,
    qkv_ema,
    out_weight,
    out_first,
    out_second,
    out_ema,
    up_weight,
    up_first,
    up_second,
    up_ema,
    down_weight,
    down_first,
    down_second,
    down_ema,
    gain_rows,
    gain_first,
    gain_second,
    gain_ema,
    gate_weight,
    gate_first,
    gate_second,
    gate_ema,
):
    parts = lax.axis_size(TENSOR)
    share = activations.shape[0] // parts
    width = activations.shape[2]
    heads_each = gate_weight.shape[1]

    def flip(group):
        return [a.swapaxes(-1, -2) for a in group]

    states = [
        [qkv_weight, qkv_first, qkv_second, qkv_ema],
        flip([out_weight, out_first, out_second, out_ema]),
        [up_weight, up_first, up_second, up_ema],
        flip([down_weight, down_first, down_second, down_ema]),
        [gain_rows, gain_first, gain_second, gain_ema],
        flip([gate_weight, gate_first, gate_second, gate_ema]),
    ]
    near = neighbours.transpose(0, 2, 1)
    started = start_up(*[group[0] for group in states], activations, memory_one, memory_two, near, 0)
    attn_shard, attn_two_shard, feed_shard, feed_two_shard, slab_one, line, start = started[:7]
    memories, near = started[7:9], started[9]
    slab_one = flat(slab_one)
    cosine, sine = tables(MEM + SEG)
    shape = (share * SEG, width)
    back = (share, SEG, width)

    guest = FirstForward(heads_each, 1, line, attn_two_shard, feed_two_shard)
    one = attend(start, memories[0], resets, slab_one, slab_one, cosine, sine, None, guest)
    after_one = one[0].reshape(shape)
    feed_one = flat(one[6])
    steps = 2 * parts * up_weight.shape[2] // (2 * CHUNK)
    early = (share + 1) // 2
    guest = MiddleForward(heads_each + 1, 2, one[7], cotangent, early, steps)
    before_two, slab_two, ending = feed(after_one, feed_one, slab_one, guest)
    slab_two = flat(slab_two)
    before_rows = before_two.reshape(back)
    guest = SecondForward(heads_each + 2, 3, one[8], cotangent, ending, early)
    two = attend(before_rows, memories[1], resets, slab_two, slab_one, cosine, sine, near, guest)
    after_two = two[0].reshape(shape)
    feed_two, ending = flat(two[9]), two[10].reshape(shape)
    guest = Guest(heads_each + 3)
    result, grad, feed_grad_two = feed_back(after_two, feed_two, slab_one, ending, True, guest)
    result = result.reshape(back)
    points = ((0, 2), (1, 0), (1, END))
    guest = Backward(heads_each + 2, 4, feed_grad_two, points, result, late=True)
    grad, attn_grad_two, partial, arrived_rows = attend_back(
        before_rows,
        memories[1],
        resets,
        slab_two,
        slab_one,
        cosine,
        sine,
        grad.reshape(back),
        two[1:],
        near,
        guest,
    )
    points = ((1, BEGIN), (steps - 1, END))
    guest = Backward(heads_each + 1, 5, attn_grad_two[None], points, None, partial, half=True)
    grad, feed_grad_one, own, feed_two_part = feed_back(
        after_one, feed_one, slab_one, grad.reshape(shape), False, guest
    )
    points = ((0, 2), (1, 0), (1, END))
    guest = Backward(heads_each, 6, feed_grad_one, points, pending=(attn_grad_two[None], own))
    grad, attn_grad_one, away, partial, attn_two_part = attend_back(
        start, memories[0], resets, slab_one, slab_one, cosine, sine, grad.reshape(back), one[1:], None, guest
    )
    attn_one_part, feed_one_part, arrived_grad, stats = finish_reduce(
        attn_grad_one[None],
        away,
        partial,
        [attn_two_part, feed_two_part],
        [attn_shard, feed_shard, attn_two_shard, feed_two_shard],
        heads_each,
        7,
    )
    outs = (
        jax.ShapeDtypeStruct(activations.shape, LOW),
        jax.ShapeDtypeStruct(activations.shape, F32),
        jax.ShapeDtypeStruct((1, WIDE), F32),
        jax.ShapeDtypeStruct((2, gain_rows.shape[1]), F32),
    )
    done = update(
        (grad, arrived_grad, result, arrived_rows),
        (attn_one_part, attn_two_part, feed_one_part, feed_two_part),
        stats,
        states,
        outs,
        heads_each,
    )
    result_rows, input_grad, norm = done[:3]
    groups = [list(done[3 + 4 * group : 7 + 4 * group]) for group in range(6)]
    for group in (1, 3, 5):
        groups[group] = flip(groups[group])
    updated = [a for group in groups for a in group]
    return (result_rows, input_grad, norm[0, 0], *updated, done[27])


def solution(mesh):
    in_specs = (
        P(DP, TENSOR, None),
        P(DP, None, None),
        P(DP, None, None),
        P(DP, None, None),
        P(DP),
        P(DP, TENSOR, None),
        P(None, None, DP, TENSOR),
        P(None, None, DP, TENSOR),
        P(None, None, DP, TENSOR),
        P(None, None, DP, TENSOR),
        P(None, TENSOR, DP),
        P(None, TENSOR, DP),
        P(None, TENSOR, DP),
        P(None, TENSOR, DP),
        P(None, DP, TENSOR),
        P(None, DP, TENSOR),
        P(None, DP, TENSOR),
        P(None, DP, TENSOR),
        P(None, TENSOR, DP),
        P(None, TENSOR, DP),
        P(None, TENSOR, DP),
        P(None, TENSOR, DP),
        P(None, DP),
        P(None, DP),
        P(None, DP),
        P(None, DP),
        P(DP, TENSOR),
        P(DP, TENSOR),
        P(DP, TENSOR),
        P(DP, TENSOR),
    )
    out_specs = (
        P(DP, TENSOR, None),
        P(DP, TENSOR, None),
        P(),
        P(None, None, DP, TENSOR),
        P(None, None, DP, TENSOR),
        P(None, None, DP, TENSOR),
        P(None, None, DP, TENSOR),
        P(None, TENSOR, DP),
        P(None, TENSOR, DP),
        P(None, TENSOR, DP),
        P(None, TENSOR, DP),
        P(None, DP, TENSOR),
        P(None, DP, TENSOR),
        P(None, DP, TENSOR),
        P(None, DP, TENSOR),
        P(None, TENSOR, DP),
        P(None, TENSOR, DP),
        P(None, TENSOR, DP),
        P(None, TENSOR, DP),
        P(None, DP),
        P(None, DP),
        P(None, DP),
        P(None, DP),
        P(DP, TENSOR),
        P(DP, TENSOR),
        P(DP, TENSOR),
        P(DP, TENSOR),
        P(None, DP),
    )
    parts = mesh.shape[TENSOR]
    regular = parts == 2 and mesh.shape[DP] % 4 == 0

    def choose(activations, *rest):
        fits = regular and activations.shape[0] // mesh.shape[DP] % parts == 0
        route = whole_body if fits else body
        spread = jax.shard_map(
            route, mesh=mesh, in_specs=in_specs, out_specs=out_specs, check_vma=False
        )
        return spread(activations, *rest)

    return choose
```

```python
import functools
import itertools
import math

import jax
import jax.numpy as jnp
import numpy as np
from jax import lax
from jax.experimental import pallas as pl
from jax.experimental.pallas import tpu as pltpu
from jax.sharding import PartitionSpec as P

HEAD_DIM = 64
SEG = 512
MEM = 512
STEP = 4
DP = "dp"
TENSOR = "tensor"


CLIP = 1.0
BETA_ONE = 0.9
BETA_TWO = 0.999
EPS_ADAM = 1e-08
STEP_RATES = (0.05, 0.5, 0.05, 0.03, 0.5, 0.05)
STEP_DECAYS = (0.1, 0.1, 0.1, 0.1, 0.0, 0.1)
HIGH = lax.Precision.HIGHEST
RULE_0 = "hij,ihd->jhd"
RULE_1 = "hij,jhd->ihd"
RULE_2 = "ihd,jhd->hij"
RULE_4 = "sic,sie->ce"
RULE_9 = "sie,ce->sic"
RULE_13 = "sihd,sikhd->sihk"
RULE_14 = "sihk,sihd->sikhd"
RULE_15 = "sihk,sikhd->sihd"
RULE_18 = "sjc,sje->ce"
RULE_19 = "sje,ce->sjc"
KEEP_ACTIVE = "active"
KEEP_ATTENDED = "attended"
KEEP_DOWN_WHOLE = "down_whole"
KEEP_FETCHED = "fetched"
KEEP_GATE_OPEN = "gate_open"
KEEP_HIDDEN = "hidden"
KEEP_KEY_ROT = "key_rot"
KEEP_LOG_TOTAL = "log_total"
KEEP_MIXTURE_LOW = "mixture_low"
KEEP_NEAR_KEYS = "near_keys"
KEEP_NEAR_VALUES = "near_values"
KEEP_NEAR_WEIGHTS = "near_weights"
KEEP_NORMAL_MEM = "normal_mem"
KEEP_NORMAL_ROWS = "normal_rows"
KEEP_PRE_ACTIVE = "pre_active"
KEEP_QUERY_PLAIN = "query_plain"
KEEP_QUERY_ROT = "query_rot"
KEEP_UP_WHOLE = "up_whole"
KEEP_VALUE_ALL = "value_all"


def normed(values, gain_row):
    spread = lax.rsqrt(jnp.mean(values * values, axis=-1, keepdims=True) + 1e-06)
    return values * spread * gain_row


def turning(length, offset):
    half_dim = HEAD_DIM // 2
    places = (jnp.arange(length) + offset).astype(jnp.float32)
    frequency = jnp.exp(-math.log(10000.0) * jnp.arange(half_dim).astype(jnp.float32) / half_dim)
    angles = places[:, None] * frequency[None, :]
    return (jnp.cos(angles), jnp.sin(angles))


def rotate(values, cosine, sine_table):
    half_dim = values.shape[-1] // 2
    first_half = values[..., :half_dim]
    second_half = values[..., half_dim:]
    cosine_b = cosine[:, None, :]
    sine_b = sine_table[:, None, :]
    return jnp.concatenate(
        [
            first_half * cosine_b - second_half * sine_b,
            first_half * sine_b + second_half * cosine_b,
        ],
        axis=-1,
    )


def to_heads(values):
    return values.reshape(values.shape[:-1] + (values.shape[-1] // HEAD_DIM, HEAD_DIM))


def flat_low(values):
    return values.reshape(values.shape[0], values.shape[1], -1).astype(jnp.bfloat16)


def allowed_keys(reset_flag):
    row_place = jnp.arange(SEG)[:, None]
    key_place = jnp.arange(MEM + SEG)[None, :]
    return jnp.where(key_place < MEM, reset_flag == 0, key_place - MEM <= row_place)


def masked_scores(query_rot, key_rot, reset_flag):
    scores = jnp.einsum(
        RULE_2, query_rot, key_rot, preferred_element_type=jnp.float32
    ) * HEAD_DIM ** (-0.5)
    return jnp.where(allowed_keys(reset_flag), scores, -1e30)


def attend_forward(query_rot, key_rot, value_all, reset_flag):
    scores = masked_scores(query_rot, key_rot, reset_flag)
    row_max = jnp.max(scores, axis=-1, keepdims=True)
    raised = jnp.exp(scores - row_max)
    summed = jnp.sum(raised, axis=-1, keepdims=True)
    weights_soft = (raised / summed).astype(jnp.bfloat16)
    attended = jnp.einsum(
        RULE_1, weights_soft, value_all, preferred_element_type=jnp.float32
    )
    return (attended, row_max[..., 0] + jnp.log(summed[..., 0]))


def attend_backward(query_rot, key_rot, value_all, reset_flag, log_total, grad_attended):
    scores = masked_scores(query_rot, key_rot, reset_flag)
    probs_exact = jnp.exp(scores - log_total[..., None])
    grad_value = jnp.einsum(
        RULE_0,
        probs_exact.astype(jnp.bfloat16),
        grad_attended,
        preferred_element_type=jnp.float32,
    )
    grad_probs = jnp.einsum(
        RULE_2, grad_attended, value_all, preferred_element_type=jnp.float32
    )
    weighted = jnp.sum(probs_exact * grad_probs, axis=-1, keepdims=True)
    grad_scores = (probs_exact * (grad_probs - weighted)).astype(jnp.bfloat16)
    grad_query = jnp.einsum(
        RULE_1, grad_scores, key_rot, preferred_element_type=jnp.float32
    ) * HEAD_DIM ** (-0.5)
    grad_key = jnp.einsum(
        RULE_0, grad_scores, query_rot, preferred_element_type=jnp.float32
    ) * HEAD_DIM ** (-0.5)
    return (grad_query, grad_key, grad_value)


def selection(neighbours, kind):
    return (neighbours[..., None] == jnp.arange(MEM)[None, None, None, :]).astype(kind)


def pick_rows(table, neighbours):
    flat_table = table.reshape(table.shape[0], table.shape[1], -1)
    chosen = jnp.einsum(
        "sikm,smc->sikc",
        selection(neighbours, table.dtype),
        flat_table,
        preferred_element_type=jnp.float32,
    )
    return chosen.reshape(chosen.shape[:3] + table.shape[2:])


def place_rows(values, neighbours):
    flat_values = values.reshape(values.shape[:3] + (-1,))
    placed = jnp.einsum(
        "sikm,sikc->smc", selection(neighbours, jnp.float32), flat_values, precision=HIGH
    )
    return placed.reshape((values.shape[0], MEM) + values.shape[3:])


def collect_rows(values):
    return lax.all_gather(values, TENSOR, axis=1, tiled=True)


def spread_rows(partial_term):
    return lax.psum_scatter(partial_term, TENSOR, scatter_dimension=1, tiled=True)


def collect_grads(values):
    return lax.all_gather(values, TENSOR, axis=1, tiled=True)


def spread_grads(partial_term):
    return lax.psum_scatter(partial_term, TENSOR, scatter_dimension=1, tiled=True)


def attention_forward(
    hidden, memory, neighbours, resets, qkv_layer, out_layer, gain_row, gate_cols, retrieve
):
    seg_count = hidden.shape[0]
    normal_rows = collect_rows(normed(hidden, gain_row).astype(jnp.bfloat16))
    normal_mem = normed(memory.astype(jnp.float32), gain_row).astype(jnp.bfloat16)
    query_raw = jnp.dot(normal_rows, qkv_layer[0], preferred_element_type=jnp.float32)
    key_raw = jnp.dot(normal_rows, qkv_layer[1], preferred_element_type=jnp.float32)
    key_mem = jnp.dot(normal_mem, qkv_layer[1], preferred_element_type=jnp.float32)
    value_rows = jnp.dot(normal_rows, qkv_layer[2], preferred_element_type=jnp.float32).astype(
        jnp.bfloat16
    )
    value_mem = jnp.dot(normal_mem, qkv_layer[2], preferred_element_type=jnp.float32).astype(
        jnp.bfloat16
    )
    cosine_rows, sine_rows = turning(SEG, MEM)
    cosine_mem, sine_mem = turning(MEM, 0)
    query_rot = rotate(to_heads(query_raw), cosine_rows, sine_rows).astype(jnp.bfloat16)
    key_rot = jnp.concatenate(
        [
            rotate(to_heads(key_mem), cosine_mem, sine_mem),
            rotate(to_heads(key_raw), cosine_rows, sine_rows),
        ],
        axis=1,
    ).astype(jnp.bfloat16)
    value_all = jnp.concatenate([to_heads(value_mem), to_heads(value_rows)], axis=1)
    attended, log_total = lax.map(
        lambda items: attend_forward(*items), (query_rot, key_rot, value_all, resets)
    )
    saved = {
        KEEP_HIDDEN: hidden,
        KEEP_NORMAL_ROWS: normal_rows,
        KEEP_NORMAL_MEM: normal_mem,
        KEEP_QUERY_ROT: query_rot,
        KEEP_KEY_ROT: key_rot,
        KEEP_VALUE_ALL: value_all,
        KEEP_LOG_TOTAL: log_total,
        KEEP_ATTENDED: attended,
    }
    if retrieve:
        query_plain = to_heads(query_raw).astype(jnp.bfloat16)
        near_keys = pick_rows(to_heads(key_mem).astype(jnp.bfloat16), neighbours).astype(
            jnp.bfloat16
        )
        near_values = pick_rows(to_heads(value_mem), neighbours)
        logits = jnp.einsum(
            RULE_13, query_plain, near_keys, preferred_element_type=jnp.float32
        ) * HEAD_DIM ** (-0.5)
        near_weights = jax.nn.softmax(logits, axis=-1)
        fetched = jnp.einsum(RULE_15, near_weights, near_values, precision=HIGH)
        gate_open = jax.nn.sigmoid(
            jnp.dot(normal_rows, gate_cols, preferred_element_type=jnp.float32)
        )[..., None]
        mixture = gate_open * attended + (1.0 - gate_open) * fetched
        saved[KEEP_QUERY_PLAIN] = query_plain
        saved[KEEP_NEAR_KEYS] = near_keys
        saved[KEEP_NEAR_VALUES] = near_values
        saved[KEEP_NEAR_WEIGHTS] = near_weights
        saved[KEEP_FETCHED] = fetched
        saved[KEEP_GATE_OPEN] = gate_open
    else:
        mixture = attended
    mixture_low = mixture.astype(jnp.bfloat16).reshape(seg_count, SEG, -1)
    saved[KEEP_MIXTURE_LOW] = mixture_low
    hidden_new = hidden + spread_rows(
        jnp.dot(mixture_low, out_layer, preferred_element_type=jnp.float32)
    )
    return (hidden_new, saved)


def attention_backward(
    grad_hidden,
    saved,
    memory,
    neighbours,
    resets,
    qkv_layer,
    out_layer,
    gain_row,
    gate_cols,
    retrieve,
):
    normal_rows = saved[KEEP_NORMAL_ROWS]
    normal_mem = saved[KEEP_NORMAL_MEM]
    grad_full = collect_grads(grad_hidden.astype(jnp.bfloat16))
    grad_out_layer = jnp.einsum(
        "sic,sid->cd", saved[KEEP_MIXTURE_LOW], grad_full, preferred_element_type=jnp.float32
    )
    grad_mixture = to_heads(
        jnp.einsum("sid,cd->sic", grad_full, out_layer, preferred_element_type=jnp.float32).astype(
            jnp.bfloat16
        )
    )
    extra_query = 0.0
    extra_key = 0.0
    extra_value = 0.0
    grad_gate_layer = None
    if retrieve:
        gate_open = saved[KEEP_GATE_OPEN]
        near_weights = saved[KEEP_NEAR_WEIGHTS]
        grad_mix_f = grad_mixture.astype(jnp.float32)
        grad_attended = (gate_open * grad_mix_f).astype(jnp.bfloat16)
        grad_fetched = (1.0 - gate_open) * grad_mix_f
        gate_value = gate_open[..., 0]
        grad_gate_logit = (
            jnp.sum(grad_mix_f * (saved[KEEP_ATTENDED] - saved[KEEP_FETCHED]), axis=-1)
            * gate_value
            * (1.0 - gate_value)
        ).astype(jnp.bfloat16)
        grad_near_weights = jnp.einsum(
            RULE_13, grad_fetched, saved[KEEP_NEAR_VALUES], precision=HIGH
        )
        grad_near_values = jnp.einsum(
            RULE_14, near_weights, grad_fetched, precision=HIGH
        )
        weighted = jnp.sum(near_weights * grad_near_weights, axis=-1, keepdims=True)
        grad_logits = near_weights * (grad_near_weights - weighted) * HEAD_DIM ** (-0.5)
        extra_query = jnp.einsum(
            RULE_15, grad_logits, saved[KEEP_NEAR_KEYS].astype(jnp.float32), precision=HIGH
        )
        grad_near_keys = jnp.einsum(
            RULE_14,
            grad_logits,
            saved[KEEP_QUERY_PLAIN].astype(jnp.float32),
            precision=HIGH,
        )
        extra_key = place_rows(grad_near_keys, neighbours)
        extra_value = place_rows(grad_near_values, neighbours)
        grad_gate_layer = jnp.einsum(
            "sic,sih->ch", normal_rows, grad_gate_logit, preferred_element_type=jnp.float32
        )
    else:
        grad_attended = grad_mixture
    grad_query_rot, grad_key_rot, grad_value_all = lax.map(
        lambda items: attend_backward(*items),
        (
            saved[KEEP_QUERY_ROT],
            saved[KEEP_KEY_ROT],
            saved[KEEP_VALUE_ALL],
            resets,
            saved[KEEP_LOG_TOTAL],
            grad_attended,
        ),
    )
    cosine_rows, sine_rows = turning(SEG, MEM)
    cosine_mem, sine_mem = turning(MEM, 0)
    grad_query = flat_low(rotate(grad_query_rot, cosine_rows, -sine_rows) + extra_query)
    grad_key_mem = flat_low(rotate(grad_key_rot[:, :MEM], cosine_mem, -sine_mem) + extra_key)
    grad_key_rows = flat_low(rotate(grad_key_rot[:, MEM:], cosine_rows, -sine_rows))
    grad_value_mem = flat_low(grad_value_all[:, :MEM] + extra_value)
    grad_value_rows = flat_low(grad_value_all[:, MEM:])
    grad_qkv_layer = jnp.stack(
        [
            jnp.einsum(RULE_4, normal_rows, grad_query, preferred_element_type=jnp.float32),
            jnp.einsum(
                RULE_4, normal_rows, grad_key_rows, preferred_element_type=jnp.float32
            )
            + jnp.einsum(
                RULE_18, normal_mem, grad_key_mem, preferred_element_type=jnp.float32
            ),
            jnp.einsum(
                RULE_4, normal_rows, grad_value_rows, preferred_element_type=jnp.float32
            )
            + jnp.einsum(
                RULE_18, normal_mem, grad_value_mem, preferred_element_type=jnp.float32
            ),
        ]
    )
    rows_term = (
        jnp.einsum(RULE_9, grad_query, qkv_layer[0], preferred_element_type=jnp.float32)
        + jnp.einsum(RULE_9, grad_key_rows, qkv_layer[1], preferred_element_type=jnp.float32)
        + jnp.einsum(
            RULE_9, grad_value_rows, qkv_layer[2], preferred_element_type=jnp.float32
        )
    )
    if retrieve:
        rows_term = rows_term + jnp.einsum(
            "sih,ch->sic", grad_gate_logit, gate_cols, preferred_element_type=jnp.float32
        )
    grad_normal = spread_grads(rows_term)
    grad_normal_mem = jnp.einsum(
        RULE_19, grad_key_mem, qkv_layer[1], preferred_element_type=jnp.float32
    ) + jnp.einsum(RULE_19, grad_value_mem, qkv_layer[2], preferred_element_type=jnp.float32)
    grad_gain_mem = jnp.sum(grad_normal_mem * normed(memory.astype(jnp.float32), 1.0), axis=(0, 1))
    _, pullback = jax.vjp(normed, saved[KEEP_HIDDEN], gain_row)
    grad_inputs, grad_gain_part = pullback(grad_normal)
    return (
        grad_hidden + grad_inputs,
        grad_qkv_layer,
        grad_out_layer,
        grad_gain_part + grad_gain_mem,
        grad_gate_layer,
    )


def feed_forward(hidden, up_layer, down_layer, gain_row):
    up_whole, down_whole = (up_layer, down_layer)
    normal_rows = collect_rows(normed(hidden, gain_row).astype(jnp.bfloat16))
    pre_active = jnp.dot(normal_rows, up_whole, preferred_element_type=jnp.float32)
    active = jax.nn.gelu(pre_active).astype(jnp.bfloat16)
    branch_out = jnp.dot(active, down_whole, preferred_element_type=jnp.float32)
    hidden_new = hidden + spread_rows(branch_out)
    saved = {
        KEEP_HIDDEN: hidden,
        KEEP_NORMAL_ROWS: normal_rows,
        KEEP_PRE_ACTIVE: pre_active,
        KEEP_ACTIVE: active,
        KEEP_UP_WHOLE: up_whole,
        KEEP_DOWN_WHOLE: down_whole,
    }
    return (hidden_new, saved)


def feed_backward(grad_hidden, saved, gain_row):
    grad_full = collect_grads(grad_hidden.astype(jnp.bfloat16))
    grad_down = jnp.einsum(
        "sif,sid->fd", saved[KEEP_ACTIVE], grad_full, preferred_element_type=jnp.float32
    )
    grad_active = jnp.einsum(
        "sid,fd->sif", grad_full, saved[KEEP_DOWN_WHOLE], preferred_element_type=jnp.float32
    )
    _, gelu_pull = jax.vjp(jax.nn.gelu, saved[KEEP_PRE_ACTIVE])
    grad_pre = gelu_pull(grad_active)[0].astype(jnp.bfloat16)
    grad_up = jnp.einsum(
        "sic,sif->cf", saved[KEEP_NORMAL_ROWS], grad_pre, preferred_element_type=jnp.float32
    )
    rows_term = jnp.einsum(
        "sif,cf->sic", grad_pre, saved[KEEP_UP_WHOLE], preferred_element_type=jnp.float32
    )
    grad_normal = spread_grads(rows_term)
    _, pullback = jax.vjp(normed, saved[KEEP_HIDDEN], gain_row)
    grad_inputs, grad_gain_part = pullback(grad_normal)
    return (grad_hidden + grad_inputs, grad_up, grad_down, grad_gain_part)


def adamw(weight, first, second, average, grad, rate, decay):
    ema_keep = min(0.999, (1.0 + STEP) / (10.0 + STEP))
    first_new = BETA_ONE * first + (1.0 - BETA_ONE) * grad
    second_new = BETA_TWO * second + (1.0 - BETA_TWO) * grad * grad
    first_hat = first_new / (1.0 - BETA_ONE**STEP)
    second_hat = second_new / (1.0 - BETA_TWO**STEP)
    weight_new = weight - rate * (first_hat / (jnp.sqrt(second_hat) + EPS_ADAM) + decay * weight)
    average_new = ema_keep * average + (1.0 - ema_keep) * weight_new
    return (first_new, second_new, weight_new, average_new)


def body(
    activations,
    memory_one,
    memory_two,
    neighbours,
    resets,
    cotangent,
    qkv_weight,
    qkv_first,
    qkv_second,
    qkv_ema,
    out_weight,
    out_first,
    out_second,
    out_ema,
    up_weight,
    up_first,
    up_second,
    up_ema,
    down_weight,
    down_first,
    down_second,
    down_ema,
    gain_rows,
    gain_first,
    gain_second,
    gain_ema,
    gate_weight,
    gate_first,
    gate_second,
    gate_ema,
):
    qkv_full, out_full, up_full, down_full, gains_full, gate_full = (
        lax.all_gather(qkv_weight.astype(jnp.bfloat16), DP, axis=2, tiled=True),
        lax.all_gather(out_weight.astype(jnp.bfloat16), DP, axis=2, tiled=True),
        lax.all_gather(up_weight.astype(jnp.bfloat16), DP, axis=1, tiled=True),
        lax.all_gather(down_weight.astype(jnp.bfloat16), DP, axis=2, tiled=True),
        lax.all_gather(gain_rows.astype(jnp.bfloat16), DP, axis=1, tiled=True),
        lax.all_gather(gate_weight.astype(jnp.bfloat16), DP, axis=0, tiled=True),
    )
    gain_values = gains_full.astype(jnp.float32)
    memories = (memory_one, memory_two)
    hidden = activations.astype(jnp.float32)
    saved_attention = []
    saved_feed = []
    for depth in range(2):
        hidden, saved = attention_forward(
            hidden,
            memories[depth],
            neighbours,
            resets,
            qkv_full[depth],
            out_full[depth],
            gain_values[2 * depth],
            gate_full,
            depth == 1,
        )
        saved_attention.append(saved)
        hidden, saved = feed_forward(
            hidden, up_full[depth], down_full[depth], gain_values[2 * depth + 1]
        )
        saved_feed.append(saved)
    result_rows = hidden.astype(jnp.bfloat16)
    grad_hidden = cotangent.astype(jnp.float32)
    grad_qkv_list = [None, None]
    grad_out_list = [None, None]
    grad_up_list = [None, None]
    grad_down_list = [None, None]
    grad_gain_list = [None, None, None, None]
    grad_gate = None
    for depth in (1, 0):
        grad_hidden, grad_up_list[depth], grad_down_list[depth], grad_gain_list[2 * depth + 1] = (
            feed_backward(grad_hidden, saved_feed[depth], gain_values[2 * depth + 1])
        )
        (
            grad_hidden,
            grad_qkv_list[depth],
            grad_out_list[depth],
            grad_gain_list[2 * depth],
            gate_part,
        ) = attention_backward(
            grad_hidden,
            saved_attention[depth],
            memories[depth],
            neighbours,
            resets,
            qkv_full[depth],
            out_full[depth],
            gain_values[2 * depth],
            gate_full,
            depth == 1,
        )
        if depth == 1:
            grad_gate = gate_part
    grad_qkv = jnp.stack(grad_qkv_list)
    grad_out = jnp.stack(grad_out_list)
    grad_up = jnp.stack(grad_up_list)
    grad_down = jnp.stack(grad_down_list)
    grad_gains = jnp.stack(grad_gain_list)
    grad_qkv, grad_out, grad_up, grad_down, gain_part, grad_gate = (
        lax.psum_scatter(grad_qkv, DP, scatter_dimension=2, tiled=True),
        lax.psum_scatter(grad_out, DP, scatter_dimension=2, tiled=True),
        lax.psum_scatter(grad_up, DP, scatter_dimension=1, tiled=True),
        lax.psum_scatter(grad_down, DP, scatter_dimension=2, tiled=True),
        lax.psum_scatter(grad_gains, DP, scatter_dimension=1, tiled=True),
        lax.psum_scatter(grad_gate, DP, scatter_dimension=0, tiled=True),
    )
    grad_gains = lax.psum(gain_part, TENSOR)
    local_squares = sum(
        (
            jnp.sum(piece_grad * piece_grad)
            for piece_grad in (grad_qkv, grad_out, grad_up, grad_down, grad_gate)
        )
    )
    local_squares = local_squares + jnp.sum(grad_gains * grad_gains) / lax.axis_size(TENSOR)
    squares = lax.psum(local_squares, (DP, TENSOR))
    grad_norm = jnp.sqrt(squares)
    factor = CLIP / jnp.maximum(grad_norm, CLIP)
    masters = (qkv_weight, out_weight, up_weight, down_weight, gain_rows, gate_weight)
    firsts = (qkv_first, out_first, up_first, down_first, gain_first, gate_first)
    seconds = (qkv_second, out_second, up_second, down_second, gain_second, gate_second)
    averages = (qkv_ema, out_ema, up_ema, down_ema, gain_ema, gate_ema)
    grads = (grad_qkv, grad_out, grad_up, grad_down, grad_gains, grad_gate)
    updated = []
    for group in range(6):
        updated.append(
            adamw(
                masters[group],
                firsts[group],
                seconds[group],
                averages[group],
                grads[group] * factor,
                STEP_RATES[group],
                STEP_DECAYS[group],
            )
        )
    feed_gain_grads = jnp.stack([grad_gains[1], grad_gains[3]]) * factor
    return (
        result_rows,
        grad_hidden,
        grad_norm,
        updated[0][0],
        updated[0][1],
        updated[0][2],
        updated[0][3],
        updated[1][0],
        updated[1][1],
        updated[1][2],
        updated[1][3],
        updated[2][0],
        updated[2][1],
        updated[2][2],
        updated[2][3],
        updated[3][0],
        updated[3][1],
        updated[3][2],
        updated[3][3],
        updated[4][0],
        updated[4][1],
        updated[4][2],
        updated[4][3],
        updated[5][0],
        updated[5][1],
        updated[5][2],
        updated[5][3],
        feed_gain_grads,
    )


VMEM_BYTES = 60 * 1024 * 1024
LOW = jnp.bfloat16
F32 = jnp.float32
WIDE = 128


def nn(left, right):
    return lax.dot_general(left, right, (((1,), (0,)), ((), ())), preferred_element_type=F32)


def nt(left, right):
    return lax.dot_general(left, right, (((1,), (1,)), ((), ())), preferred_element_type=F32)


def unit_rows(values):
    spread = lax.rsqrt(jnp.mean(values * values, axis=-1, keepdims=True) + 1e-06)
    return values * spread, spread


def low_normal(values, gain):
    hat, _ = unit_rows(values.astype(F32))
    return (hat * gain).astype(LOW)


def norm_back_rows(values, gain, grad_normal, grad):
    hat, spread = unit_rows(values.astype(F32))
    return grad.astype(F32) + norm_back(hat, spread, gain, grad_normal)


def norm_back(hat, spread, gain, grad_normal):
    scaled = grad_normal * gain
    inner = jnp.mean(scaled * hat, axis=-1, keepdims=True)
    return spread * (scaled - hat * inner)


def turn_store(target, base, columns, values, cosine, sine, scale):
    half = HEAD_DIM // 2
    first = values[:half]
    second = values[half:]
    target[base : base + half, columns] = ((first * cosine - second * sine).astype(LOW) * scale).astype(LOW)
    target[base + half : base + 2 * half, columns] = (
        (first * sine + second * cosine).astype(LOW) * scale
    ).astype(LOW)


def turned_back(values, cosine, sine):
    half = HEAD_DIM // 2
    first = values[:half]
    second = values[half:]
    return jnp.concatenate(
        [first * cosine + second * sine, second * cosine - first * sine], axis=0
    )


def per_head(values):
    return values.reshape(values.shape[0] // HEAD_DIM, HEAD_DIM, values.shape[1])


def head_sums(values):
    return jnp.sum(per_head(values), axis=1)


def spread_heads(values, like):
    return jnp.broadcast_to(values[:, None, :], (values.shape[0], HEAD_DIM, values.shape[1])).reshape(like)


def later(scores):
    count = scores.shape[1]
    place = lax.broadcasted_iota(jnp.int32, (count, count), 0)
    row = lax.broadcasted_iota(jnp.int32, (count, count), 1)
    own = jnp.where(place <= row, scores[-count:], -1e30)
    return jnp.concatenate([scores[:-count], own], axis=0)


def three_parts(values):
    high = values.astype(LOW).astype(F32)
    rest = values - high
    middle = rest.astype(LOW).astype(F32)
    return high, middle, rest - middle


def with_rows(top, first, parts):
    count = top.shape[1]
    row = lax.broadcasted_iota(jnp.int32, (16, count), 0)
    under = jnp.where(row == 0, first, 0.0)
    for index, part in enumerate(parts):
        under = jnp.where(row == index + 1, part, under)
    blank = jnp.zeros((WIDE - HEAD_DIM - 16, count), LOW)
    return jnp.concatenate([top, under.astype(LOW), blank], axis=0)


def extra_rows(count, bias):
    row = lax.broadcasted_iota(jnp.int32, (WIDE - HEAD_DIM, count), 0)
    place = lax.broadcasted_iota(jnp.int32, (WIDE - HEAD_DIM, count), 1)
    first = jnp.where(place < MEM, bias, 0.0)
    return jnp.where(row == 0, first, jnp.where(row <= 3, 1.0, 0.0)).astype(LOW)


ROWS = 256
BEGIN = -1
POST = -2
END = -3


def retrieved(near, c_ref, v_ref):
    place = lax.broadcasted_iota(jnp.int32, (MEM, SEG), 0)
    chosen = [(place == near[0, r : r + 1, :]).astype(F32).astype(LOW) for r in range(near.shape[1])]
    keys = [nn(c_ref[0], c).astype(LOW) for c in chosen]
    values = [nn(v_ref[0, :, :MEM], c).astype(LOW) for c in chosen]
    return keys, values, chosen


def column_sum(values):
    return jnp.sum(values, axis=0, keepdims=True)


def near_weights(plain, keys):
    logits = [column_sum(plain * key.astype(F32)) * HEAD_DIM ** (-0.5) for key in keys]
    top = functools.reduce(jnp.maximum, logits)
    raised = [jnp.exp(logit - top) for logit in logits]
    inverse = 1.0 / functools.reduce(jnp.add, raised)
    return [e * inverse for e in raised]


def weigh(soft, values):
    return functools.reduce(jnp.add, [a * v.astype(F32) for a, v in zip(soft, values)])


def small_row(small, row):
    return small[0].astype(F32).T[row : row + 1]


def gate_logits(small, normal, heads):
    each = heads // small.shape[0]
    rows = [small[part].astype(F32).T[:each] for part in range(small.shape[0])]
    blank = jnp.zeros((WIDE - heads, small.shape[1]), F32)
    return nn(jnp.concatenate(rows + [blank], axis=0).astype(LOW), normal)[:heads]


def attend_kernel(retrieve, guest, *refs):
    refs = list(refs)
    resets, hidden, memory, slab, small, cosine, sine = refs[:7]
    refs = refs[7:]
    if retrieve:
        near = refs.pop(0)
    guest_ins, refs = refs[: guest.ins], refs[guest.ins :]
    out, q_ref, k_ref, v_ref, log_ref, mix_ref = refs[:6]
    refs = refs[6:]
    if retrieve:
        o_ref, qu_ref, c_ref = refs[:3]
        refs = refs[3:]
    guest_outs, refs = refs[: guest.outs], refs[guest.outs :]
    turned, k_rows, n_both = refs[:3]
    step = pl.program_id(0)
    visit = guest.bind(guest_ins, guest_outs, refs[3:], step)
    parts, width, _ = slab.shape
    visit(BEGIN)
    gain = small_row(small, guest.gain_row)
    cols = width // parts
    pairs = width // WIDE

    @pl.when(step == 0)
    def _():
        for part in range(parts):
            for kind in range(3):
                turned[pl.ds(kind * width + part * cols, cols), :] = slab[
                    part, :, kind * cols : (kind + 1) * cols
                ].T

    bias = jnp.where(resets[lax.axis_index(TENSOR) * pl.num_programs(0) + step] == 0, 0.0, -1e30)
    n_both[:, MEM:] = low_normal(hidden[0], gain).T
    n_both[:, :MEM] = low_normal(memory[0], gain).T
    scale = HEAD_DIM ** (-0.5)
    all_rows = slice(None)
    query = nn(turned[:width], n_both[:, MEM:])
    for head in range(width // HEAD_DIM):
        base = head * HEAD_DIM
        turn_store(
            q_ref.at[0], base, all_rows, query[base : base + HEAD_DIM], cosine[:, MEM:], sine[:, MEM:], scale
        )
    if retrieve:
        qu_ref[0] = query.astype(LOW)
    keys = nn(turned[width : 2 * width], n_both[...])
    for head in range(width // HEAD_DIM):
        base = head * HEAD_DIM
        turn_store(k_ref.at[0], base, all_rows, keys[base : base + HEAD_DIM], cosine[...], sine[...], 1.0)
    if retrieve:
        c_ref[0] = keys[:, :MEM].astype(LOW)
    v_ref[0] = nn(turned[2 * width :], n_both[...]).astype(LOW)
    extra = extra_rows(k_ref.shape[2], bias)
    for head in range(width // HEAD_DIM):
        own = slice(head * HEAD_DIM, (head + 1) * HEAD_DIM)
        k_rows[head] = jnp.concatenate([k_ref[0, own, :], extra], axis=0).T

    def head_pair(pair, carry):
        visit(pair)
        for which in range(2):
            head = pair * 2 + which
            own = pl.ds(pl.multiple_of(head * HEAD_DIM, HEAD_DIM), HEAD_DIM)
            for block in range(SEG // ROWS):
                count = MEM + (block + 1) * ROWS
                span = slice(block * ROWS, (block + 1) * ROWS)
                wanted = with_rows(q_ref[0, own, span], 1.0, ())
                scores = later(nn(k_rows[head, :count], wanted))
                top = jnp.max(scores, axis=0, keepdims=True)
                soft = jnp.exp(scores - top)
                total = jnp.sum(soft, axis=0, keepdims=True)
                got = nn(v_ref[0, own, :count], soft.astype(LOW)) * (1.0 / total)
                log_ref[0, pl.ds(head, 1), span] = top + jnp.log(total)
                if retrieve:
                    o_ref[0, own, span] = got
                else:
                    mix_ref[0, own, span] = got.astype(LOW)
        return carry

    lax.fori_loop(0, pairs, head_pair, 0)
    visit(POST)
    if retrieve:
        keys_near, values_near, _ = retrieved(near, c_ref, v_ref)
        opened = jax.nn.sigmoid(gate_logits(small, n_both[:, MEM:], width // HEAD_DIM))
        for head in range(width // HEAD_DIM):
            own = slice(head * HEAD_DIM, (head + 1) * HEAD_DIM)
            soft = near_weights(qu_ref[0, own, :].astype(F32), [a[own] for a in keys_near])
            fetched = weigh(soft, [a[own] for a in values_near])
            gate = opened[head : head + 1]
            mix_ref[0, own, :] = (gate * o_ref[0, own, :] + (1.0 - gate) * fetched).astype(LOW)
    mix = mix_ref[0].T
    total = hidden[0].astype(F32)
    for part in range(parts):
        total = total + nt(mix[:, part * cols : (part + 1) * cols], slab[part, :, 3 * cols : 4 * cols])
    out[0] = total
    visit(END)


def attend_back_kernel(retrieve, guest, *refs):
    refs = list(refs)
    resets, hidden, memory, slab, small, cosine, sine = refs[:7]
    grad, q_ref, k_ref, v_ref, log_ref, mix_ref = refs[7:13]
    refs = refs[13:]
    if retrieve:
        near, o_ref, qu_ref, c_ref = refs[:4]
        refs = refs[4:]
    guest_ins, refs = refs[: guest.ins], refs[guest.ins :]
    grad_in, grad_slab = refs[:2]
    refs = refs[2:]
    if not retrieve:
        away = refs.pop(0)
    guest_outs, refs = refs[: guest.outs], refs[guest.outs :]
    wo, k_rows, v_rows, n_both, do, dq, dk, dv, total, inner_ref = refs[:10]
    visit = guest.bind(guest_ins, guest_outs, refs[10:], pl.program_id(0))
    visit(BEGIN)
    gain = small_row(small, guest.gain_row)
    parts, width, _ = slab.shape
    cols = width // parts
    pairs = width // WIDE
    heads = width // HEAD_DIM
    step = pl.program_id(0)

    @pl.when(step == 0)
    def _():
        total[...] = jnp.zeros_like(total)
        for part in range(parts):
            wo[pl.ds(part * cols, cols), :] = slab[part, :, 3 * cols : 4 * cols].T

    bias = jnp.where(resets[lax.axis_index(TENSOR) * pl.num_programs(0) + step] == 0, 0.0, -1e30)
    scale = HEAD_DIM ** (-0.5)
    n_both[:, MEM:] = low_normal(hidden[0], gain).T
    n_both[:, :MEM] = low_normal(memory[0], gain).T
    grad_low = grad[0].astype(LOW)
    grad_t = grad_low.T
    for part in range(parts):
        total[part, :, 3 * cols : 4 * cols] += nt(grad_t, mix_ref[0, part * cols : (part + 1) * cols, :])
    grad_mix = nn(wo[...], grad_t).astype(LOW)
    if retrieve:
        keys_near, values_near, chosen = retrieved(near, c_ref, v_ref)
        opened = jax.nn.sigmoid(gate_logits(small, n_both[:, MEM:], heads))
        gate_rows, extra_q = [], []
        near_k, near_v = [[] for _ in chosen], [[] for _ in chosen]
        for head in range(heads):
            own = slice(head * HEAD_DIM, (head + 1) * HEAD_DIM)
            plain = qu_ref[0, own, :].astype(F32)
            keys, values = [a[own] for a in keys_near], [a[own] for a in values_near]
            soft = near_weights(plain, keys)
            gate = opened[head : head + 1]
            grads = grad_mix[own].astype(F32)
            attended = o_ref[0, own, :]
            grad_attended = (gate * grads).astype(LOW)
            do[own, :] = grad_attended
            inner_ref[head : head + 1, :] = column_sum(grad_attended.astype(F32) * attended)
            gate_sum = column_sum(grads * (attended - weigh(soft, values)))
            gate_rows.append(gate_sum * gate * (1.0 - gate))
            grad_fetched = (1.0 - gate) * grads
            grad_soft = [column_sum(grad_fetched * v.astype(F32)) for v in values]
            mean = functools.reduce(jnp.add, [a * b for a, b in zip(soft, grad_soft)])
            grad_logits = [a * (b - mean) * scale for a, b in zip(soft, grad_soft)]
            extra_q.append(weigh(grad_logits, keys))
            for r in range(len(chosen)):
                near_k[r].append((grad_logits[r] * plain).astype(LOW))
                near_v[r].append((soft[r] * grad_fetched).astype(LOW))
        grad_gate = jnp.concatenate(gate_rows, axis=0)
        both = jnp.concatenate(chosen, axis=1)
        extra_k = nt(jnp.concatenate([jnp.concatenate(a, axis=0) for a in near_k], axis=1), both)
        extra_v = nt(jnp.concatenate([jnp.concatenate(a, axis=0) for a in near_v], axis=1), both)
    else:
        do[...] = grad_mix
        for head in range(heads):
            own = slice(head * HEAD_DIM, (head + 1) * HEAD_DIM)
            inner_ref[head : head + 1, :] = column_sum(
                grad_mix[own].astype(F32) * mix_ref[0, own, :].astype(F32)
            )
    extra = extra_rows(k_ref.shape[2], bias)
    for head in range(heads):
        own = slice(head * HEAD_DIM, (head + 1) * HEAD_DIM)
        k_rows[head] = jnp.concatenate([k_ref[0, own, :], extra], axis=0).T
        v_rows[head] = jnp.concatenate([v_ref[0, own, :], extra], axis=0).T

    def head_pair(pair, carry):
        visit(pair)
        for which in range(2):
            head = pair * 2 + which
            own = pl.ds(pl.multiple_of(head * HEAD_DIM, HEAD_DIM), HEAD_DIM)
            row = pl.ds(head, 1)
            for block in reversed(range(SEG // ROWS)):
                count = MEM + (block + 1) * ROWS
                span = slice(block * ROWS, (block + 1) * ROWS)
                wanted = with_rows(q_ref[0, own, span], 1.0, three_parts(-log_ref[0, row, span]))
                grad_o = with_rows(do[own, span], 0.0, three_parts(-inner_ref[row, span]))
                probs = jnp.exp(later(nn(k_rows[head, :count], wanted)))
                probs_low = probs.astype(LOW)
                grad_scores = (probs * nn(v_rows[head, :count], grad_o)).astype(LOW)
                dq[own, span] = nn(k_ref[0, own, :count], grad_scores) * scale
                key_part = nt(q_ref[0, own, span], grad_scores)
                value_part = nt(do[own, span], probs_low)
                if block == SEG // ROWS - 1:
                    dk[own, :] = key_part
                    dv[own, :] = value_part
                else:
                    dk[own, :count] += key_part
                    dv[own, :count] += value_part
        return carry

    lax.fori_loop(0, pairs, head_pair, 0)
    visit(POST)
    cos_rows, sin_rows = cosine[:, MEM:], sine[:, MEM:]
    turned_q = []
    turned_k = []
    for head in range(heads):
        own = slice(head * HEAD_DIM, (head + 1) * HEAD_DIM)
        turned_q.append(turned_back(dq[own, :], cos_rows, sin_rows))
        turned_k.append(turned_back(dk[own, :], cosine[...], sine[...]))
    grad_q = jnp.concatenate(turned_q, axis=0)
    grad_k = jnp.concatenate(turned_k, axis=0)
    grad_v = dv[...]
    if retrieve:
        grad_q = grad_q + jnp.concatenate(extra_q, axis=0)
        grad_k = jnp.concatenate([grad_k[:, :MEM] + extra_k, grad_k[:, MEM:]], axis=1)
        grad_v = jnp.concatenate([grad_v[:, :MEM] + extra_v, grad_v[:, MEM:]], axis=1)
    grad_q = grad_q.astype(LOW)
    grad_k = grad_k.astype(LOW)
    grad_v = grad_v.astype(LOW)
    normal_t = jnp.zeros((width, SEG), F32)
    for part in range(parts):
        own = slice(part * cols, (part + 1) * cols)
        total[part, :, :cols] += nt(n_both[:, MEM:], grad_q[own])
        total[part, :, cols : 2 * cols] += nt(n_both[...], grad_k[own])
        total[part, :, 2 * cols : 3 * cols] += nt(n_both[...], grad_v[own])
        normal_t = (
            normal_t
            + nn(slab[part, :, :cols], grad_q[own])
            + nn(slab[part, :, cols : 2 * cols], grad_k[own, MEM:])
            + nn(slab[part, :, 2 * cols : 3 * cols], grad_v[own, MEM:])
        )
    if retrieve:
        each = heads // parts
        blank = jnp.zeros((WIDE - each, SEG), F32)
        for part in range(parts):
            own_gate = jnp.concatenate([grad_gate[part * each : (part + 1) * each], blank], axis=0)
            own_gate = own_gate.astype(LOW)
            normal_t = normal_t + nn(small[part], own_gate)
            total[part, :, 4 * cols :] += nt(n_both[:, MEM:], own_gate)
    grad_in[0] = norm_back_rows(hidden[0], gain, normal_t.T, grad[0])
    if not retrieve:
        half = away.shape[1]
        other = pl.multiple_of((1 - lax.axis_index(TENSOR)) * half, half)
        away[0] = grad_in[0, pl.ds(other, half), :].astype(LOW)

    @pl.when(step == pl.num_programs(0) - 1)
    def _():
        grad_slab[...] = total[...].astype(grad_slab.dtype)

    visit(END)


GELU_A = math.sqrt(2.0 / math.pi)
GELU_B = 0.044715


def feed_kernel(guest, *refs):
    hidden, small, up, down = refs[:4]
    guest_ins, refs = refs[4 : 4 + guest.ins], refs[4 + guest.ins :]
    out, guest_outs, refs = refs[0], refs[1 : 1 + guest.outs], refs[1 + guest.outs :]
    normal = refs[0]
    visit = guest.bind(guest_ins, guest_outs, refs[1:], pl.program_id(0))
    visit(BEGIN)

    @pl.when(pl.program_id(0) == 0)
    def _():
        rows = hidden[...]
        normal[...] = low_normal(rows, small_row(small, guest.gain_row))
        out[...] = rows

    pre = nn(normal[...], up[0])
    bent = jnp.tanh(GELU_A * (pre + GELU_B * (pre * pre * pre)))
    active = (0.5 * pre * (1.0 + bent)).astype(LOW)
    out[...] += nt(active, down[0])
    visit(END)


def feed_back_kernel(ahead, guest, *refs):
    hidden, small, up, down, grad = refs[:5]
    refs = list(refs[5:])
    guest_ins, refs = refs[: guest.ins], refs[guest.ins :]
    if ahead:
        result = refs.pop(0)
    grad_in, grad_slab = refs[:2]
    guest_outs, refs = refs[2 : 2 + guest.outs], refs[2 + guest.outs :]
    normal, normal_t, grad_low, grad_t, total = refs[:5]
    refs = refs[5:]
    if ahead:
        rows_out = refs.pop(0)
    visit = guest.bind(guest_ins, guest_outs, refs, pl.program_id(0))
    visit(BEGIN)

    @pl.when(pl.program_id(0) == 0)
    def _():
        low = low_normal(hidden[...], small_row(small, guest.gain_row))
        normal[...] = low
        normal_t[...] = low.T
        start = grad[...].astype(LOW)
        grad_low[...] = start
        grad_t[...] = start.T
        total[...] = jnp.zeros_like(total)
        if ahead:
            rows_out[...] = hidden[...]

    pre = nn(normal[...], up[0])
    square = pre * pre
    bent = jnp.tanh(GELU_A * (pre + GELU_B * (square * pre)))
    active = (0.5 * pre * (1.0 + bent)).astype(LOW)
    if ahead:
        rows_out[...] += nt(active, down[0])
    slope = 0.5 * (1.0 + bent) + 0.5 * pre * (1.0 - bent * bent) * (
        GELU_A * (1.0 + 3.0 * GELU_B * square)
    )
    grad_pre = (nn(grad_low[...], down[0]) * slope).astype(LOW)
    grad_slab[0, 0] = nn(normal_t[...], grad_pre).astype(grad_slab.dtype)
    grad_slab[1, 0] = nn(grad_t[...], active).astype(grad_slab.dtype)
    total[...] += nt(grad_pre, up[0])

    @pl.when(pl.program_id(0) == pl.num_programs(0) - 1)
    def _():
        gain = small_row(small, guest.gain_row)
        grad_in[...] = norm_back_rows(hidden[...], gain, total[...], grad[...])
        if ahead:
            result[...] = rows_out[...].astype(LOW)

    visit(END)


def whole_spec(shape):
    return pl.BlockSpec(shape, lambda i: (0,) * len(shape))


def seg_spec(shape):
    return pl.BlockSpec((1,) + tuple(shape[1:]), lambda i: (i,) + (0,) * (len(shape) - 1))


def cost(flops, moved):
    return pl.CostEstimate(flops=int(flops), bytes_accessed=int(moved), transcendentals=0)


def any_spec():
    return pl.BlockSpec(memory_space=pl.ANY)


def slab_specs(slab, width, cols):
    columns = 4 * cols
    return pl.BlockSpec((slab.shape[0], width, columns), lambda i: (0, 0, 0))


def small_spec(slab):
    last = slab.shape[2] // WIDE - 1
    return pl.BlockSpec((slab.shape[0], slab.shape[1], WIDE), lambda i: (0, 0, last))


def run(kernel, guest, grid, ins, specs, outs, out_specs, scratch, flops, moved):
    more_ins, more_outs, more_out_specs, more_scratch = guest.parts()
    params = dict(vmem_limit_bytes=VMEM_BYTES)
    if guest.number is not None:
        params.update(collective_id=guest.number, has_side_effects=True)
    return pl.pallas_call(
        kernel,
        grid=(grid,),
        in_specs=specs + [any_spec()] * len(more_ins),
        out_specs=out_specs + more_out_specs,
        out_shape=outs + more_outs,
        scratch_shapes=scratch + more_scratch,
        compiler_params=pltpu.CompilerParams(**params),
        cost_estimate=cost(flops, moved),
        input_output_aliases=guest.aliases(len(ins), len(outs)),
    )(*ins, *more_ins)


def attend(hidden, memory, resets, slab, small, cosine, sine, near, guest):
    retrieve = near is not None
    count, rows, width = hidden.shape
    keys = memory.shape[1] + rows
    heads = width // HEAD_DIM
    cols = width // slab.shape[0]
    ins = [resets, hidden, memory, slab, small, cosine, sine]
    specs = [pl.BlockSpec(memory_space=pltpu.SMEM), seg_spec(hidden.shape), seg_spec(memory.shape)]
    specs += [slab_specs(slab, width, cols), small_spec(small)]
    specs += [whole_spec(cosine.shape), whole_spec(sine.shape)]
    if retrieve:
        ins.append(near)
        specs.append(seg_spec(near.shape))
    outs = [
        jax.ShapeDtypeStruct((count, rows, width), F32),
        jax.ShapeDtypeStruct((count, width, rows), LOW),
        jax.ShapeDtypeStruct((count, width, keys), LOW),
        jax.ShapeDtypeStruct((count, width, keys), LOW),
        jax.ShapeDtypeStruct((count, heads, rows), F32),
        jax.ShapeDtypeStruct((count, width, rows), LOW),
    ]
    if retrieve:
        outs += [
            jax.ShapeDtypeStruct((count, width, rows), F32),
            jax.ShapeDtypeStruct((count, width, rows), LOW),
            jax.ShapeDtypeStruct((count, width, memory.shape[1]), LOW),
        ]
    scratch = [
        pltpu.VMEM((3 * width, width), LOW),
        pltpu.VMEM((heads, keys, WIDE), LOW),
        pltpu.VMEM((width, keys), LOW),
    ]
    kernel = functools.partial(attend_kernel, retrieve, guest)
    out_specs = [seg_spec(o.shape) for o in outs]
    return run(kernel, guest, count, ins, specs, outs, out_specs, scratch, count * 1.2e10, 2e7)


def attend_back(hidden, memory, resets, slab, small, cosine, sine, grad, saved, near, guest):
    retrieve = near is not None
    count, rows, width = hidden.shape
    keys = memory.shape[1] + rows
    heads = width // HEAD_DIM
    parts = slab.shape[0]
    cols = width // parts
    ins = [resets, hidden, memory, slab, small, cosine, sine, grad] + list(saved[:5])
    specs = [pl.BlockSpec(memory_space=pltpu.SMEM), seg_spec(hidden.shape), seg_spec(memory.shape)]
    specs += [slab_specs(slab, width, cols), small_spec(small)]
    specs += [whole_spec(cosine.shape), whole_spec(sine.shape)]
    specs += [seg_spec(a.shape) for a in ins[7:]]
    if retrieve:
        more = [near] + list(saved[5:8])
        ins += more
        specs += [seg_spec(a.shape) for a in more]
    total = (parts, width, 4 * cols + (WIDE if retrieve else 0))
    outs = [
        jax.ShapeDtypeStruct((count, rows, width), F32),
        jax.ShapeDtypeStruct(total, LOW),
    ]
    out_specs = [seg_spec(outs[0].shape), whole_spec(total)]
    if not retrieve:
        outs.append(jax.ShapeDtypeStruct((count, rows // parts, width), LOW))
        out_specs.append(seg_spec(outs[-1].shape))
    scratch = [
        pltpu.VMEM((width, width), LOW),
        pltpu.VMEM((heads, keys, WIDE), LOW),
        pltpu.VMEM((heads, keys, WIDE), LOW),
        pltpu.VMEM((width, keys), LOW),
        pltpu.VMEM((width, rows), LOW),
        pltpu.VMEM((width, rows), F32),
        pltpu.VMEM((width, keys), F32),
        pltpu.VMEM((width, keys), F32),
        pltpu.VMEM(total, F32),
        pltpu.VMEM((heads, rows), F32),
    ]
    kernel = functools.partial(attend_back_kernel, retrieve, guest)
    return run(kernel, guest, count, ins, specs, outs, out_specs, scratch, count * 3e10, 3e7)


def feed_specs(width, units, chunk):
    each = units // chunk
    up = pl.BlockSpec((1, width, chunk), lambda i: (i // each, 0, i % each))
    down = pl.BlockSpec((1, width, chunk), lambda i: (i // each, 0, each + i % each))
    return up, down, each


CHUNK = 512


def feed(hidden, slab, small, guest):
    rows, width = hidden.shape
    parts, _, both = slab.shape
    up, down, each = feed_specs(width, both // 2, CHUNK)
    ins = [hidden, small, slab, slab]
    specs = [whole_spec(hidden.shape), small_spec(small), up, down]
    outs = [jax.ShapeDtypeStruct(hidden.shape, F32)]
    scratch = [pltpu.VMEM((rows, width), LOW)]
    kernel = functools.partial(feed_kernel, guest)
    flops = 2 * rows * width * parts * both
    return run(kernel, guest, parts * each, ins, specs, outs, [whole_spec(hidden.shape)], scratch, flops, 1e7)


def feed_back(hidden, slab, small, grad, ahead, guest):
    rows, width = hidden.shape
    parts, _, both = slab.shape
    units = both // 2
    up, down, each = feed_specs(width, units, CHUNK)
    outs = [
        jax.ShapeDtypeStruct((rows, width), F32),
        jax.ShapeDtypeStruct((2, parts, width, units), LOW),
    ]
    out_specs = [
        whole_spec((rows, width)),
        pl.BlockSpec((2, 1, width, CHUNK), lambda i: (0, i // each, 0, i % each)),
    ]
    scratch = [
        pltpu.VMEM((rows, width), LOW),
        pltpu.VMEM((width, rows), LOW),
        pltpu.VMEM((rows, width), LOW),
        pltpu.VMEM((width, rows), LOW),
        pltpu.VMEM((rows, width), F32),
    ]
    if ahead:
        outs.insert(0, jax.ShapeDtypeStruct((rows, width), LOW))
        out_specs.insert(0, whole_spec((rows, width)))
        scratch.append(pltpu.VMEM((rows, width), F32))
    ins = [hidden, small, slab, slab, grad]
    specs = [whole_spec(hidden.shape), small_spec(small), up, down, whole_spec(grad.shape)]
    kernel = functools.partial(feed_back_kernel, ahead, guest)
    flops = 6 * rows * width * parts * both
    return run(kernel, guest, parts * each, ins, specs, outs, out_specs, scratch, flops, 2e7)


MESH = pl.DeviceIdType.MESH


def spot():
    place = lax.axis_index(DP)
    return place // 4, place // 2 % 2, place % 2, lax.axis_index(TENSOR)


def at(z, x, core, y):
    return ((z * 2 + x) * 2 + core, y)


def announce(partners):
    for partner in partners:
        pl.semaphore_signal(
            pltpu.get_barrier_semaphore(), inc=1, device_id=partner, device_id_type=MESH
        )


def await_all(partners):
    pl.semaphore_wait(pltpu.get_barrier_semaphore(), len(partners))


def greet(partners):
    announce(partners)
    await_all(partners)


def send(source, target, sems, device):
    return pltpu.make_async_remote_copy(
        src_ref=source,
        dst_ref=target,
        send_sem=sems[0],
        recv_sem=sems[1],
        device_id=device,
        device_id_type=MESH,
    )


def halves(cols):
    first = cols // (2 * WIDE) * WIDE
    return pl.ds(0, first), pl.ds(first, cols - first)


class Hop:
    def __init__(self, source, target, buffer, sems):
        self.first = pltpu.make_async_copy(source, buffer, sems.at[0])
        self.second = pltpu.make_async_copy(buffer, target, sems.at[1])

    def start(self):
        self.first.start()

    def push(self):
        self.first.wait()
        self.second.start()

    def wait(self):
        self.second.wait()


class Burst:
    def __init__(self, source, target, sems, device, cuts):
        self.whole = send(source, target, sems, device)
        self.pieces = []
        for place in itertools.product(*[range(cut) for cut in cuts]):
            self.pieces.append(send(source.at[place], target.at[place], sems, device))

    def start(self):
        for piece in self.pieces:
            piece.start()

    def wait(self):
        self.whole.wait()


class Gather:
    def __init__(self, shard, full, sends, receives, local, line=None, buffer=None):
        self.shard, self.full, self.local, self.line, self.buffer = shard, full, local, line, buffer
        self.sems = lambda k: (sends.at[k], receives.at[k])
        self.depth = full.shape[1]
        self.left, self.right = halves(full.shape[-1])

    def sibling(self, source, place, k):
        z, x, core, y = spot()
        return Burst(source, place, self.sems(self.depth + k), at(z, x, 1 - core, y), (self.depth,))

    def along_z(self):
        z, x, core, y = spot()
        mine = self.full.at[y, z, x, core]
        return [
            send(self.shard, mine, self.sems(k - 1), at((z + k) % self.depth, x, core, y))
            for k in range(1, self.depth)
        ]

    def to_sides(self):
        z, x, core, y = spot()
        mine = self.full.at[y, :, x, core]
        held = mine if self.line is None else self.line
        base = self.depth + 4
        return [
            Burst(held, mine, self.sems(base), at(z, 1 - x, core, y), (self.depth,)),
            Burst(held, mine, self.sems(base + 1), at(z, x, core, 1 - y), (self.depth,)),
            self.sibling(held, mine, 0),
        ]

    def onward(self):
        z, x, core, y = spot()
        base = self.depth + 6
        one = self.full.at[y, :, 1 - x, core]
        two = self.full.at[1 - y, :, x, core]
        left = one.at[:, :, self.left]
        right = two.at[:, :, self.right]
        return [
            Burst(left, left, self.sems(base), at(z, x, core, 1 - y), (self.depth,)),
            Burst(right, right, self.sems(base + 1), at(z, 1 - x, core, y), (self.depth,)),
            self.sibling(one, one, 1),
            self.sibling(two, two, 2),
        ]

    def to_sibling(self):
        z, x, core, y = spot()
        mine = self.full.at[1 - y, :, 1 - x, core]
        return [self.sibling(mine, mine, 3)]

    def keep(self):
        z, x, core, y = spot()
        if self.line is not None:
            return Hop(self.line, self.full.at[y, :, x, core], self.buffer, self.local)
        return pltpu.make_async_copy(self.shard, self.full.at[y, z, x, core], self.local)

    def start(self, phase):
        first = phase == (0 if self.line is None else 1)
        if first:
            self.keep().start()
        for copy in self.phase(phase):
            copy.start()
        if first and self.line is not None:
            self.keep().push()

    def finish(self, phase):
        if phase == (0 if self.line is None else 1):
            self.keep().wait()
        for copy in self.phase(phase):
            copy.wait()

    def phase(self, phase):
        return (self.along_z, self.to_sides, self.onward, self.to_sibling)[phase]()


EXTRA = 8
PHASES = 4


def neighbours_of(depth):
    z, x, core, y = spot()
    around = [at((z + k) % depth, x, core, y) for k in range(1, depth)]
    return around + [at(z, 1 - x, core, y), at(z, x, core, 1 - y), at(z, x, 1 - core, y)]


def pipelined(groups):
    for stage in range(len(groups) + PHASES):
        for index, group in enumerate(groups):
            phase = stage - index
            if 0 < phase <= PHASES:
                group.finish(phase - 1)
            if 0 <= phase < PHASES:
                group.start(phase)


class Line:
    def __init__(self, shard, line, sends, receives, local):
        self.shard, self.line, self.sends, self.receives, self.local = shard, line, sends, receives, local

    def copies(self):
        z, x, core, y = spot()
        depth = self.line.shape[0]
        mine = self.line.at[z]
        away = [
            send(self.shard, mine, (self.sends.at[k], self.receives.at[k]), at((z + k) % depth, x, core, y))
            for k in range(1, depth)
        ]
        return [pltpu.make_async_copy(self.shard, mine, self.local)] + away

    def start(self):
        for copy in self.copies():
            copy.start()

    def finish(self):
        for copy in self.copies():
            copy.wait()


class Trade:
    def __init__(self, source, target, sends, receives, local, buffer, first=0):
        self.source, self.target, self.first = source, target, first
        self.sems, self.local, self.buffer = (sends, receives), local, buffer

    def copies(self):
        z, x, core, y = spot()
        share, rows, count = self.target.shape[0], self.source.shape[1], self.buffer.shape[0]
        place = self.target.at[
            pl.ds(self.first, count), pl.ds(pl.multiple_of(y * rows, rows), rows)
        ]
        mine = self.source.at[pl.ds(y * share + self.first, count)]
        away = self.source.at[pl.ds((1 - y) * share + self.first, count)]
        return [
            Hop(mine, place, self.buffer, self.local),
            send(away, place, self.sems, at(z, x, core, 1 - y)),
        ]

    def start(self):
        copies = self.copies()
        for copy in copies:
            copy.start()
        copies[0].push()

    def finish(self):
        for copy in self.copies():
            copy.wait()


def sems(*counts):
    return [pltpu.SemaphoreType.DMA((count,)) for count in counts]


def trade_buffer(rows, count=None):
    share = rows.shape[0] // lax.axis_size(TENSOR)
    return pltpu.VMEM((count or share,) + rows.shape[1:], rows.dtype)


def in_two(count):
    early = (count + 1) // 2
    return [(first, size) for first, size in ((0, early), (early, count - early)) if size]


def columns(ref, first, last):
    return ref.at[(slice(None),) * (len(ref.shape) - 1) + (pl.ds(first, last - first),)]


def start_kernel(*refs):
    qkv, out, up, down, gain, gate, acts, memory_one, memory_two, near = refs[:10]
    attn_one, attn_two, feed_one, feed_two, full, line, rows, own_one, own_two, own_near = refs[10:20]
    sends, receives, local, more_sends, more_receives, own_sems = refs[20:26]
    trade_sends, trade_receives, trade_sems = refs[26:29]
    buffers, trade_buffers = refs[29:32], refs[32:]
    near_devices = neighbours_of(line.shape[0])
    announce(near_devices)
    cols = out.shape[2]
    units = up.shape[2]
    y = lax.axis_index(TENSOR)
    pairs = ((memory_one, own_one), (memory_two, own_two), (near, own_near))
    owns = [
        Hop(a.at[pl.ds(y * b.shape[0], b.shape[0])], b, buffers[k], own_sems.at[k])
        for k, (a, b) in enumerate(pairs)
    ]

    def pack_attn(target, depth):
        for kind in range(3):
            target[:, kind * cols : (kind + 1) * cols] = qkv[depth, kind].astype(LOW)
        target[:, 3 * cols : 4 * cols] = out[depth].astype(LOW)

    def pack_feed(target, depth):
        target[:, :units] = up[depth].astype(LOW)
        target[:, units:] = down[depth].astype(LOW)

    pack_attn(attn_one, 0)
    blank = jnp.zeros((WIDE - gate.shape[0] - gain.shape[0], gain.shape[1]), F32)
    small = jnp.concatenate([gate[...], gain[...], blank], axis=0)
    attn_one[:, 4 * cols :] = small.T.astype(LOW)
    groups = []
    for g, (first, last) in enumerate(((0, 2 * cols), (2 * cols, 4 * cols + WIDE))):
        part, whole = columns(attn_one, first, last), columns(full, first, last)
        groups.append(Gather(part, whole, sends.at[g], receives.at[g], local.at[g]))
    trades, first = [], 0
    for k, buffer in enumerate(trade_buffers):
        pair = (trade_sends.at[k], trade_receives.at[k], trade_sems.at[k])
        trades.append(Trade(acts, rows, *pair, buffer, first))
        first += buffer.shape[0]
    fetch = Line(feed_one, line, more_sends, more_receives, local.at[2])
    await_all(near_devices)
    groups[0].start(0)
    groups[1].start(0)
    trades[0].start()
    for copy in owns:
        copy.start()
    pack_feed(feed_one, 0)
    pack_attn(attn_two, 1)
    pack_feed(feed_two, 1)
    for copy in owns:
        copy.push()
    for phase in range(PHASES):
        for group in groups:
            group.finish(phase)
            if phase + 1 < PHASES:
                group.start(phase + 1)
        if phase == 0:
            fetch.start()
        if phase == 1:
            for trade in trades[1:]:
                trade.start()
    for trade in trades:
        trade.finish()
    fetch.finish()
    for copy in owns:
        copy.wait()


def start_up(qkv, out, up, down, gain, gate, acts, memory_one, memory_two, near, number):
    depth = lax.axis_size(DP) // 4
    parts = lax.axis_size(TENSOR)
    rows, cols, units = qkv.shape[2], qkv.shape[3], up.shape[2]
    vmem = pl.BlockSpec(memory_space=pltpu.VMEM)
    shapes = [(rows, 4 * cols + WIDE), (rows, 4 * cols), (rows, 2 * units), (rows, 2 * units)]
    shapes += [(parts, depth, 2, 2, rows, 4 * cols + WIDE), (depth, rows, 2 * units)]
    shapes += [(acts.shape[0] // parts, acts.shape[1] * parts, acts.shape[2])]
    outs = [jax.ShapeDtypeStruct(s, LOW) for s in shapes]
    for a in (memory_one, memory_two, near):
        outs.append(jax.ShapeDtypeStruct((a.shape[0] // parts,) + a.shape[1:], a.dtype))
    return pl.pallas_call(
        start_kernel,
        out_shape=outs,
        in_specs=[vmem] * 6 + [any_spec()] * 4,
        out_specs=[vmem] * 4 + [any_spec()] * 6,
        scratch_shapes=[pltpu.SemaphoreType.DMA((2, depth + EXTRA))] * 2
        + sems(3, depth, depth)
        + [pltpu.SemaphoreType.DMA((3, 2))]
        + sems(2, 2)
        + [pltpu.SemaphoreType.DMA((2, 2))]
        + [pltpu.VMEM(o.shape, o.dtype) for o in outs[7:]]
        + [trade_buffer(acts, count) for _, count in in_two(acts.shape[0] // parts)],
        compiler_params=pltpu.CompilerParams(
            collective_id=number, has_side_effects=True, vmem_limit_bytes=VMEM_BYTES
        ),
    )(qkv, out, up, down, gain, gate, acts, memory_one, memory_two, near)


def flat(full):
    return full.reshape((full.shape[0], -1, full.shape[-1]))


class Reduce:
    def __init__(self, whole, out, own, one, two_left, two_right, three, four, sends, receives, local):
        self.whole, self.out, self.own, self.one = whole, out, own, one
        self.two_left, self.two_right, self.three, self.four = two_left, two_right, three, four
        self.sems = lambda k: (sends.at[k], receives.at[k])
        self.local = local
        self.kinds, self.parts, self.depth = whole.shape[:3]
        self.cols = whole.shape[-1]
        self.left, self.right = halves(self.cols)
        self.cut = self.left.size
        self.cuts = (self.kinds, self.depth)

    def keep(self):
        z, x, core, y = spot()
        return pltpu.make_async_copy(self.whole.at[:, :, :, :, core], self.own, self.local)

    def sibling(self, part, side, k):
        z, x, core, y = spot()
        away = self.whole.at[:, part, :, side, 1 - core]
        return Burst(away, self.one.at[:, part, :, side], self.sems(k), at(z, x, 1 - core, y), self.cuts)

    def first(self):
        z, x, core, y = spot()
        return [self.sibling(1 - y, 1 - x, 0)]

    def second(self):
        z, x, core, y = spot()
        far = self.own.at[:, 1 - y, :, 1 - x]
        return [
            Burst(far.at[:, :, :, self.left], self.two_left, self.sems(1), at(z, 1 - x, core, y), self.cuts),
            Burst(far.at[:, :, :, self.right], self.two_right, self.sems(2), at(z, x, core, 1 - y), self.cuts),
            self.sibling(y, 1 - x, 3),
            self.sibling(1 - y, x, 4),
        ]

    def third(self):
        z, x, core, y = spot()
        return [
            Burst(self.own.at[:, y, :, 1 - x], self.three, self.sems(5), at(z, 1 - x, core, y), self.cuts),
            Burst(self.own.at[:, 1 - y, :, x], self.four, self.sems(6), at(z, x, core, 1 - y), self.cuts),
            self.sibling(y, x, 7),
        ]

    def phase(self, phase):
        return (self.first, self.second, self.third)[phase]()

    def start(self, phase):
        if phase == 0:
            self.keep().start()
        for copy in self.phase(phase):
            copy.start()

    def finish(self, phase):
        if phase == 0:
            self.keep().wait()
        for copy in self.phase(phase):
            copy.wait()
        z, x, core, y = spot()
        own, one = self.own, self.one
        left, right = slice(0, self.cut), slice(self.cut, self.cols)

        def add(place, *sources):
            own[place] = functools.reduce(jnp.add, [s.astype(F32) for s in (own[place],) + sources]).astype(
                own.dtype
            )

        def over_z(k):
            def step(d, carry):
                if phase == 0:
                    add((k, 1 - y, d, 1 - x), one[k, 1 - y, d, 1 - x])
                elif phase == 1:
                    rows = slice(None)
                    add((k, 1 - y, d, x, rows, left), one[k, 1 - y, d, x, :, left], self.two_left[k, d])
                    add((k, 1 - y, d, x, rows, right), one[k, 1 - y, d, x, :, right])
                    add((k, y, d, 1 - x, rows, left), one[k, y, d, 1 - x, :, left])
                    add((k, y, d, 1 - x, rows, right), one[k, y, d, 1 - x, :, right], self.two_right[k, d])
                else:
                    sources = (own[k, y, d, x], one[k, y, d, x], self.three[k, d], self.four[k, d])
                    total = functools.reduce(jnp.add, [s.astype(F32) for s in sources])
                    self.out[k, d] = total.astype(self.out.dtype)
                return carry

            return step

        for k in range(self.kinds):
            lax.fori_loop(0, self.depth, over_z(k), 0)


class AlongZ:
    def __init__(self, partial, out, mine, rest, sends, receives, local):
        self.partial, self.out, self.mine, self.rest = partial, out, mine, rest
        self.sends, self.receives, self.local = sends, receives, local

    def copies(self):
        z, x, core, y = spot()
        depth = self.partial.shape[1]
        copies = [pltpu.make_async_copy(self.partial.at[:, z], self.mine, self.local)]
        for k in range(1, depth):
            to = (z + k) % depth
            pair = (self.sends.at[k], self.receives.at[k])
            copies.append(send(self.partial.at[:, to], self.rest.at[k - 1], pair, at(to, x, core, y)))
        return copies

    def start(self):
        for copy in self.copies():
            copy.start()

    def finish(self):
        for copy in self.copies():
            copy.wait()
        for k in range(self.out.shape[0]):
            total = self.mine[k].astype(F32)
            for other in range(self.rest.shape[0]):
                total = total + self.rest[other, k].astype(F32)
            self.out[k] = total


def along_z_shapes(partial):
    kinds, depth, rows, cols = partial
    return [
        pltpu.VMEM((kinds, rows, cols), LOW),
        pltpu.VMEM((depth - 1, kinds, rows, cols), LOW),
    ] + sems(depth, depth, 1)


def reduce_shapes(whole):
    kinds, parts, depth, _, _, rows, cols = whole.shape
    cut = halves(cols)[0].size
    return [
        pltpu.VMEM((kinds, parts, depth, 2, rows, cols), LOW),
        pltpu.VMEM((kinds, parts, depth, 2, rows, cols), LOW),
        pltpu.VMEM((kinds, depth, rows, cut), LOW),
        pltpu.VMEM((kinds, depth, rows, cols - cut), LOW),
        pltpu.VMEM((kinds, depth, rows, cols), LOW),
        pltpu.VMEM((kinds, depth, rows, cols), LOW),
    ]


PIECES = 6


def on(step, point, here, table):
    for (at_step, at_point), actions in table.items():
        if isinstance(here, int):
            if here != at_point:
                continue
            wanted = step == at_step
        else:
            if at_point < 0:
                continue
            wanted = jnp.logical_and(step == at_step, here == at_point)

        @pl.when(wanted)
        def _(actions=actions):
            for action in actions:
                action()


class Guest:
    ins = outs = 0
    number = None

    def __init__(self, gain_row):
        self.gain_row = gain_row

    def parts(self):
        return [], [], [], []

    def aliases(self, first_in, first_out):
        return {}

    def bind(self, ins, outs, scratch, step):
        table = self.table(ins, outs, scratch)
        return lambda point: on(step, None, point, table)

    def table(self, ins, outs, scratch):
        return {}


def call(method, *args):
    return functools.partial(method, *args)


class FirstForward(Guest):
    ins, outs = 3, 3

    def __init__(self, gain_row, number, line, shard, feed_shard):
        self.gain_row, self.number = gain_row, number
        self.line, self.shard, self.feed_shard = line, shard, feed_shard

    def parts(self):
        parts, depth = lax.axis_size(TENSOR), self.line.shape[0]
        rows = self.shard.shape[0]
        shapes = [(parts, depth, 2, 2, rows, a.shape[-1]) for a in (self.line, self.shard)]
        outs = [jax.ShapeDtypeStruct(s, LOW) for s in shapes + [self.line.shape]]
        scratch = sems(depth + EXTRA, depth + EXTRA, depth + EXTRA, depth + EXTRA, 2, depth, depth, 2)
        scratch.append(pltpu.VMEM(self.line.shape, LOW))
        return [self.line, self.shard, self.feed_shard], outs, [any_spec()] * 3, scratch

    def table(self, ins, outs, scratch):
        sends, receives, more_sends, more_receives, hop, line_sends, line_receives, local, buffer = scratch
        feeds = Gather(None, outs[0], sends, receives, hop, ins[0], buffer)
        attn = Gather(ins[1], outs[1], more_sends, more_receives, local.at[0])
        fetch = Line(ins[2], outs[2], line_sends, line_receives, local.at[1])
        return {
            (0, BEGIN): [call(greet, neighbours_of(attn.depth)), call(attn.start, 0), call(feeds.start, 1)],
            (0, 1): [call(attn.finish, 0)],
            (0, 3): [call(attn.start, 1), fetch.start],
            (0, POST): [call(feeds.finish, 1), call(feeds.start, 2)],
            (1, 1): [call(attn.finish, 1), call(attn.start, 2)],
            (1, 3): [call(feeds.finish, 2), call(feeds.start, 3)],
            (1, END): [fetch.finish, call(attn.finish, 2), call(feeds.finish, 3)],
        }


class MiddleForward(Guest):
    ins, outs = 2, 2

    def __init__(self, gain_row, number, full, rows, early, steps):
        self.gain_row, self.number, self.full, self.steps = gain_row, number, full, steps
        self.rows, self.early = rows, early

    def parts(self):
        depth = self.full.shape[1]
        count, held, width = self.rows.shape
        parts = lax.axis_size(TENSOR)
        outs = [
            jax.ShapeDtypeStruct(self.full.shape, LOW),
            jax.ShapeDtypeStruct((count // parts, held * parts, width), LOW),
        ]
        scratch = sems(depth + EXTRA, depth + EXTRA, 1, 2) + [pltpu.SemaphoreType.DMA] * 2
        scratch.append(trade_buffer(self.rows, self.early))
        return [self.full, self.rows], outs, [any_spec()] * 2, scratch

    def aliases(self, first_in, first_out):
        return {first_in: first_out}

    def table(self, ins, outs, scratch):
        sends, receives, local, hop, one_send, one_receive, buffer = scratch
        attn = Gather(None, outs[0], sends, receives, local.at[0])
        trade = Trade(ins[1], outs[1], one_send, one_receive, hop, buffer)
        return {
            (0, BEGIN): [call(greet, neighbours_of(attn.depth)), call(attn.start, 3), trade.start],
            (self.steps - 1, END): [call(attn.finish, 3), trade.finish],
        }


class SecondForward(Guest):
    ins, outs = 3, 2

    def __init__(self, gain_row, number, line, rows, ending, early):
        self.gain_row, self.number, self.line, self.rows = gain_row, number, line, rows
        self.ending, self.early = ending, early

    def parts(self):
        parts, depth = lax.axis_size(TENSOR), self.line.shape[0]
        shapes = [(parts, depth, 2, 2) + self.line.shape[1:], self.ending.shape]
        outs = [jax.ShapeDtypeStruct(s, LOW) for s in shapes]
        scratch = sems(depth + EXTRA, depth + EXTRA, 2, 2) + [pltpu.SemaphoreType.DMA] * 2
        scratch.append(pltpu.VMEM(self.line.shape, LOW))
        scratch.append(trade_buffer(self.rows, self.ending.shape[0] - self.early))
        return [self.line, self.rows, self.ending], outs, [any_spec()] * 2, scratch

    def aliases(self, first_in, first_out):
        return {first_in + 2: first_out + 1}

    def table(self, ins, outs, scratch):
        sends, receives, hop, trade_hop, one_send, one_receive, buffer, rows_buffer = scratch
        feeds = Gather(None, outs[0], sends, receives, hop, ins[0], buffer)
        table = {
            (0, BEGIN): [call(greet, neighbours_of(feeds.depth)), call(feeds.start, 1)],
            (0, POST): [call(feeds.finish, 1), call(feeds.start, 2)],
            (1, 2): [call(feeds.finish, 2), call(feeds.start, 3)],
            (1, END): [call(feeds.finish, 3)],
        }
        if self.early < self.ending.shape[0]:
            trade = Trade(ins[1], outs[1], one_send, one_receive, trade_hop, rows_buffer, self.early)
            table[0, POST].append(trade.start)
            table[1, END].append(trade.finish)
        return table


def split_whole(whole):
    kinds, parts, width, cols = whole.shape
    depth = lax.axis_size(DP) // 4
    return whole.reshape(kinds, parts, depth, 2, 2, width // (4 * depth), cols)


class ReduceTail:
    def __init__(self, whole, own, partial, base, one, three, four, sends, receives, local):
        self.whole, self.own, self.partial = whole, own, partial
        self.base, self.one, self.three, self.four = base, one, three, four
        self.sems = lambda k: (sends.at[k], receives.at[k])
        self.local = local

    def copies(self):
        z, x, core, y = spot()
        own, cuts = self.own, self.partial.shape[:2]
        away = self.whole.at[:, y, :, x, 1 - core]
        return [
            pltpu.make_async_copy(own.at[:, y, :, x], self.base, self.local),
            Burst(own.at[:, y, :, 1 - x], self.three, self.sems(0), at(z, 1 - x, core, y), cuts),
            Burst(own.at[:, 1 - y, :, x], self.four, self.sems(1), at(z, x, core, 1 - y), cuts),
            Burst(away, self.one, self.sems(2), at(z, x, 1 - core, y), cuts),
        ]

    def start(self):
        for copy in self.copies():
            copy.start()

    def finish(self):
        for copy in self.copies():
            copy.wait()
        for k in range(self.partial.shape[0]):
            for d in range(self.partial.shape[1]):
                sources = (self.base, self.one, self.three, self.four)
                total = functools.reduce(jnp.add, [s[k, d].astype(F32) for s in sources])
                self.partial[k, d] = total.astype(self.partial.dtype)


class Backward(Guest):
    def __init__(self, gain_row, number, whole, points, rows=None, partial=None, half=False, pending=None, late=False):
        self.gain_row, self.number, self.points, self.rows = gain_row, number, points, rows
        self.whole, self.partial, self.half, self.late = split_whole(whole), partial, half, late
        self.pending = pending and (split_whole(pending[0]), pending[1])
        self.outs = 1 + (rows is not None) + (partial is not None) + (pending is not None)
        self.ins = self.outs + (pending is not None)

    def parts(self):
        shape = self.whole.shape
        depth = shape[2]
        kept = shape[:4] + shape[5:] if self.half else (shape[0], depth, shape[5], shape[6])
        outs = [jax.ShapeDtypeStruct(kept, LOW)]
        specs = [whole_spec(outs[0].shape)]
        ins = [self.whole]
        scratch = reduce_shapes(self.whole)[1 if self.half else 0 :] + sems(EXTRA, EXTRA, 1)
        if self.rows is not None:
            count, rows, width = self.rows.shape
            ins.append(self.rows)
            outs.append(jax.ShapeDtypeStruct((count, rows // 2, width), self.rows.dtype))
            specs.append(any_spec())
            scratch += [pltpu.SemaphoreType.DMA] * 2
        line = None
        if self.partial is not None:
            ins.append(self.partial)
            line = self.partial.shape
        if self.pending is not None:
            ins += list(self.pending)
            kinds, _, depth, _, _, rows, cols = self.pending[0].shape
            line = (kinds, depth, rows, cols)
            scratch += [pltpu.VMEM(line, LOW)] * 5 + sems(3, 3, 1)
        if line is not None:
            outs.append(jax.ShapeDtypeStruct((line[0],) + line[2:], F32))
            specs.append(whole_spec(outs[-1].shape))
            scratch += along_z_shapes(line)
        return ins, outs, specs, scratch

    def table(self, ins, outs, scratch):
        kept = PIECES - self.half
        buffers, scratch = list(scratch[:kept]), scratch[kept:]
        if self.half:
            buffers.insert(0, outs[0])
        sends, receives, local = scratch[:3]
        scratch = scratch[3:]
        group = Reduce(ins[0], outs[0], *buffers, sends, receives, local.at[0])
        near = neighbours_of(group.depth)
        first, last = [call(group.start, 0)], []
        points = self.points
        if self.rows is not None:
            z, x, core, y = spot()
            half = outs[1].shape[1]
            away = ins[1].at[:, pl.ds(pl.multiple_of((1 - y) * half, half), half)]
            copy = send(away, outs[1], (scratch[0], scratch[1]), at(z, x, core, 1 - y))
            first.append(copy.start)
            last.append(copy.wait)
            scratch = scratch[2:]
        middle = []
        if self.pending is not None:
            partial, base, one, three, four, sends, receives, local = scratch[:8]
            scratch = scratch[8:]
            tail = ReduceTail(ins[-2], ins[-1], partial, base, one, three, four, sends, receives, local.at[0])
            first.insert(0, tail.start)
            middle.append(tail.finish)
        if self.partial is not None or self.pending is not None:
            if self.partial is not None:
                partial = ins[-1]
            mine, rest, sends, receives, local = scratch
            line = AlongZ(partial, outs[-1], mine, rest, sends, receives, local.at[0])
            (first if self.pending is None else middle).append(line.start)
            last.append(line.finish)
        if self.late:
            table = {(0, BEGIN): [call(announce, near)], (0, 0): [call(await_all, near)] + first}
        else:
            table = {(0, BEGIN): [call(greet, near)] + first}
        phases = 2 if self.half else 3
        for phase in range(phases):
            actions = table.setdefault(points[phase], [])
            if phase == 0:
                actions.extend(middle)
            actions.append(call(group.finish, phase))
            if phase + 1 < phases:
                actions.append(call(group.start, phase + 1))
        table[points[phases - 1]].extend(last)
        return table


def reduce_kernel(total, heads_each, *refs):
    whole, away, feed_partial, part_two, feed_two_grad = refs[:5]
    attn_one, feed_one, attn_two, feed_two = refs[5:9]
    out, feed_one_grad, arrived, stats = refs[9:13]
    refs = refs[13:]
    groups, lines = [], []
    place = 0
    for half in range(2):
        cols = refs[0].shape[-1]
        buffers, line_refs, refs = refs[:PIECES], refs[PIECES : PIECES + 6], refs[PIECES + 6 :]
        partial, mine, rest, sends, receives, local = line_refs
        part = columns(whole, place, place + cols)
        group_sems, refs = refs[:3], refs[3:]
        groups.append(Reduce(part, partial, *buffers, group_sems[0], group_sems[1], group_sems[2].at[0]))
        target = columns(out, place, place + cols)
        lines.append(AlongZ(partial, target, mine, rest, sends, receives, local.at[0]))
        place += cols
    mine, rest, sends, receives, local = refs[:5]
    feed_line = AlongZ(feed_partial, feed_one_grad, mine, rest, sends, receives, local.at[0])
    tiles, stat_sends, stat_receives, hand_sends, hand_receives = refs[5:]
    parts = lax.axis_size(TENSOR)
    me = lax.axis_index(DP) * parts + lax.axis_index(TENSOR)
    others = [(me + k) % total for k in range(1, total)]
    z, x, core, y = spot()
    handed = []
    for k, (first, size) in enumerate(in_two(away.shape[0])):
        piece = pl.ds(first, size)
        pair = (hand_sends.at[k], hand_receives.at[k])
        handed.append(send(away.at[piece], arrived.at[piece], pair, at(z, x, core, 1 - y)))
    greet([(other // parts, other % parts) for other in others])
    for group in groups:
        group.start(0)
    handed[0].start()
    feed_line.start()
    for phase in range(3):
        for group, line in zip(groups, lines):
            group.finish(phase)
            if phase < 2:
                group.start(phase + 1)
            else:
                line.start()
    for copy in handed[1:]:
        copy.start()
    feed_line.finish()
    for line in lines:
        line.finish()
    outs = (feed_two_grad, part_two, feed_one_grad, out)
    attn_two_grad, attn_one_grad = part_two, out
    qkv = 3 * (attn_two.shape[1] // 4)
    small = attn_one[:, 4 * (attn_two.shape[1] // 4) :].astype(F32)
    gate_grad = attn_two_grad[0, :, attn_two.shape[1] :]
    units = feed_one.shape[1] // 2

    def row_sums(values):
        return jnp.sum(values, axis=1, keepdims=True)

    lane = lax.broadcasted_iota(jnp.int32, small.shape, 1)
    gate_only = jnp.where(lane < heads_each, small, 0.0)
    sums = [
        row_sums(attn_one[:, :qkv].astype(F32) * attn_one_grad[0, :, :qkv]),
        row_sums(feed_one[:, :units].astype(F32) * feed_one_grad[0]),
        row_sums(attn_two[:, :qkv].astype(F32) * attn_two_grad[0, :, :qkv])
        + row_sums(gate_only * gate_grad),
        row_sums(feed_two[:, :units].astype(F32) * feed_two_grad[0]),
    ]
    squares = functools.reduce(
        jnp.add, [row_sums(out[k] * out[k]) for out in outs for k in range(out.shape[0])]
    )
    tile = jnp.where(lane == 4, squares, 0.0)
    for row in range(4):
        gain = row_sums(jnp.where(lane == heads_each + row, small, 0.0))
        tile = tile + jnp.where(lane == row, sums[row] / gain, 0.0)
    blank = jnp.zeros((WIDE - tile.shape[0], WIDE), F32)
    tiles[me] = jnp.concatenate([tile, blank], axis=0).T[:8]
    copies = [
        send(tiles.at[me], tiles.at[me], (stat_sends.at[k], stat_receives.at[k]), (o // parts, o % parts))
        for k, o in enumerate(others)
    ]
    for copy in copies:
        copy.start()
    for copy in copies:
        copy.wait()
    row = lax.broadcasted_iota(jnp.int32, (8, WIDE), 0)
    found = jnp.zeros((8, WIDE), F32)
    for device in range(0, total, parts):
        pair = functools.reduce(jnp.add, [tiles[device + part] for part in range(parts)])
        found = found + jnp.where(row < 4, pair * pair, jnp.where(row == 4, pair, 0.0))
    start = me - me % parts
    stats[0] = functools.reduce(jnp.add, [tiles[start + part] for part in range(parts)])
    stats[1] = jnp.broadcast_to(jnp.sum(found, keepdims=True), found.shape)
    for copy in handed:
        copy.wait()


def finish_reduce(whole, away, feed_partial, grads, shards, heads_each, number):
    depth = lax.axis_size(DP) // 4
    total = lax.axis_size(TENSOR) * lax.axis_size(DP)
    whole = split_whole(whole)
    kinds, _, _, _, _, rows, cols = whole.shape
    scratch = []
    for part in halves(cols):
        piece = jax.ShapeDtypeStruct(whole.shape[:-1] + (part.size,), LOW)
        line = (kinds, depth, rows, part.size)
        scratch += reduce_shapes(piece) + [pltpu.VMEM(line, LOW)] + along_z_shapes(line)
        scratch += sems(EXTRA, EXTRA, 1)
    scratch += along_z_shapes(feed_partial.shape)
    scratch += [pltpu.VMEM((total, 8, WIDE), F32)] + sems(total - 1, total - 1)
    vmem = pl.BlockSpec(memory_space=pltpu.VMEM)
    return pl.pallas_call(
        functools.partial(reduce_kernel, total, heads_each),
        out_shape=[
            jax.ShapeDtypeStruct((kinds, rows, cols), F32),
            jax.ShapeDtypeStruct((feed_partial.shape[0], rows, feed_partial.shape[3]), F32),
            jax.ShapeDtypeStruct(away.shape, away.dtype),
            jax.ShapeDtypeStruct((2, 8, WIDE), F32),
        ],
        in_specs=[any_spec()] * 3 + [vmem] * 6,
        out_specs=[vmem, vmem, any_spec(), vmem],
        scratch_shapes=scratch + sems(2, 2),
        compiler_params=pltpu.CompilerParams(
            collective_id=number, has_side_effects=True, vmem_limit_bytes=VMEM_BYTES
        ),
    )(whole, away, feed_partial, *grads, *shards)


def update_kernel(heads_each, *refs):
    grad, arrived_grad, result, arrived_rows = refs[:4]
    attn_one, attn_two, feed_one, feed_two, stats = refs[4:9]
    states = [refs[9 + 4 * g : 13 + 4 * g] for g in range(6)]
    refs = refs[33:]
    rows_out, grad_out, norm_out = refs[:3]
    outs = [refs[3 + 4 * g : 7 + 4 * g] for g in range(6)]
    feed_gains = refs[27]
    y = lax.axis_index(TENSOR)
    share, half = arrived_rows.shape[0], arrived_rows.shape[1]
    mine = pl.ds(pl.multiple_of(y * half, half), half)
    grad_out[pl.ds(y * share, share)] = grad[:, mine]
    grad_out[pl.ds((1 - y) * share, share)] = arrived_grad[...].astype(F32)
    rows_out[pl.ds(y * share, share)] = result[:, mine]
    rows_out[pl.ds((1 - y) * share, share)] = arrived_rows[...]
    norm = jnp.sqrt(stats[1, :1, :])
    norm_out[...] = norm
    factor = (CLIP / jnp.maximum(norm, CLIP))[:, :1]

    def apply(group, spot_at, piece):
        state = [ref[spot_at] for ref in states[group]]
        new = adamw(*state, piece * factor, STEP_RATES[group], STEP_DECAYS[group])
        for ref, value in zip(outs[group], new):
            ref[spot_at] = value

    cols = states[0][0].shape[3]
    for depth, part in enumerate((attn_one, attn_two)):
        for kind in range(3):
            apply(0, (depth, kind), part[0, :, kind * cols : (kind + 1) * cols])
        apply(1, (depth,), part[0, :, 3 * cols : 4 * cols])
    for depth, part in enumerate((feed_one, feed_two)):
        apply(2, (depth,), part[0])
        apply(3, (depth,), part[1])
    gains = stats[0][: states[4][0].shape[0], : states[4][0].shape[1]]
    apply(4, (slice(None),), gains)
    apply(5, (slice(None),), attn_two[0, :, 4 * cols :].T[:heads_each])
    feed_gains[0:1] = gains[1:2] * factor
    feed_gains[1:2] = gains[3:4] * factor


def update(moves, grads, stats, states, outs, heads_each):
    vmem = pl.BlockSpec(memory_space=pltpu.VMEM)
    flat_states = [a for group in states for a in group]
    ins = list(moves) + list(grads) + [stats] + flat_states
    shapes = list(outs[:3]) + [jax.ShapeDtypeStruct(a.shape, F32) for a in flat_states] + [outs[3]]
    return pl.pallas_call(
        functools.partial(update_kernel, heads_each),
        out_shape=shapes,
        in_specs=[vmem] * len(ins),
        out_specs=[vmem] * len(shapes),
        compiler_params=pltpu.CompilerParams(vmem_limit_bytes=VMEM_BYTES),
    )(*ins)


def tables(length):
    half_dim = HEAD_DIM // 2
    places = np.arange(length).astype(np.float32)
    frequency = np.exp(
        np.float32(-math.log(10000.0)) * np.arange(half_dim).astype(np.float32) / np.float32(half_dim)
    )
    angles = (frequency[:, None] * places[None, :]).astype(np.float64)
    return jnp.asarray(np.cos(angles), F32), jnp.asarray(np.sin(angles), F32)


def whole_body(
    activations,
    memory_one,
    memory_two,
    neighbours,
    resets,
    cotangent,
    qkv_weight,
    qkv_first,
    qkv_second,
    qkv_ema,
    out_weight,
    out_first,
    out_second,
    out_ema,
    up_weight,
    up_first,
    up_second,
    up_ema,
    down_weight,
    down_first,
    down_second,
    down_ema,
    gain_rows,
    gain_first,
    gain_second,
    gain_ema,
    gate_weight,
    gate_first,
    gate_second,
    gate_ema,
):
    parts = lax.axis_size(TENSOR)
    share = activations.shape[0] // parts
    width = activations.shape[2]
    heads_each = gate_weight.shape[1]

    def flip(group):
        return [a.swapaxes(-1, -2) for a in group]

    states = [
        [qkv_weight, qkv_first, qkv_second, qkv_ema],
        flip([out_weight, out_first, out_second, out_ema]),
        [up_weight, up_first, up_second, up_ema],
        flip([down_weight, down_first, down_second, down_ema]),
        [gain_rows, gain_first, gain_second, gain_ema],
        flip([gate_weight, gate_first, gate_second, gate_ema]),
    ]
    near = neighbours.transpose(0, 2, 1)
    started = start_up(*[group[0] for group in states], activations, memory_one, memory_two, near, 0)
    attn_shard, attn_two_shard, feed_shard, feed_two_shard, slab_one, line, start = started[:7]
    memories, near = started[7:9], started[9]
    slab_one = flat(slab_one)
    cosine, sine = tables(MEM + SEG)
    shape = (share * SEG, width)
    back = (share, SEG, width)

    guest = FirstForward(heads_each, 1, line, attn_two_shard, feed_two_shard)
    one = attend(start, memories[0], resets, slab_one, slab_one, cosine, sine, None, guest)
    after_one = one[0].reshape(shape)
    feed_one = flat(one[6])
    steps = 2 * parts * up_weight.shape[2] // (2 * CHUNK)
    early = (share + 1) // 2
    guest = MiddleForward(heads_each + 1, 2, one[7], cotangent, early, steps)
    before_two, slab_two, ending = feed(after_one, feed_one, slab_one, guest)
    slab_two = flat(slab_two)
    before_rows = before_two.reshape(back)
    guest = SecondForward(heads_each + 2, 3, one[8], cotangent, ending, early)
    two = attend(before_rows, memories[1], resets, slab_two, slab_one, cosine, sine, near, guest)
    after_two = two[0].reshape(shape)
    feed_two, ending = flat(two[9]), two[10].reshape(shape)
    guest = Guest(heads_each + 3)
    result, grad, feed_grad_two = feed_back(after_two, feed_two, slab_one, ending, True, guest)
    result = result.reshape(back)
    points = ((0, 2), (1, 0), (1, END))
    guest = Backward(heads_each + 2, 4, feed_grad_two, points, result, late=True)
    grad, attn_grad_two, partial, arrived_rows = attend_back(
        before_rows,
        memories[1],
        resets,
        slab_two,
        slab_one,
        cosine,
        sine,
        grad.reshape(back),
        two[1:],
        near,
        guest,
    )
    points = ((1, BEGIN), (steps - 1, END))
    guest = Backward(heads_each + 1, 5, attn_grad_two[None], points, None, partial, half=True)
    grad, feed_grad_one, own, feed_two_part = feed_back(
        after_one, feed_one, slab_one, grad.reshape(shape), False, guest
    )
    points = ((0, 2), (1, 0), (1, END))
    guest = Backward(heads_each, 6, feed_grad_one, points, pending=(attn_grad_two[None], own))
    grad, attn_grad_one, away, partial, attn_two_part = attend_back(
        start, memories[0], resets, slab_one, slab_one, cosine, sine, grad.reshape(back), one[1:], None, guest
    )
    attn_one_part, feed_one_part, arrived_grad, stats = finish_reduce(
        attn_grad_one[None],
        away,
        partial,
        [attn_two_part, feed_two_part],
        [attn_shard, feed_shard, attn_two_shard, feed_two_shard],
        heads_each,
        7,
    )
    outs = (
        jax.ShapeDtypeStruct(activations.shape, LOW),
        jax.ShapeDtypeStruct(activations.shape, F32),
        jax.ShapeDtypeStruct((1, WIDE), F32),
        jax.ShapeDtypeStruct((2, gain_rows.shape[1]), F32),
    )
    done = update(
        (grad, arrived_grad, result, arrived_rows),
        (attn_one_part, attn_two_part, feed_one_part, feed_two_part),
        stats,
        states,
        outs,
        heads_each,
    )
    result_rows, input_grad, norm = done[:3]
    groups = [list(done[3 + 4 * group : 7 + 4 * group]) for group in range(6)]
    for group in (1, 3, 5):
        groups[group] = flip(groups[group])
    updated = [a for group in groups for a in group]
    return (result_rows, input_grad, norm[0, 0], *updated, done[27])


def solution(mesh):
    in_specs = (
        P(DP, TENSOR, None),
        P(DP, None, None),
        P(DP, None, None),
        P(DP, None, None),
        P(DP),
        P(DP, TENSOR, None),
        P(None, None, DP, TENSOR),
        P(None, None, DP, TENSOR),
        P(None, None, DP, TENSOR),
        P(None, None, DP, TENSOR),
        P(None, TENSOR, DP),
        P(None, TENSOR, DP),
        P(None, TENSOR, DP),
        P(None, TENSOR, DP),
        P(None, DP, TENSOR),
        P(None, DP, TENSOR),
        P(None, DP, TENSOR),
        P(None, DP, TENSOR),
        P(None, TENSOR, DP),
        P(None, TENSOR, DP),
        P(None, TENSOR, DP),
        P(None, TENSOR, DP),
        P(None, DP),
        P(None, DP),
        P(None, DP),
        P(None, DP),
        P(DP, TENSOR),
        P(DP, TENSOR),
        P(DP, TENSOR),
        P(DP, TENSOR),
    )
    out_specs = (
        P(DP, TENSOR, None),
        P(DP, TENSOR, None),
        P(),
        P(None, None, DP, TENSOR),
        P(None, None, DP, TENSOR),
        P(None, None, DP, TENSOR),
        P(None, None, DP, TENSOR),
        P(None, TENSOR, DP),
        P(None, TENSOR, DP),
        P(None, TENSOR, DP),
        P(None, TENSOR, DP),
        P(None, DP, TENSOR),
        P(None, DP, TENSOR),
        P(None, DP, TENSOR),
        P(None, DP, TENSOR),
        P(None, TENSOR, DP),
        P(None, TENSOR, DP),
        P(None, TENSOR, DP),
        P(None, TENSOR, DP),
        P(None, DP),
        P(None, DP),
        P(None, DP),
        P(None, DP),
        P(DP, TENSOR),
        P(DP, TENSOR),
        P(DP, TENSOR),
        P(DP, TENSOR),
        P(None, DP),
    )
    parts = mesh.shape[TENSOR]
    regular = parts == 2 and mesh.shape[DP] % 4 == 0

    def choose(activations, *rest):
        fits = regular and activations.shape[0] // mesh.shape[DP] % parts == 0
        route = whole_body if fits else body
        spread = jax.shard_map(
            route, mesh=mesh, in_specs=in_specs, out_specs=out_specs, check_vma=False
        )
        return spread(activations, *rest)

    return choose
```
